256 devices in a mesh: dp: 32 (over z_hi, x, core), ctx: 8 (over y, z_lo).
Axes of the slice: x: 4, y: 4, z: 8 (z_hi: 4, z_lo: 2; z = z_hi * 2 + z_lo), core: 2. Of those that a mesh axis runs over, the one named last changes fastest.
Arguments:
- layer_input: bfloat16 [32, 2048, 4096], P('dp', 'ctx'), may hold values from -6 to 6
- queries: bfloat16 [32, 2048, 1024], P('dp', 'ctx'), may hold values from -6 to 6
- key_head: bfloat16 [32, 2048, 128], P('dp', 'ctx'), may hold values from -6 to 6
- shared_value_head: bfloat16 [32, 2048, 128], P('dp', 'ctx'), may hold values from -6 to 6
- grad_output: bfloat16 [32, 2048, 1024], P('dp', 'ctx'), may hold values from -6 to 6
- doc_ids: int32 [32, 2048], P('dp'), may hold values from 0 to 3, never falling along the last dimension, each value on 1 to 2045 neighbouring positions
Outputs:
- grad_query: bfloat16 [32, 2048, 1024], P('dp', 'ctx')
- grad_key: bfloat16 [32, 2048, 128], P('dp', 'ctx')
- grad_value: bfloat16 [32, 2048, 128], P('dp', 'ctx')
- query_weight_grad: float32 [4096, 1024], P(('dp', 'ctx'))
- key_weight_grad: float32 [4096, 128], P(('dp', 'ctx'))
- value_weight_grad: float32 [4096, 128], P(('dp', 'ctx'))
The draws below stay inside these ranges and needn't reach their ends.
Inputs may be any that keep to these rules, and one draw needn't show every extreme that they name: `doc_ids`: along each row the document number never falls and starts at 0; every one of the 4 documents holds 1 to 2045 tokens.
All inputs are finite; a program needn't handle non-finite values.
Results may differ from the reference program's by a relative error of at most 0.019.
Values may be sent and summed in bfloat16 or wider, within the bound.
No kernel may reach another device: no remote copies, remote signals or barrier semaphores. Data moves between devices by JAX's collectives and lax.ppermute only.
A program may use at most 128 MiB of HBM per device.

```python
import math
import jax
import jax.numpy as jnp
import numpy as np
from jax import lax

D = 4096
HD = 128
HQ = 8
DOCS = 4
SEQ = 2048
N_DP = 32


def draw_queries(key, part):
    key = jax.random.fold_in(key, 5)
    values = jnp.clip(jax.random.normal(key, (N_DP, SEQ, HQ * HD), jnp.float32), -6.0, 6.0)
    return values.astype(jnp.bfloat16)


def draw_key_head(key, part):
    key = jax.random.fold_in(key, 7)
    values = jnp.clip(jax.random.normal(key, (N_DP, SEQ, HD), jnp.float32), -6.0, 6.0)
    return values.astype(jnp.bfloat16)


def strengthened(drawn, rng, source, target, blocks, factor):
    owner, partner = [(jnp.arange(drawn.shape[axis_at]) // (drawn.shape[axis_at] // blocks)).reshape([-1 if axis == axis_at else 1 for axis in range(drawn.ndim)]) for axis_at in (source, target)]
    chosen = jax.random.permutation(rng, blocks)[partner]
    strong = (owner == chosen) | (owner == (partner + blocks // 2) % blocks)
    return jnp.where(strong, factor * drawn, drawn)


def shard_levels(stream_key, dims, shards, smallest, largest):
    gain, own = 1.0, jax.random.fold_in(stream_key, 6)
    for axis_at, parts in shards:
        steps = jnp.exp(jax.random.uniform(jax.random.fold_in(own, axis_at), (parts,), jnp.float32, smallest / len(shards), largest / len(shards)))
        gain = gain * jnp.repeat(steps, dims[axis_at] // parts).reshape([-1 if axis == axis_at else 1 for axis in range(len(dims))])
    return gain


def length_profile(count, total, limit, lean):
    weights = [(1 << 20) // math.isqrt(standing ** lean) + 1 for standing in range(2, count + 1)]
    surplus, given = total - limit - (count - 1), [1] * (count - 1)
    while surplus > 0:
        candidates = [i for i in range(count - 1) if given[i] < limit]
        mass, remaining = sum([weights[i] for i in candidates]), surplus
        for i in candidates:
            extra = min(limit - given[i], max(1, remaining * weights[i] // mass), surplus)
            given[i] = given[i] + extra
            surplus = surplus - extra
    return np.array([limit] + given)


def ragged_sizes(stream_key, amount, total, most, lean):
    if amount == 2:
        one = jax.random.randint(stream_key, (), max(1, total - most), min(most, total - 1) + 1)
        return jnp.stack([one, total - one])
    tallies = jnp.asarray(length_profile(amount, total, most, lean), jnp.int32)
    twos = (amount - 1) // 2
    donor, sink = tallies[1:1 + 2 * twos:2], tallies[2:2 + 2 * twos:2]
    room = jnp.minimum(donor - 1, most - sink)
    moved = jax.random.randint(jax.random.fold_in(stream_key, 1), (twos,), 0, 1 << 20) % (room + 1)
    tallies = tallies.at[1:1 + 2 * twos:2].set(donor - moved).at[2:2 + 2 * twos:2].set(sink + moved)
    return tallies[jax.random.permutation(jax.random.fold_in(stream_key, 2), amount)]


def centred(own_key, extent, spread, reach, cuts=(), held_as=jnp.bfloat16):
    array = spread * jax.random.normal(own_key, extent, jnp.float32)
    if cuts:
        array = array * shard_levels(own_key, extent, cuts, -0.22, 0.18)
    return jnp.clip(array, -reach, reach).astype(held_as)


def bell_draw_with(rng, shape, width, bound, shards, heavy, kind=jnp.bfloat16):
    values = width * jax.random.normal(rng, shape, jnp.float32)
    if shards:
        values = values * shard_levels(rng, shape, shards, -0.22, 0.18)
    return jnp.clip(strengthened(values, jax.random.fold_in(rng, 3), *heavy), -bound, bound).astype(kind)


def setup_inputs(seed: int = 0) -> dict:
    seeds = jax.random.split(jax.random.key(seed), 7)
    layer_input = bell_draw_with(seeds[0], (N_DP, SEQ, D), 1.0, 6.0, ((0, 32), (1, 8)), (1, 2, 8, 2.0))
    queries = draw_queries(jax.random.fold_in(seeds[6], 71), 0)
    key_head = draw_key_head(jax.random.fold_in(seeds[6], 71), 0)
    shared_value_head = centred(seeds[3], (N_DP, SEQ, HD), 1.0, 6.0, ((0, 32), (1, 8)))
    grad_output = centred(seeds[4], (N_DP, SEQ, HQ * HD), 1.0, 6.0, ((0, 32), (1, 8)))
    doc_ids = jax.vmap(lambda own: jnp.searchsorted(jnp.cumsum(ragged_sizes(own, DOCS, SEQ, SEQ - DOCS + 1, 2)), jnp.arange(SEQ), side="right"))(jax.random.split(seeds[5], N_DP)).reshape((N_DP, SEQ)).astype(jnp.int32)
    return dict(layer_input=layer_input, queries=queries, key_head=key_head, shared_value_head=shared_value_head, grad_output=grad_output, doc_ids=doc_ids)


NEG = -1e+30

def attend(queries, key_head, shared_value_head, grad_output, docs):
    seq = docs.shape[0]
    hd = key_head.shape[1]
    heads = queries.shape[1] // hd
    scale = hd ** (-0.5)
    qmat = queries.reshape(seq, heads, hd).astype(jnp.float32)
    kmat = key_head.astype(jnp.float32)
    value_matrix = shared_value_head.astype(jnp.float32)
    scores = jnp.einsum('xua,ia->uxi', qmat, kmat) * scale
    places = jnp.arange(seq)
    allowed = (docs[:, None] == docs[None, :]) & (places[None, :] <= places[:, None])
    scores = jnp.where(allowed[None], scores, NEG)
    summit = lax.optimization_barrier(jnp.max(scores, axis=-1, keepdims=True))
    raised = jnp.exp(scores - summit)
    prob = raised / lax.optimization_barrier(jnp.sum(raised, axis=-1, keepdims=True))
    probability_reduced = prob.astype(jnp.bfloat16).astype(jnp.float32)
    rebuilt_probabilities = jnp.einsum('jgl,lw->jgw', probability_reduced, value_matrix)
    output_gradient = grad_output.reshape(seq, heads, hd).astype(jnp.float32)
    delta = jnp.einsum('thd,htd->ht', output_gradient, rebuilt_probabilities)
    probability_gradient = jnp.einsum('xua,ia->uxi', output_gradient, value_matrix)
    score_gradient = (prob * (probability_gradient - delta[..., None])).astype(jnp.bfloat16).astype(jnp.float32)
    grad_q = (jnp.einsum('hts,sd->thd', score_gradient, kmat) * scale).astype(jnp.bfloat16).reshape(seq, heads * hd)
    grad_k = (jnp.einsum('hts,thd->sd', score_gradient, qmat) * scale).astype(jnp.bfloat16)
    grad_v = jnp.einsum('hts,thd->sd', probability_reduced, output_gradient).astype(jnp.bfloat16)
    return (grad_q, grad_k, grad_v)

def reference(layer_input, queries, key_head, shared_value_head, grad_output, doc_ids):
    grad_q, grad_k, grad_v = lax.map(lambda items: attend(*items), (queries, key_head, shared_value_head, grad_output, doc_ids))
    flat = layer_input.reshape(-1, D)
    factor = 1.0 / (N_DP * SEQ) ** 0.5

    def weight_grad(grads):
        rows = grads.reshape(flat.shape[0], -1)
        return lax.dot_general(flat, rows, (((0,), (0,)), ((), ())), preferred_element_type=jnp.float32) * factor
    return (grad_q, grad_k, grad_v, weight_grad(grad_q), weight_grad(grad_k), weight_grad(grad_v))
```

```python
import math

import jax
import jax.numpy as jnp
from jax import lax
from jax.sharding import Mesh, PartitionSpec as P

NEG = -1e30
AXES = ("zh", "x", "core", "y", "zl")
SIZES = (4, 4, 2, 4, 2)
GROUP = ("x", "core")
CTX = ("y", "zl")
BF = jnp.bfloat16
F32 = jnp.float32


def shifted(value, axes, count, step, wrap):
    pairs = []
    for src in range(count):
        dst = src + step
        if wrap:
            pairs.append((src, dst % count))
        elif 0 <= dst < count:
            pairs.append((src, dst))
    return lax.ppermute(value, axes, pairs)


def attention(q, do, kv, docs, place):
    rows = q.shape[0]
    hd = kv[0].shape[1] // 2
    heads = q.shape[1] // hd
    scale = hd ** (-0.5)
    blocks = len(kv)
    kv = jnp.concatenate(kv, axis=0)
    keys, values = kv[:, :hd], kv[:, hd:]
    first = place * rows
    my_places = first + jnp.arange(rows)
    my_docs = lax.dynamic_slice_in_dim(docs, first, rows)
    starts = jnp.sum(docs[None, :] < my_docs[:, None], axis=1)
    key_places = (
        (place - jnp.arange(blocks))[:, None] * rows + jnp.arange(rows)[None, :]
    ).reshape(-1)
    allowed = (key_places[None, :] >= starts[:, None]) & (
        key_places[None, :] <= my_places[:, None]
    )
    q = q.reshape(rows, heads, hd)
    do = do.reshape(rows, heads, hd)
    scores = jnp.einsum("xua,ia->uxi", q, keys, preferred_element_type=F32) * scale
    scores = jnp.where(allowed[None], scores, NEG)
    top = jnp.max(scores, axis=-1, keepdims=True)
    raised = jnp.exp(scores - top)
    prob = raised / jnp.sum(raised, axis=-1, keepdims=True)
    prob_low = prob.astype(BF)
    dprob = jnp.einsum("xua,ia->uxi", do, values, preferred_element_type=F32)
    delta = jnp.sum(prob * dprob, axis=-1, keepdims=True)
    dscore = (prob * (dprob - delta)).astype(BF)
    dq = jnp.einsum("hts,sd->thd", dscore, keys, preferred_element_type=F32) * scale
    dk = jnp.einsum("hts,thd->sd", dscore, q, preferred_element_type=F32) * scale
    dv = jnp.einsum("hts,thd->sd", prob_low, do, preferred_element_type=F32)
    dkv = jnp.concatenate([dk, dv], axis=1).reshape(blocks, rows, 2 * hd)
    return dq.astype(BF).reshape(rows, heads * hd), [dkv[d] for d in range(blocks)]


def local(layer_input, queries, key_head, value_head, grad_output, doc_ids):
    x, q, k, v, do, docs = (
        a[0] for a in (layer_input, queries, key_head, value_head, grad_output, doc_ids)
    )
    rows, hd = k.shape
    dim = x.shape[1]
    ctx = lax.axis_size(CTX)
    group = lax.axis_size(GROUP)
    z_hi = lax.axis_size("zh")
    place = lax.axis_index(CTX)
    me = lax.axis_index(GROUP)

    kv = jnp.concatenate([k, v], axis=1)
    kv_blocks = [kv] + [shifted(kv, CTX, ctx, d, False) for d in range(1, ctx)]

    wide = dim // (z_hi * group)
    split = x.reshape(rows, z_hi, group, wide).transpose(2, 0, 1, 3).reshape(group, rows, z_hi * wide)
    features = lax.all_to_all(split, GROUP, 0, 0, tiled=True).reshape(group * rows, z_hi * wide)

    dq, dkv = attention(q, do, kv_blocks, docs, place)

    total = dkv[0]
    for d in range(1, ctx):
        total = total + shifted(dkv[d].astype(BF), CTX, ctx, -d, False).astype(F32)
    dkv_own = total.astype(BF)

    grads = jnp.concatenate([dq, dkv_own], axis=1)
    grads_all = lax.all_gather(grads, GROUP, axis=0, tiled=True)
    part = lax.dot_general(
        features, grads_all, (((0,), (0,)), ((), ())), preferred_element_type=F32
    ).astype(BF)
    n = part.shape[1]
    y, zl = lax.axis_size("y"), lax.axis_size("zl")
    keep = wide // (y * zl)
    part = part.reshape(z_hi, y, zl * keep * n).transpose(1, 0, 2)
    part = lax.all_to_all(part, "y", 0, 0, tiled=True)
    part = jnp.sum(part.astype(F32), axis=0).astype(BF)
    part = part.reshape(z_hi * zl, keep, n)
    part = lax.all_to_all(part, ("zh", "zl"), 0, 0, tiled=True)
    tokens = rows * ctx * group * z_hi
    weight = jnp.sum(part.astype(F32), axis=0) * (1.0 / math.sqrt(tokens))
    width = q.shape[1]
    return (
        dq[None],
        dkv_own[None, :, :hd],
        dkv_own[None, :, hd:],
        weight[:, :width],
        weight[:, width : width + hd],
        weight[:, width + hd :],
    )


def solution(mesh):
    fine = Mesh(mesh.devices.reshape(SIZES), AXES)
    dp = ("zh", "x", "core")
    tok = P(dp, CTX, None)
    row = P(dp + CTX, None)
    return jax.shard_map(
        local,
        mesh=fine,
        in_specs=(tok, tok, tok, tok, tok, P(dp, None)),
        out_specs=(tok, tok, tok, row, row, row),
        check_vma=False,
    )
```

```python
import functools
import math

import jax
import jax.numpy as jnp
from jax import lax
from jax.experimental import pallas as pl
from jax.experimental.pallas import tpu as pltpu
from jax.sharding import Mesh, PartitionSpec as P

NEG = -1e30
AXES = ("zh", "x", "core", "y", "zl")
SIZES = (4, 4, 2, 4, 2)
CTX = ("y", "zl")
BF = jnp.bfloat16
F32 = jnp.float32
NT = (((1,), (1,)), ((), ()))
NN = (((1,), (0,)), ((), ()))
TN = (((0,), (0,)), ((), ()))


def dot(a, b, dims):
    return lax.dot_general(a, b, dims, preferred_element_type=F32)


def shifted(value, axes, count, step, wrap):
    pairs = []
    for src in range(count):
        dst = src + step
        if wrap:
            pairs.append((src, dst % count))
        elif 0 <= dst < count:
            pairs.append((src, dst))
    return lax.ppermute(value, axes, pairs)


def attention_kernel(blocks, per, scale, info, starts_ref, q_ref, do_ref, *refs):
    kv_refs, refs = refs[:blocks], refs[blocks:]
    dq_ref, refs = refs[0], refs[1:]
    out_refs, refs = refs[:blocks], refs[blocks:]
    kv_s, kt_s, acc_s, e_s, dp_s, md_s, stat_s, dqt_s = refs
    rows = q_ref.shape[0]
    hd = kt_s.shape[1]
    used, place, limit = info[0], info[1], info[2]
    step = pl.program_id(0)
    power = scale * math.log2(math.e)

    @pl.when(step == 0)
    def _():
        acc_s[...] = jnp.zeros_like(acc_s)
        for d in range(blocks):

            @pl.when(d < used)
            def _():
                kv_s[d] = kv_refs[d][...]
                kt_s[d] = kv_refs[d][:, :hd].astype(F32).T.astype(BF)

    for h in range(per):
        stat_s[0, h] = jnp.full((1, rows), NEG, F32)
        stat_s[1, h] = jnp.zeros((1, rows), F32)
        stat_s[2, h] = jnp.zeros((1, rows), F32)
    dqt_s[...] = jnp.zeros_like(dqt_s)

    def forward(d, masked):
        kd = kv_s[d, :, :hd]
        vd = kv_s[d, :, hd:]
        if masked:
            base = (place - d) * rows
            kp = lax.broadcasted_iota(jnp.int32, (rows, rows), 0) + base
            qp = lax.broadcasted_iota(jnp.int32, (rows, rows), 1) + place * rows
            ok = (kp >= starts_ref[...]) & (kp <= qp)
        for h in range(per):
            cols = slice(h * hd, (h + 1) * hd)
            s = dot(kd, q_ref[:, cols], NT)
            if masked:
                s = jnp.where(ok, s, NEG)
            old = stat_s[0, h]
            top = jnp.maximum(old, jnp.max(s, axis=0, keepdims=True))
            e = jnp.exp2(s * power - top * power)
            alpha = jnp.exp2((old - top) * power)
            dp = dot(vd, do_ref[:, cols], NT)
            stat_s[0, h] = top
            stat_s[1, h] = stat_s[1, h] * alpha + jnp.sum(e, axis=0, keepdims=True)
            stat_s[2, h] = stat_s[2, h] * alpha + jnp.sum(e * dp, axis=0, keepdims=True)
            e_s[d, h] = e
            dp_s[d, h] = dp
            md_s[d, h] = top

    def first(d, carry):
        masked = (d == 0) | ((place - d) * rows < limit)
        pl.when(masked)(lambda: forward(d, True))
        pl.when(jnp.logical_not(masked))(lambda: forward(d, False))
        return carry

    lax.fori_loop(0, used, first, 0)

    tops = [stat_s[0, h] for h in range(per)]
    inverse = [1.0 / stat_s[1, h] for h in range(per)]
    delta = [stat_s[2, h] * inverse[h] for h in range(per)]

    def second(d, carry):
        kt = kt_s[d]
        dk = jnp.zeros((rows, hd), F32)
        dv = jnp.zeros((rows, hd), F32)
        for h in range(per):
            cols = slice(h * hd, (h + 1) * hd)
            p = e_s[d, h] * (jnp.exp2((md_s[d, h] - tops[h]) * power) * inverse[h])
            ds = (p * (dp_s[d, h] - delta[h])).astype(BF)
            dv += dot(p.astype(BF), do_ref[:, cols], NN)
            dk += dot(ds, q_ref[:, cols], NN)
            dqt_s[h] += dot(kt, ds, NN)
        acc_s[d, :, :hd] += dk
        acc_s[d, :, hd:] += dv
        return carry

    lax.fori_loop(0, used, second, 0)

    for h in range(per):
        dq_ref[:, h * hd : (h + 1) * hd] = (dqt_s[h].T * scale).astype(BF)

    @pl.when(step == pl.num_programs(0) - 1)
    def _():
        for d in range(blocks):
            out_refs[d][:, :hd] = (acc_s[d, :, :hd] * scale).astype(BF)
            out_refs[d][:, hd:] = acc_s[d, :, hd:].astype(BF)


def attention(q, do, kv, docs, place):
    rows = q.shape[0]
    hd = kv[0].shape[1] // 2
    heads = q.shape[1] // hd
    blocks = len(kv)
    per = 2
    my_docs = lax.dynamic_slice_in_dim(docs, place * rows, rows)
    starts = jnp.sum((docs[:, None] < my_docs[None, :]).astype(jnp.int32), axis=0)
    info = jnp.stack([place - starts[0] // rows + 1, place, starts[rows - 1]])
    whole = lambda shape: pl.BlockSpec(shape, lambda g: (0,) * len(shape))
    slab = pl.BlockSpec((rows, per * hd), lambda g: (0, g))
    kv_shape = (rows, 2 * hd)
    outs = pl.pallas_call(
        functools.partial(attention_kernel, blocks, per, hd ** (-0.5)),
        grid=(heads // per,),
        in_specs=[pl.BlockSpec(memory_space=pltpu.SMEM), whole((1, rows)), slab, slab]
        + [whole(kv_shape)] * blocks,
        out_specs=[slab] + [whole(kv_shape)] * blocks,
        out_shape=[jax.ShapeDtypeStruct(q.shape, BF)]
        + [jax.ShapeDtypeStruct(kv_shape, BF)] * blocks,
        scratch_shapes=[
            pltpu.VMEM((blocks, rows, 2 * hd), BF),
            pltpu.VMEM((blocks, hd, rows), BF),
            pltpu.VMEM((blocks, rows, 2 * hd), F32),
            pltpu.VMEM((blocks, per, rows, rows), F32),
            pltpu.VMEM((blocks, per, rows, rows), F32),
            pltpu.VMEM((blocks, per, 1, rows), F32),
            pltpu.VMEM((3, per, 1, rows), F32),
            pltpu.VMEM((per, hd, rows), F32),
        ],
        compiler_params=pltpu.CompilerParams(vmem_limit_bytes=40 * 2**20),
        cost_estimate=pl.CostEstimate(
            flops=10 * heads * rows * rows * blocks * hd,
            bytes_accessed=8 * 2**20,
            transcendentals=heads * rows * rows * blocks,
        ),
        name="attention_backward",
    )(info, starts[None, :], q, do, *kv)
    return outs[0], outs[1:]


def local(layer_input, queries, key_head, value_head, grad_output, doc_ids):
    x, q, k, v, do, docs = (
        a[0] for a in (layer_input, queries, key_head, value_head, grad_output, doc_ids)
    )
    rows, hd = k.shape
    dim = x.shape[1]
    ctx = lax.axis_size(CTX)
    nx, nc, z_hi = lax.axis_size("x"), lax.axis_size("core"), lax.axis_size("zh")
    place = lax.axis_index(CTX)
    my_x, my_core = lax.axis_index("x"), lax.axis_index("core")
    wide = dim // (z_hi * nx * nc)

    kv = jnp.concatenate([k, v], axis=1)
    kv_blocks = [kv] + [shifted(kv, CTX, ctx, d, False) for d in range(1, ctx)]

    split = x.reshape(rows, z_hi, nx, nc, wide)

    def owned(core):
        part = lax.dynamic_index_in_dim(split, core, 3, keepdims=False)
        return part.transpose(2, 0, 1, 3).reshape(nx, rows, z_hi * wide)

    kept = owned(my_core)
    given = shifted(owned(1 - my_core), "core", nc, 1, True)
    both = jnp.stack([kept, given], axis=1).reshape(nx, nc * rows, z_hi * wide)
    features = []
    for s in range(nx):
        mine = lax.dynamic_index_in_dim(both, (my_x + s) % nx, 0, keepdims=False)
        features.append(shifted(mine, "x", nx, s, True) if s else mine)

    dq, dkv = attention(q, do, kv_blocks, docs, place)

    total = dkv[0].astype(F32)
    for d in range(1, ctx):
        total = total + shifted(dkv[d], CTX, ctx, -d, False).astype(F32)
    dkv_own = total.astype(BF)

    grads = jnp.concatenate([dq, dkv_own], axis=1)
    along = [grads] + [shifted(grads, "x", nx, s, True) for s in range(1, nx)]
    along = jnp.stack(along)
    other = shifted(along, "core", nc, 1, True)
    grads_all = jnp.stack([along, other], axis=1).reshape(nx * nc * rows, -1)
    part = dot(jnp.concatenate(features, axis=0), grads_all, TN).astype(BF)
    n = part.shape[1]
    y, zl = lax.axis_size("y"), lax.axis_size("zl")
    keep = wide // (y * zl)
    part = part.reshape(z_hi, y, zl * keep * n).transpose(1, 0, 2)
    part = lax.all_to_all(part, "y", 0, 0, tiled=True)
    part = jnp.sum(part.astype(F32), axis=0).astype(BF)
    part = part.reshape(z_hi * zl, keep, n)
    part = lax.all_to_all(part, ("zh", "zl"), 0, 0, tiled=True)
    tokens = rows * ctx * nx * nc * z_hi
    weight = jnp.sum(part.astype(F32), axis=0) * (1.0 / math.sqrt(tokens))
    width = q.shape[1]
    return (
        dq[None],
        dkv_own[None, :, :hd],
        dkv_own[None, :, hd:],
        weight[:, :width],
        weight[:, width : width + hd],
        weight[:, width + hd :],
    )


def solution(mesh):
    fine = Mesh(mesh.devices.reshape(SIZES), AXES)
    dp = ("zh", "x", "core")
    tok = P(dp, CTX, None)
    row = P(dp + CTX, None)
    return jax.shard_map(
        local,
        mesh=fine,
        in_specs=(tok, tok, tok, tok, tok, P(dp, None)),
        out_specs=(tok, tok, tok, row, row, row),
        check_vma=False,
    )
```

```python
import functools
import math

import jax
import jax.numpy as jnp
from jax import lax
from jax.experimental import pallas as pl
from jax.experimental.pallas import tpu as pltpu
from jax.sharding import Mesh, PartitionSpec as P

NEG = -1e30
AXES = ("zh", "x", "core", "y", "zl")
SIZES = (4, 4, 2, 4, 2)
CTX = ("y", "zl")
BF = jnp.bfloat16
F32 = jnp.float32
NT = (((1,), (1,)), ((), ()))
NN = (((1,), (0,)), ((), ()))
TN = (((0,), (0,)), ((), ()))


def dot(a, b, dims):
    return lax.dot_general(a, b, dims, preferred_element_type=F32)


def shifted(value, axes, count, step, wrap):
    pairs = []
    for src in range(count):
        dst = src + step
        if wrap:
            pairs.append((src, dst % count))
        elif 0 <= dst < count:
            pairs.append((src, dst))
    return lax.ppermute(value, axes, pairs)


def attention_kernel(blocks, per, scale, info, starts_ref, q_ref, do_ref, *refs):
    kv_refs, refs = refs[:blocks], refs[blocks:]
    dq_ref, refs = refs[0], refs[1:]
    out_refs, refs = refs[:blocks], refs[blocks:]
    kv_s, kt_s, acc_s, e_s, dp_s, md_s, stat_s, dqt_s = refs
    rows = q_ref.shape[0]
    hd = kt_s.shape[1]
    used, place, limit = info[0], info[1], info[2]
    step = pl.program_id(0)
    power = scale * math.log2(math.e)

    @pl.when(step == 0)
    def _():
        acc_s[...] = jnp.zeros_like(acc_s)
        for d in range(blocks):

            @pl.when(d < used)
            def _():
                kv_s[d] = kv_refs[d][...]
                kt_s[d] = kv_refs[d][:, :hd].astype(F32).T.astype(BF)

    for h in range(per):
        stat_s[0, h] = jnp.full((1, rows), NEG, F32)
        stat_s[1, h] = jnp.zeros((1, rows), F32)
        stat_s[2, h] = jnp.zeros((1, rows), F32)
    dqt_s[...] = jnp.zeros_like(dqt_s)

    def forward(d, masked):
        kd = kv_s[d, :, :hd]
        vd = kv_s[d, :, hd:]
        if masked:
            base = (place - d) * rows
            kp = lax.broadcasted_iota(jnp.int32, (rows, rows), 0) + base
            qp = lax.broadcasted_iota(jnp.int32, (rows, rows), 1) + place * rows
            ok = (kp >= starts_ref[...]) & (kp <= qp)
        for h in range(per):
            cols = slice(h * hd, (h + 1) * hd)
            s = dot(kd, q_ref[:, cols], NT)
            if masked:
                s = jnp.where(ok, s, NEG)
            old = stat_s[0, h]
            top = jnp.maximum(old, jnp.max(s, axis=0, keepdims=True))
            e = jnp.exp2(s * power - top * power)
            alpha = jnp.exp2((old - top) * power)
            dp = dot(vd, do_ref[:, cols], NT)
            stat_s[0, h] = top
            stat_s[1, h] = stat_s[1, h] * alpha + jnp.sum(e, axis=0, keepdims=True)
            stat_s[2, h] = stat_s[2, h] * alpha + jnp.sum(e * dp, axis=0, keepdims=True)
            e_s[d, h] = e
            dp_s[d, h] = dp
            md_s[d, h] = top

    def first(d, carry):
        masked = (d == 0) | ((place - d) * rows < limit)
        pl.when(masked)(lambda: forward(d, True))
        pl.when(jnp.logical_not(masked))(lambda: forward(d, False))
        return carry

    lax.fori_loop(0, used, first, 0)

    tops = [stat_s[0, h] for h in range(per)]
    inverse = [1.0 / stat_s[1, h] for h in range(per)]
    delta = [stat_s[2, h] * inverse[h] for h in range(per)]

    def second(d, carry):
        kt = kt_s[d]
        dk = jnp.zeros((rows, hd), F32)
        dv = jnp.zeros((rows, hd), F32)
        for h in range(per):
            cols = slice(h * hd, (h + 1) * hd)
            p = e_s[d, h] * (jnp.exp2((md_s[d, h] - tops[h]) * power) * inverse[h])
            ds = (p * (dp_s[d, h] - delta[h])).astype(BF)
            dv += dot(p.astype(BF), do_ref[:, cols], NN)
            dk += dot(ds, q_ref[:, cols], NN)
            dqt_s[h] += dot(kt, ds, NN)
        acc_s[d, :, :hd] += dk
        acc_s[d, :, hd:] += dv
        return carry

    lax.fori_loop(0, used, second, 0)

    for h in range(per):
        dq_ref[:, h * hd : (h + 1) * hd] = (dqt_s[h].T * scale).astype(BF)

    @pl.when(step == pl.num_programs(0) - 1)
    def _():
        for d in range(blocks):
            out_refs[d][:, :hd] = (acc_s[d, :, :hd] * scale).astype(BF)
            out_refs[d][:, hd:] = acc_s[d, :, hd:].astype(BF)


def attention(q, do, kv, docs, place):
    rows = q.shape[0]
    hd = kv[0].shape[1] // 2
    heads = q.shape[1] // hd
    blocks = len(kv)
    per = 2
    my_docs = lax.dynamic_slice_in_dim(docs, place * rows, rows)
    starts = jnp.sum((docs[:, None] < my_docs[None, :]).astype(jnp.int32), axis=0)
    info = jnp.stack([place - starts[0] // rows + 1, place, starts[rows - 1]])
    whole = lambda shape: pl.BlockSpec(shape, lambda g: (0,) * len(shape))
    slab = pl.BlockSpec((rows, per * hd), lambda g: (0, g))
    kv_shape = (rows, 2 * hd)
    outs = pl.pallas_call(
        functools.partial(attention_kernel, blocks, per, hd ** (-0.5)),
        grid=(heads // per,),
        in_specs=[pl.BlockSpec(memory_space=pltpu.SMEM), whole((1, rows)), slab, slab]
        + [whole(kv_shape)] * blocks,
        out_specs=[slab] + [whole(kv_shape)] * blocks,
        out_shape=[jax.ShapeDtypeStruct(q.shape, BF)]
        + [jax.ShapeDtypeStruct(kv_shape, BF)] * blocks,
        scratch_shapes=[
            pltpu.VMEM((blocks, rows, 2 * hd), BF),
            pltpu.VMEM((blocks, hd, rows), BF),
            pltpu.VMEM((blocks, rows, 2 * hd), F32),
            pltpu.VMEM((blocks, per, rows, rows), F32),
            pltpu.VMEM((blocks, per, rows, rows), F32),
            pltpu.VMEM((blocks, per, 1, rows), F32),
            pltpu.VMEM((3, per, 1, rows), F32),
            pltpu.VMEM((per, hd, rows), F32),
        ],
        compiler_params=pltpu.CompilerParams(vmem_limit_bytes=40 * 2**20),
        cost_estimate=pl.CostEstimate(
            flops=10 * heads * rows * rows * blocks * hd,
            bytes_accessed=8 * 2**20,
            transcendentals=heads * rows * rows * blocks,
        ),
        name="attention_backward",
    )(info, starts[None, :], q, do, *kv)
    return outs[0], outs[1:]


def split_kernel(info, *refs):
    half = len(refs) // 2
    for src, dst in zip(refs[:half], refs[half:]):
        dst[...] = src[...]


def split_features(x, my_x, z_hi, nx):
    rows, dim = x.shape
    wide = dim // (z_hi * nx)

    def source(s):
        return pl.BlockSpec((rows, wide), lambda g, info: (0, g * nx + (info[0] + s) % nx))

    return pl.pallas_call(
        split_kernel,
        grid_spec=pltpu.PrefetchScalarGridSpec(
            num_scalar_prefetch=1,
            grid=(z_hi,),
            in_specs=[source(s) for s in range(1, nx)],
            out_specs=[pl.BlockSpec((rows, wide), lambda g, info: (0, g))] * (nx - 1),
        ),
        out_shape=[jax.ShapeDtypeStruct((rows, z_hi * wide), x.dtype)] * (nx - 1),
        compiler_params=pltpu.CompilerParams(vmem_limit_bytes=16 * 2**20),
        name="split_features",
    )(my_x[None], *([x] * (nx - 1)))


def weight_kernel(nx, z_hi, ny, info, x_ref, *refs):
    f_refs, g_refs, out_ref, ft_s = refs[: nx - 1], refs[nx - 1 : 2 * nx - 1], refs[-2], refs[-1]
    rows = x_ref.shape[0]
    wide = x_ref.shape[1] // (z_hi * nx * 2)
    my_x, which = info[0], info[1]

    @pl.when(pl.program_id(0) == 0)
    def _():
        for s in range(nx):
            for z in range(z_hi):
                if s == 0:
                    at = pl.multiple_of(((z * nx + my_x) * 2 + which) * wide, wide)
                    block = x_ref[:, pl.ds(at, wide)]
                else:
                    at = pl.multiple_of((z * 2 + which) * wide, wide)
                    block = f_refs[s - 1][:, pl.ds(at, wide)]
                ft_s[z * wide : (z + 1) * wide, s * rows : (s + 1) * rows] = (
                    block.astype(F32).T.astype(BF)
                )

    total = dot(ft_s[:, :rows], g_refs[0][...], NN)
    for s in range(1, nx):
        total += dot(ft_s[:, s * rows : (s + 1) * rows], g_refs[s][...], NN)
    total = total.astype(BF)
    part = wide // ny
    for z in range(z_hi):
        for y in range(ny):
            at = z * wide + y * part
            out_ref[y, z] = total[at : at + part]


def weight_part(x, features, grads, my_x, which, z_hi, ny):
    nx = len(grads)
    rows, dim = x.shape
    n = grads[0].shape[1]
    wide = dim // (z_hi * nx * 2)
    cols = min(n, 256)
    whole = lambda shape: pl.BlockSpec(shape, lambda g: (0,) * len(shape))
    return pl.pallas_call(
        functools.partial(weight_kernel, nx, z_hi, ny),
        grid=(n // cols,),
        in_specs=[pl.BlockSpec(memory_space=pltpu.SMEM), whole(x.shape)]
        + [whole(features[0].shape)] * (nx - 1)
        + [pl.BlockSpec((rows, cols), lambda g: (0, g))] * nx,
        out_specs=pl.BlockSpec((ny, z_hi, wide // ny, cols), lambda g: (0, 0, 0, g)),
        out_shape=jax.ShapeDtypeStruct((ny, z_hi, wide // ny, n), BF),
        scratch_shapes=[pltpu.VMEM((z_hi * wide, nx * rows), BF)],
        compiler_params=pltpu.CompilerParams(vmem_limit_bytes=32 * 2**20),
        cost_estimate=pl.CostEstimate(
            flops=2 * z_hi * wide * nx * rows * n,
            bytes_accessed=6 * 2**20,
            transcendentals=0,
        ),
        name="weight_part",
    )(jnp.stack([my_x, which]), x, *features, *grads)


def local(layer_input, queries, key_head, value_head, grad_output, doc_ids):
    x, q, k, v, do, docs = (
        a[0] for a in (layer_input, queries, key_head, value_head, grad_output, doc_ids)
    )
    rows, hd = k.shape
    ctx = lax.axis_size(CTX)
    nx, nc, z_hi = lax.axis_size("x"), lax.axis_size("core"), lax.axis_size("zh")
    y, zl = lax.axis_size("y"), lax.axis_size("zl")
    place = lax.axis_index(CTX)
    my_x, my_core = lax.axis_index("x"), lax.axis_index("core")

    kv = jnp.concatenate([k, v], axis=1)
    kv_blocks = [kv] + [shifted(kv, CTX, ctx, d, False) for d in range(1, ctx)]
    features = [
        shifted(part, "x", nx, s + 1, True)
        for s, part in enumerate(split_features(x, my_x, z_hi, nx))
    ]

    dq, dkv = attention(q, do, kv_blocks, docs, place)
    dq, *features = lax.optimization_barrier((dq, *features))

    def term(grads):
        along = [grads] + [shifted(grads, "x", nx, s, True) for s in range(1, nx)]
        theirs = weight_part(x, features, along, my_x, 1 - my_core, z_hi, y)
        theirs = shifted(theirs, "core", nc, 1, True)
        mine = weight_part(x, features, along, my_x, my_core, z_hi, y)
        return mine.astype(F32) + theirs.astype(F32)

    total = dkv[0].astype(F32)
    for d in range(1, ctx):
        total = total + shifted(dkv[d], CTX, ctx, -d, False).astype(F32)
    dkv_own = total.astype(BF)

    part = jnp.concatenate([term(dq), term(dkv_own)], axis=-1).astype(BF)
    n = part.shape[-1]
    part = lax.all_to_all(part.reshape(y, -1, n), "y", 0, 0, tiled=True)
    part = jnp.sum(part.astype(F32), axis=0).astype(BF)
    part = lax.all_to_all(part.reshape(z_hi * zl, -1, n), ("zh", "zl"), 0, 0, tiled=True)
    tokens = rows * ctx * nx * nc * z_hi
    weight = jnp.sum(part.astype(F32), axis=0) * (1.0 / math.sqrt(tokens))
    width = q.shape[1]
    return (
        dq[None],
        dkv_own[None, :, :hd],
        dkv_own[None, :, hd:],
        weight[:, :width],
        weight[:, width : width + hd],
        weight[:, width + hd :],
    )


def solution(mesh):
    fine = Mesh(mesh.devices.reshape(SIZES), AXES)
    dp = ("zh", "x", "core")
    tok = P(dp, CTX, None)
    row = P(dp + CTX, None)
    return jax.shard_map(
        local,
        mesh=fine,
        in_specs=(tok, tok, tok, tok, tok, P(dp, None)),
        out_specs=(tok, tok, tok, row, row, row),
        check_vma=False,
    )
```

```python
import functools
import math

import jax
import jax.numpy as jnp
from jax import lax
from jax.experimental import pallas as pl
from jax.experimental.pallas import tpu as pltpu
from jax.sharding import Mesh, PartitionSpec as P

NEG = -1e30
AXES = ("zh", "x", "core", "y", "zl")
SIZES = (4, 4, 2, 4, 2)
CTX = ("y", "zl")
HALVES = 2
BF = jnp.bfloat16
F32 = jnp.float32
NN = (((1,), (0,)), ((), ()))


def dot(a, b):
    return lax.dot_general(a, b, NN, preferred_element_type=F32)


def shifted(value, axis, count, step, wrap=True):
    pairs = []
    for src in range(count):
        dst = src + step
        if wrap:
            pairs.append((src, dst % count))
        elif 0 <= dst < count:
            pairs.append((src, dst))
    return lax.ppermute(value, axis, pairs)


def whole(shape):
    return pl.BlockSpec(shape, lambda *g: (0,) * len(shape))


def attention_kernel(ny, per, scale, last, info, starts_ref, q_ref, do_ref, *refs):
    kv_refs, refs = refs[:ny], refs[ny:]
    if last:
        old_refs, refs = refs[:ny], refs[ny:]
    dq_ref, refs = refs[0], refs[1:]
    out_refs, refs = refs[:ny], refs[ny:]
    kv_s, kt_s, acc_s, e_s, dp_s, md_s, stat_s, dqt_s, qt_s, dot_s, p_s, ds_s, qk_s, dk_s, sem = refs
    rows = q_ref.shape[0]
    hd = kt_s.shape[1]
    used, place, limit = info[0], info[1], info[2]
    power = scale * math.log2(math.e)
    farthest = place // 2 - (place - used + 1) // 2

    for s in range(ny):

        @pl.when(s <= farthest)
        def _():
            pltpu.make_async_copy(kv_refs[s], kv_s.at[pl.ds(2 * s, 2)], sem.at[s]).start()

    for s in range(ny):
        for k in range(2):
            if last:
                acc_s[2 * s + k] = old_refs[s][k].astype(F32)
            else:
                acc_s[2 * s + k] = jnp.zeros(acc_s.shape[1:], F32)
    for h in range(per):
        cols = slice(h * hd, (h + 1) * hd)
        span = slice(h * rows, (h + 1) * rows)
        qk_s[span] = q_ref[:, cols]
        dk_s[span] = do_ref[:, cols]
        qt_s[h] = q_ref[:, cols].T
        dot_s[h] = do_ref[:, cols].T
        stat_s[0, h] = jnp.full((1, rows), NEG, F32)
        stat_s[1, h] = jnp.zeros((1, rows), F32)
        stat_s[2, h] = jnp.zeros((1, rows), F32)
    dqt_s[...] = jnp.zeros_like(dqt_s)

    for s in range(ny):

        @pl.when(s <= farthest)
        def _():
            pltpu.make_async_copy(kv_refs[s], kv_s.at[pl.ds(2 * s, 2)], sem.at[s]).wait()
            for k in range(2):
                kt_s[2 * s + k] = kv_s[2 * s + k, :, :hd].T

    def slot(d):
        block = place - d
        return 2 * (place // 2 - block // 2) + (d % 2)

    def forward(d, masked):
        at = slot(d)
        kd = kv_s[at, :, :hd]
        vd = kv_s[at, :, hd:]
        if masked:
            kp = lax.broadcasted_iota(jnp.int32, (rows, rows), 0) + (place - d) * rows
            qp = lax.broadcasted_iota(jnp.int32, (rows, rows), 1) + place * rows
            ok = (kp >= starts_ref[...]) & (kp <= qp)
        for h in range(per):
            s = dot(kd, qt_s[h])
            if masked:
                s = jnp.where(ok, s, NEG)
            old = stat_s[0, h]
            top = jnp.maximum(old, jnp.max(s, axis=0, keepdims=True))
            e = jnp.exp2(s * power - top * power)
            alpha = jnp.exp2((old - top) * power)
            dp = dot(vd, dot_s[h])
            stat_s[0, h] = top
            stat_s[1, h] = stat_s[1, h] * alpha + jnp.sum(e, axis=0, keepdims=True)
            stat_s[2, h] = stat_s[2, h] * alpha + jnp.sum(e * dp, axis=0, keepdims=True)
            e_s[d, h] = e
            dp_s[d, h] = dp
            md_s[d, h] = top

    def first(d, carry):
        masked = (d == 0) | ((place - d) * rows < limit)
        pl.when(masked)(lambda: forward(d, True))
        pl.when(jnp.logical_not(masked))(lambda: forward(d, False))
        return carry

    lax.fori_loop(0, used, first, 0)

    tops = [stat_s[0, h] for h in range(per)]
    inverse = [1.0 / stat_s[1, h] for h in range(per)]
    delta = [stat_s[2, h] * inverse[h] for h in range(per)]

    def second(d, carry):
        at = slot(d)
        for h in range(per):
            p = e_s[d, h] * (jnp.exp2((md_s[d, h] - tops[h]) * power) * inverse[h])
            p_s[:, h * rows : (h + 1) * rows] = p.astype(BF)
            ds_s[:, h * rows : (h + 1) * rows] = (p * (dp_s[d, h] - delta[h])).astype(BF)
        acc_s[at, :, hd:] += dot(p_s[...], dk_s[...])
        acc_s[at, :, :hd] += dot(ds_s[...], qk_s[...])
        dqt_s[...] += dot(kt_s[at], ds_s[...])
        return carry

    lax.fori_loop(0, used, second, 0)

    for h in range(per):
        dq_ref[:, h * hd : (h + 1) * hd] = (dqt_s[:, h * rows : (h + 1) * rows].T * scale).astype(BF)
    for s in range(ny):
        for k in range(2):
            at = 2 * s + k
            dk = acc_s[at, :, :hd]
            out_refs[s][k, :, :hd] = (dk * scale if last else dk).astype(BF)
            out_refs[s][k, :, hd:] = acc_s[at, :, hd:].astype(BF)


def attention_half(q, do, kv, info, starts, half, old):
    rows = q.shape[0]
    hd = kv[0].shape[2] // 2
    width = q.shape[1] // HALVES
    per = width // hd
    ny = len(kv)
    blocks = 2 * ny
    last = old is not None
    slab = pl.BlockSpec((rows, width), lambda g: (0, half))
    pair = kv[0].shape
    outs = pl.pallas_call(
        functools.partial(attention_kernel, ny, per, hd ** (-0.5), last),
        grid=(1,),
        in_specs=[pl.BlockSpec(memory_space=pltpu.SMEM), whole((1, rows)), slab, slab]
        + [pl.BlockSpec(memory_space=pl.ANY)] * ny
        + ([whole(pair)] * ny if last else []),
        out_specs=[whole((rows, width))] + [whole(pair)] * ny,
        out_shape=[jax.ShapeDtypeStruct((rows, width), BF)] + [jax.ShapeDtypeStruct(pair, BF)] * ny,
        scratch_shapes=[
            pltpu.VMEM((blocks, rows, 2 * hd), BF),
            pltpu.VMEM((blocks, hd, rows), BF),
            pltpu.VMEM((blocks, rows, 2 * hd), F32),
            pltpu.VMEM((blocks, per, rows, rows), F32),
            pltpu.VMEM((blocks, per, rows, rows), F32),
            pltpu.VMEM((blocks, per, 1, rows), F32),
            pltpu.VMEM((3, per, 1, rows), F32),
            pltpu.VMEM((hd, per * rows), F32),
            pltpu.VMEM((per, hd, rows), BF),
            pltpu.VMEM((per, hd, rows), BF),
            pltpu.VMEM((rows, per * rows), BF),
            pltpu.VMEM((rows, per * rows), BF),
            pltpu.VMEM((per * rows, hd), BF),
            pltpu.VMEM((per * rows, hd), BF),
            pltpu.SemaphoreType.DMA((ny,)),
        ],
        compiler_params=pltpu.CompilerParams(vmem_limit_bytes=28 * 2**20),
        cost_estimate=pl.CostEstimate(
            flops=10 * per * rows * rows * blocks * hd * 2,
            bytes_accessed=4 * 2**20,
            transcendentals=per * rows * rows * blocks,
        ),
        name="attention_backward",
    )(info, starts, q, do, *kv, *(old or []))
    return outs[0], outs[1:]


def split_kernel(info, *refs):
    half = len(refs) // 2
    for src, dst in zip(refs[:half], refs[half:]):
        dst[...] = src[...].T


def split_features(x, my_x, z_hi, nx):
    rows, dim = x.shape
    wide = dim // (z_hi * nx)

    def source(s):
        return pl.BlockSpec((rows, wide), lambda g, info: (0, g * nx + (info[0] + s) % nx))

    return pl.pallas_call(
        split_kernel,
        grid_spec=pltpu.PrefetchScalarGridSpec(
            num_scalar_prefetch=1,
            grid=(z_hi,),
            in_specs=[source(s) for s in range(nx)],
            out_specs=[pl.BlockSpec((wide, rows), lambda g, info: (g, 0))] * nx,
        ),
        out_shape=[jax.ShapeDtypeStruct((z_hi * wide, rows), x.dtype)] * nx,
        compiler_params=pltpu.CompilerParams(vmem_limit_bytes=16 * 2**20),
        name="split_features",
    )(my_x[None], *([x] * nx))


def weight_kernel(nx, parts, z_hi, ny, info, *refs):
    f_refs, g_refs, (out_ref, ft_s, total_s) = refs[:nx], refs[nx:-3], refs[-3:]
    rows = f_refs[0].shape[1]
    wide = f_refs[0].shape[0] // (z_hi * 2)
    which, my_y = info[0], info[1]
    step = pl.program_id(0)
    each = pl.num_programs(0) // parts

    @pl.when(step == 0)
    def _():
        for s in range(nx):
            for z in range(z_hi):
                at = pl.multiple_of((z * 2 + which) * wide, wide)
                ft_s[z * wide : (z + 1) * wide, s * rows : (s + 1) * rows] = f_refs[s][pl.ds(at, wide)]

    for i in range(parts):

        @pl.when(step // each == i)
        def _():
            total = dot(ft_s[:, :rows], g_refs[i * nx][...])
            for s in range(1, nx):
                total += dot(ft_s[:, s * rows : (s + 1) * rows], g_refs[i * nx + s][...])
            total_s[...] = total.astype(BF)

    part = wide // ny
    for z in range(z_hi):
        for r in range(ny):
            at = pl.multiple_of(z * wide + (my_y + r) % ny * part, part)
            out_ref[r, z] = total_s[pl.ds(at, part)]


def weight_part(features, grads, which, my_y, z_hi, ny):
    nx = len(features)
    parts = len(grads)
    rows, n = grads[0][0].shape
    wide = features[0].shape[0] // (z_hi * 2)
    cols = min(n, 256)
    each = n // cols

    def block(i):
        return pl.BlockSpec((rows, cols), lambda g: (0, jnp.clip(g - i * each, 0, each - 1)))

    return pl.pallas_call(
        functools.partial(weight_kernel, nx, parts, z_hi, ny),
        grid=(parts * each,),
        in_specs=[pl.BlockSpec(memory_space=pltpu.SMEM)]
        + [whole(features[0].shape)] * nx
        + [block(i) for i in range(parts) for _ in range(nx)],
        out_specs=pl.BlockSpec((ny, z_hi, wide // ny, cols), lambda g: (0, 0, 0, g)),
        out_shape=jax.ShapeDtypeStruct((ny, z_hi, wide // ny, parts * n), BF),
        scratch_shapes=[
            pltpu.VMEM((z_hi * wide, nx * rows), BF),
            pltpu.VMEM((z_hi * wide, cols), BF),
        ],
        compiler_params=pltpu.CompilerParams(vmem_limit_bytes=24 * 2**20),
        cost_estimate=pl.CostEstimate(
            flops=2 * z_hi * wide * nx * rows * parts * n,
            bytes_accessed=6 * 2**20,
            transcendentals=0,
        ),
        name="weight_part",
    )(jnp.stack([which, my_y]), *features, *[g for group in grads for g in group])


def local(layer_input, queries, key_head, value_head, grad_output, doc_ids):
    x, q, k, v, do, docs = (
        a[0] for a in (layer_input, queries, key_head, value_head, grad_output, doc_ids)
    )
    rows, hd = k.shape
    ctx = lax.axis_size(CTX)
    nx, nc, z_hi = lax.axis_size("x"), lax.axis_size("core"), lax.axis_size("zh")
    ny, zl = lax.axis_size("y"), lax.axis_size("zl")
    place = lax.axis_index(CTX)
    my_x, my_core, my_y = lax.axis_index("x"), lax.axis_index("core"), lax.axis_index("y")

    kv = jnp.concatenate([k, v], axis=1)
    pair = jnp.stack([kv, shifted(kv, "zl", zl, 1)])
    kv_pairs = [pair] + [shifted(pair, "y", ny, s, False) for s in range(1, ny)]
    features = [
        shifted(part, "x", nx, s) if s else part
        for s, part in enumerate(split_features(x, my_x, z_hi, nx))
    ]

    my_docs = lax.dynamic_slice_in_dim(docs, place * rows, rows)
    starts = jnp.sum((docs[:, None] < my_docs[None, :]).astype(jnp.int32), axis=0)
    info = jnp.stack([place - starts[0] // rows + 1, place, starts[rows - 1]])
    starts = starts[None, :]

    def along_x(grads):
        return [grads] + [shifted(grads, "x", nx, s) for s in range(1, nx)]

    def term(grads):
        theirs = weight_part(features, grads, 1 - my_core, my_y, z_hi, ny)
        theirs = shifted(theirs, "core", nc, 1)
        mine = weight_part(features, grads, my_core, my_y, z_hi, ny)
        return [(mine[r].astype(F32) + theirs[r].astype(F32)).astype(BF) for r in range(ny)]

    def along_y(pieces):
        total = pieces[0].astype(F32)
        for r in range(1, ny):
            total = total + shifted(pieces[r], "y", ny, r).astype(F32)
        return total.astype(BF)

    dq_first, dkv = attention_half(q, do, kv_pairs, info, starts, 0, None)
    dq_first, *features = lax.optimization_barrier((dq_first, *features))
    first = along_x(dq_first)
    dq_second, dkv = attention_half(q, do, kv_pairs, info, starts, 1, dkv)
    dq_second, dkv, first = lax.optimization_barrier((dq_second, dkv, first))
    second = along_x(dq_second)

    total = dkv[0].astype(F32)
    for s in range(1, ny):
        total = total + shifted(dkv[s], "y", ny, -s, False).astype(F32)
    other = shifted(total[1].astype(BF), "zl", zl, 1)
    dkv_own = (total[0] + other.astype(F32)).astype(BF)

    pieces = term([first, second])
    pieces, along = lax.optimization_barrier((pieces, along_x(dkv_own)))
    part = jnp.concatenate([along_y(pieces), along_y(term([along]))], axis=-1)
    n = part.shape[-1]
    part = lax.all_to_all(part.reshape(z_hi * zl, -1, n), ("zh", "zl"), 0, 0, tiled=True)
    tokens = rows * ctx * nx * nc * z_hi
    weight = jnp.sum(part.astype(F32), axis=0) * (1.0 / math.sqrt(tokens))
    width = q.shape[1]
    dq = jnp.concatenate([dq_first, dq_second], axis=1)
    return (
        dq[None],
        dkv_own[None, :, :hd],
        dkv_own[None, :, hd:],
        weight[:, :width],
        weight[:, width : width + hd],
        weight[:, width + hd :],
    )


def solution(mesh):
    fine = Mesh(mesh.devices.reshape(SIZES), AXES)
    dp = ("zh", "x", "core")
    tok = P(dp, CTX, None)
    row = P(dp + CTX, None)
    return jax.shard_map(
        local,
        mesh=fine,
        in_specs=(tok, tok, tok, tok, tok, P(dp, None)),
        out_specs=(tok, tok, tok, row, row, row),
        check_vma=False,
    )
```

```python
import functools
import math

import jax
import jax.numpy as jnp
from jax import lax
from jax.experimental import pallas as pl
from jax.experimental.pallas import tpu as pltpu
from jax.sharding import Mesh, PartitionSpec as P

NEG = -1e30
AXES = ("zh", "x", "core", "y", "zl")
SIZES = (4, 4, 2, 4, 2)
CTX = ("y", "zl")
BF = jnp.bfloat16
F32 = jnp.float32
NN = (((1,), (0,)), ((), ()))


def dot(a, b):
    return lax.dot_general(a, b, NN, preferred_element_type=F32)


def shifted(value, axis, count, step, wrap=True):
    pairs = []
    for src in range(count):
        dst = src + step
        if wrap:
            pairs.append((src, dst % count))
        elif 0 <= dst < count:
            pairs.append((src, dst))
    return lax.ppermute(value, axis, pairs)


def plus(a, b):
    return (a.astype(F32) + b.astype(F32)).astype(BF)


def whole(shape):
    return pl.BlockSpec(shape, lambda *g: (0,) * len(shape))


def attention_kernel(ny, per, scale, info, starts_ref, q_ref, do_ref, *refs):
    kv_refs, refs = refs[:ny], refs[ny:]
    dq_ref, refs = refs[0], refs[1:]
    out_refs, refs = refs[:ny], refs[ny:]
    kv_s, kt_s, acc_s, e_s, dp_s, md_s, stat_s, dqt_s, qt_s, dot_s, p_s, ds_s, qk_s, dk_s, sem = refs
    rows = q_ref.shape[0]
    hd = kt_s.shape[1]
    used, place, limit = info[0], info[1], info[2]
    power = scale * math.log2(math.e)
    farthest = place // 2 - (place - used + 1) // 2

    for s in range(ny):

        @pl.when(s <= farthest)
        def _():
            pltpu.make_async_copy(kv_refs[s], kv_s.at[pl.ds(2 * s, 2)], sem.at[s]).start()

    acc_s[...] = jnp.zeros_like(acc_s)
    for h in range(per):
        cols = slice(h * hd, (h + 1) * hd)
        span = slice(h * rows, (h + 1) * rows)
        qk_s[span] = q_ref[:, cols]
        dk_s[span] = do_ref[:, cols]
        qt_s[h] = q_ref[:, cols].T
        dot_s[h] = do_ref[:, cols].T
        stat_s[0, h] = jnp.full((1, rows), NEG, F32)
        stat_s[1, h] = jnp.zeros((1, rows), F32)
        stat_s[2, h] = jnp.zeros((1, rows), F32)
    dqt_s[...] = jnp.zeros_like(dqt_s)

    for s in range(ny):

        @pl.when(s <= farthest)
        def _():
            pltpu.make_async_copy(kv_refs[s], kv_s.at[pl.ds(2 * s, 2)], sem.at[s]).wait()
            for k in range(2):
                kt_s[2 * s + k] = kv_s[2 * s + k, :, :hd].T

    def slot(d):
        block = place - d
        return 2 * (place // 2 - block // 2) + (d % 2)

    def forward(d, masked):
        at = slot(d)
        kd = kv_s[at, :, :hd]
        vd = kv_s[at, :, hd:]
        if masked:
            kp = lax.broadcasted_iota(jnp.int32, (rows, rows), 0) + (place - d) * rows
            qp = lax.broadcasted_iota(jnp.int32, (rows, rows), 1) + place * rows
            ok = (kp >= starts_ref[...]) & (kp <= qp)
        for h in range(per):
            s = dot(kd, qt_s[h])
            if masked:
                s = jnp.where(ok, s, NEG)
            old = stat_s[0, h]
            top = jnp.maximum(old, jnp.max(s, axis=0, keepdims=True))
            e = jnp.exp2(s * power - top * power)
            alpha = jnp.exp2((old - top) * power)
            dp = dot(vd, dot_s[h])
            stat_s[0, h] = top
            stat_s[1, h] = stat_s[1, h] * alpha + jnp.sum(e, axis=0, keepdims=True)
            stat_s[2, h] = stat_s[2, h] * alpha + jnp.sum(e * dp, axis=0, keepdims=True)
            e_s[d, h] = e
            dp_s[d, h] = dp
            md_s[d, h] = top

    def first(d, carry):
        masked = (d == 0) | ((place - d) * rows < limit)
        pl.when(masked)(lambda: forward(d, True))
        pl.when(jnp.logical_not(masked))(lambda: forward(d, False))
        return carry

    lax.fori_loop(0, used, first, 0)

    tops = [stat_s[0, h] for h in range(per)]
    inverse = [1.0 / stat_s[1, h] for h in range(per)]
    delta = [stat_s[2, h] * inverse[h] for h in range(per)]

    def second(d, carry):
        at = slot(d)
        for h in range(per):
            p = e_s[d, h] * (jnp.exp2((md_s[d, h] - tops[h]) * power) * inverse[h])
            p_s[:, h * rows : (h + 1) * rows] = p.astype(BF)
            ds_s[:, h * rows : (h + 1) * rows] = (p * (dp_s[d, h] - delta[h])).astype(BF)
        acc_s[at, :, hd:] += dot(p_s[...], dk_s[...])
        acc_s[at, :, :hd] += dot(ds_s[...], qk_s[...])
        dqt_s[...] += dot(kt_s[at], ds_s[...])
        return carry

    lax.fori_loop(0, used, second, 0)

    for h in range(per):
        dq_ref[:, h * hd : (h + 1) * hd] = (dqt_s[:, h * rows : (h + 1) * rows].T * scale).astype(BF)
    for s in range(ny):
        for k in range(2):
            at = 2 * s + k
            out_refs[s][k, :, :hd] = (acc_s[at, :, :hd] * scale).astype(BF)
            out_refs[s][k, :, hd:] = acc_s[at, :, hd:].astype(BF)


def attention(q, do, kv, info, starts):
    rows = q.shape[0]
    hd = kv[0].shape[2] // 2
    width = q.shape[1]
    per = width // hd
    ny = len(kv)
    blocks = 2 * ny
    slab = whole((rows, width))
    pair = kv[0].shape
    outs = pl.pallas_call(
        functools.partial(attention_kernel, ny, per, hd ** (-0.5)),
        grid=(1,),
        in_specs=[pl.BlockSpec(memory_space=pltpu.SMEM), whole((1, rows)), slab, slab]
        + [pl.BlockSpec(memory_space=pl.ANY)] * ny,
        out_specs=[whole((rows, width))] + [whole(pair)] * ny,
        out_shape=[jax.ShapeDtypeStruct((rows, width), BF)] + [jax.ShapeDtypeStruct(pair, BF)] * ny,
        scratch_shapes=[
            pltpu.VMEM((blocks, rows, 2 * hd), BF),
            pltpu.VMEM((blocks, hd, rows), BF),
            pltpu.VMEM((blocks, rows, 2 * hd), F32),
            pltpu.VMEM((blocks, per, rows, rows), F32),
            pltpu.VMEM((blocks, per, rows, rows), F32),
            pltpu.VMEM((blocks, per, 1, rows), F32),
            pltpu.VMEM((3, per, 1, rows), F32),
            pltpu.VMEM((hd, per * rows), F32),
            pltpu.VMEM((per, hd, rows), BF),
            pltpu.VMEM((per, hd, rows), BF),
            pltpu.VMEM((rows, per * rows), BF),
            pltpu.VMEM((rows, per * rows), BF),
            pltpu.VMEM((per * rows, hd), BF),
            pltpu.VMEM((per * rows, hd), BF),
            pltpu.SemaphoreType.DMA((ny,)),
        ],
        compiler_params=pltpu.CompilerParams(vmem_limit_bytes=52 * 2**20),
        cost_estimate=pl.CostEstimate(
            flops=10 * per * rows * rows * blocks * hd,
            bytes_accessed=4 * 2**20,
            transcendentals=per * rows * rows * blocks,
        ),
        name="attention_backward",
    )(info, starts, q, do, *kv)
    return outs[0], outs[1:]


def split_kernel(info, *refs):
    half = len(refs) // 2
    for src, dst in zip(refs[:half], refs[half:]):
        dst[...] = src[...].T


def split_features(x, my_x, z_hi, nx):
    rows, dim = x.shape
    wide = dim // (z_hi * nx)

    def source(s):
        return pl.BlockSpec((rows, wide), lambda g, info: (0, g * nx + (info[0] + s) % nx))

    return pl.pallas_call(
        split_kernel,
        grid_spec=pltpu.PrefetchScalarGridSpec(
            num_scalar_prefetch=1,
            grid=(z_hi,),
            in_specs=[source(s) for s in range(nx)],
            out_specs=[pl.BlockSpec((wide, rows), lambda g, info: (g, 0))] * nx,
        ),
        out_shape=[jax.ShapeDtypeStruct((z_hi * wide, rows), x.dtype)] * nx,
        compiler_params=pltpu.CompilerParams(vmem_limit_bytes=16 * 2**20),
        name="split_features",
    )(my_x[None], *([x] * nx))


def weight_kernel(nx, z_hi, ny, info, *refs):
    f_refs, g_refs, (out_ref, ft_s, total_s) = refs[:nx], refs[nx:-3], refs[-3:]
    own_ref, left_ref, far_refs, right_ref = g_refs[0], g_refs[1], g_refs[2:4], g_refs[4]
    rows = f_refs[0].shape[1]
    wide = f_refs[0].shape[0] // (z_hi * 2)
    which, my_y = info[0], info[1]
    step = pl.program_id(0)
    half = pl.num_programs(0) // 2

    @pl.when(step == 0)
    def _():
        for s in range(nx):
            for z in range(z_hi):
                at = pl.multiple_of((z * 2 + which) * wide, wide)
                ft_s[z * wide : (z + 1) * wide, s * rows : (s + 1) * rows] = f_refs[s][pl.ds(at, wide)]

    def product(s, ref):
        return dot(ft_s[:, s * rows : (s + 1) * rows], ref[...])

    for i in range(2):

        @pl.when(step // half == i)
        def _():
            total = product(0, own_ref) + product(1, left_ref)
            total = total + product(2, far_refs[i]) + product(3, right_ref)
            total_s[...] = total.astype(BF)

    part = wide // ny
    for z in range(z_hi):
        for r in range(ny):
            at = pl.multiple_of(z * wide + (my_y + r) % ny * part, part)
            out_ref[r, z] = total_s[pl.ds(at, part)]


def weight_part(features, grads, which, my_y, z_hi, ny):
    own, left, far, right = grads
    nx = len(features)
    rows, n = own.shape
    wide = features[0].shape[0] // (z_hi * 2)
    cols = min(n // 2, 256)
    half = n // 2 // cols
    skip = half if far[1].shape[1] < n else 0
    block = pl.BlockSpec((rows, cols), lambda g: (0, g))
    halves = [
        pl.BlockSpec((rows, cols), lambda g: (0, jnp.minimum(g, half - 1))),
        pl.BlockSpec((rows, cols), lambda g: (0, jnp.maximum(g - skip, 0))),
    ]
    return pl.pallas_call(
        functools.partial(weight_kernel, nx, z_hi, ny),
        grid=(2 * half,),
        in_specs=[pl.BlockSpec(memory_space=pltpu.SMEM)]
        + [whole(features[0].shape)] * nx
        + [block, block, *halves, block],
        out_specs=pl.BlockSpec((ny, z_hi, wide // ny, cols), lambda g: (0, 0, 0, g)),
        out_shape=jax.ShapeDtypeStruct((ny, z_hi, wide // ny, n), BF),
        scratch_shapes=[
            pltpu.VMEM((z_hi * wide, nx * rows), BF),
            pltpu.VMEM((z_hi * wide, cols), BF),
        ],
        compiler_params=pltpu.CompilerParams(vmem_limit_bytes=24 * 2**20),
        cost_estimate=pl.CostEstimate(
            flops=2 * z_hi * wide * nx * rows * n,
            bytes_accessed=6 * 2**20,
            transcendentals=0,
        ),
        name="weight_part",
    )(jnp.stack([which, my_y]), *features, own, left, *far, right)


def local(layer_input, queries, key_head, value_head, grad_output, doc_ids):
    x, q, k, v, do, docs = (
        a[0] for a in (layer_input, queries, key_head, value_head, grad_output, doc_ids)
    )
    rows, hd = k.shape
    ctx = lax.axis_size(CTX)
    nx, nc, z_hi = lax.axis_size("x"), lax.axis_size("core"), lax.axis_size("zh")
    ny, zl = lax.axis_size("y"), lax.axis_size("zl")
    place = lax.axis_index(CTX)
    my_x, my_core, my_y = lax.axis_index("x"), lax.axis_index("core"), lax.axis_index("y")

    kv = jnp.concatenate([k, v], axis=1)
    pair = jnp.stack([kv, shifted(kv, "zl", zl, 1)])
    before, after = shifted(pair, "y", ny, 1), shifted(pair, "y", ny, -1)
    parts = split_features(x, my_x, z_hi, nx)
    before, after, parts = lax.optimization_barrier((before, after, parts))
    far = jnp.stack([shifted(before[0], "y", ny, 1), shifted(after[1], "y", ny, -1)])
    kv_pairs = [pair, before, far, after]
    features = [shifted(part, "x", nx, s) if s else part for s, part in enumerate(parts)]

    my_docs = lax.dynamic_slice_in_dim(docs, place * rows, rows)
    starts = jnp.sum((docs[:, None] < my_docs[None, :]).astype(jnp.int32), axis=0)
    info = jnp.stack([place - starts[0] // rows + 1, place, starts[rows - 1]])
    starts = starts[None, :]

    def term(grads):
        theirs = weight_part(features, grads, 1 - my_core, my_y, z_hi, ny)
        theirs = shifted(theirs, "core", nc, 1)
        mine = weight_part(features, grads, my_core, my_y, z_hi, ny)
        return [(mine[r].astype(F32) + theirs[r].astype(F32)).astype(BF) for r in range(ny)]

    def far_y(pieces):
        half = pieces[2].shape[0] // 2
        ahead = shifted(pieces[2][:half], "y", ny, 1)
        behind = shifted(pieces[2][half:], "y", ny, -1)
        ahead = jnp.concatenate([plus(pieces[1][:half], ahead), pieces[1][half:]])
        behind = jnp.concatenate([pieces[3][:half], plus(pieces[3][half:], behind)])
        return pieces[0], ahead, behind

    def near_y(pieces):
        own, ahead, behind = pieces
        total = own.astype(F32) + shifted(ahead, "y", ny, 1).astype(F32)
        return total + shifted(behind, "y", ny, -1).astype(F32)

    dq, dkv = attention(q, do, kv_pairs, info, starts)
    dq, dkv, features = lax.optimization_barrier((dq, dkv, features))
    left, right = shifted(dq, "x", nx, 1), shifted(dq, "x", nx, -1)
    total = near_y(far_y([dkv[0], dkv[3], dkv[2], dkv[1]]))
    left, right, total = lax.optimization_barrier((left, right, total))
    half = dq.shape[1] // 2
    far = shifted(left[:, :half], "x", nx, 1), shifted(right[:, half:], "x", nx, -1)
    other = shifted(total[1].astype(BF), "zl", zl, 1)
    dkv_own = (total[0] + other.astype(F32)).astype(BF)

    pieces = far_y(term((dq, left, far, right)))
    along = [shifted(dkv_own, "x", nx, s) for s in range(1, nx)]
    pieces, along = lax.optimization_barrier((pieces, along))
    part = near_y(pieces).astype(BF)
    narrow = near_y(far_y(term((dkv_own, along[0], (along[1], along[1]), along[2])))).astype(BF)
    part = jnp.concatenate([part, narrow], axis=-1)
    n = part.shape[-1]
    part = part.reshape(z_hi, zl, -1, n)
    my_zl, my_zh = lax.axis_index("zl"), lax.axis_index("zh")
    kept = lax.dynamic_index_in_dim(part, my_zl, 1, keepdims=False)
    given = shifted(lax.dynamic_index_in_dim(part, 1 - my_zl, 1, keepdims=False), "zl", zl, 1)
    part = (kept.astype(F32) + given.astype(F32)).astype(BF)
    weight = 0.0
    for s in range(z_hi):
        piece = lax.dynamic_index_in_dim(part, (my_zh + s) % z_hi, 0, keepdims=False)
        weight = weight + (shifted(piece, "zh", z_hi, s) if s else piece).astype(F32)
    tokens = rows * ctx * nx * nc * z_hi
    weight = weight * (1.0 / math.sqrt(tokens))
    width = q.shape[1]
    return (
        dq[None],
        dkv_own[None, :, :hd],
        dkv_own[None, :, hd:],
        weight[:, :width],
        weight[:, width : width + hd],
        weight[:, width + hd :],
    )


def solution(mesh):
    fine = Mesh(mesh.devices.reshape(SIZES), AXES)
    dp = ("zh", "x", "core")
    tok = P(dp, CTX, None)
    row = P(dp + CTX, None)
    return jax.shard_map(
        local,
        mesh=fine,
        in_specs=(tok, tok, tok, tok, tok, P(dp, None)),
        out_specs=(tok, tok, tok, row, row, row),
        check_vma=False,
    )
```

```python
import functools
import math

import jax
import jax.numpy as jnp
from jax import lax
from jax.experimental import pallas as pl
from jax.experimental.pallas import tpu as pltpu
from jax.sharding import Mesh, PartitionSpec as P

NEG = -1e30
AXES = ("zh", "x", "core", "y", "zl")
SIZES = (4, 4, 2, 4, 2)
CTX = ("y", "zl")
BF = jnp.bfloat16
F32 = jnp.float32
NN = (((1,), (0,)), ((), ()))


def dot(a, b):
    return lax.dot_general(a, b, NN, preferred_element_type=F32)


def shifted(value, axis, count, step, wrap=True):
    pairs = []
    for src in range(count):
        dst = src + step
        if wrap:
            pairs.append((src, dst % count))
        elif 0 <= dst < count:
            pairs.append((src, dst))
    return lax.ppermute(value, axis, pairs)


def plus(a, b):
    return (a.astype(F32) + b.astype(F32)).astype(BF)


def whole(shape):
    return pl.BlockSpec(shape, lambda *g: (0,) * len(shape))


def attention_kernel(ny, per, scale, info, starts_ref, q_ref, do_ref, *refs):
    kv_refs, refs = refs[:ny], refs[ny:]
    dq_ref, refs = refs[0], refs[1:]
    out_ref, refs = refs[0], refs[1:]
    kv_s, kt_s, acc_s, e_s, dp_s, md_s, stat_s, dqt_s, qt_s, dot_s, p_s, ds_s, qk_s, dk_s, sem = refs
    rows = q_ref.shape[0]
    hd = kt_s.shape[1]
    used, place, limit = info[0], info[1], info[2]
    power = scale * math.log2(math.e)
    farthest = place // 2 - (place - used + 1) // 2

    for s in range(ny):

        @pl.when(s <= farthest)
        def _():
            pltpu.make_async_copy(kv_refs[s], kv_s.at[pl.ds(2 * s, 2)], sem.at[s]).start()

    acc_s[...] = jnp.zeros_like(acc_s)
    for h in range(per):
        cols = slice(h * hd, (h + 1) * hd)
        span = slice(h * rows, (h + 1) * rows)
        qk_s[span] = q_ref[:, cols]
        dk_s[span] = do_ref[:, cols]
        qt_s[h] = q_ref[:, cols].T
        dot_s[h] = do_ref[:, cols].T
        stat_s[0, h] = jnp.full((1, rows), NEG, F32)
        stat_s[1, h] = jnp.zeros((1, rows), F32)
        stat_s[2, h] = jnp.zeros((1, rows), F32)
    dqt_s[...] = jnp.zeros_like(dqt_s)

    for s in range(ny):

        @pl.when(s <= farthest)
        def _():
            pltpu.make_async_copy(kv_refs[s], kv_s.at[pl.ds(2 * s, 2)], sem.at[s]).wait()
            for k in range(2):
                kt_s[2 * s + k] = kv_s[2 * s + k, :, :hd].T

    def slot(d):
        block = place - d
        return 2 * (place // 2 - block // 2) + (d % 2)

    def forward(d, masked):
        at = slot(d)
        kd = kv_s[at, :, :hd]
        vd = kv_s[at, :, hd:]
        if masked:
            kp = lax.broadcasted_iota(jnp.int32, (rows, rows), 0) + (place - d) * rows
            qp = lax.broadcasted_iota(jnp.int32, (rows, rows), 1) + place * rows
            ok = (kp >= starts_ref[...]) & (kp <= qp)
        for h in range(per):
            s = dot(kd, qt_s[h])
            if masked:
                s = jnp.where(ok, s, NEG)
            old = stat_s[0, h]
            top = jnp.maximum(old, jnp.max(s, axis=0, keepdims=True))
            e = jnp.exp2(s * power - top * power)
            alpha = jnp.exp2((old - top) * power)
            dp = dot(vd, dot_s[h])
            stat_s[0, h] = top
            stat_s[1, h] = stat_s[1, h] * alpha + jnp.sum(e, axis=0, keepdims=True)
            stat_s[2, h] = stat_s[2, h] * alpha + jnp.sum(e * dp, axis=0, keepdims=True)
            e_s[d, h] = e
            dp_s[d, h] = dp
            md_s[d, h] = top

    def first(d, carry):
        masked = (d == 0) | ((place - d) * rows < limit)
        pl.when(masked)(lambda: forward(d, True))
        pl.when(jnp.logical_not(masked))(lambda: forward(d, False))
        return carry

    lax.fori_loop(0, used, first, 0)

    tops = [stat_s[0, h] for h in range(per)]
    inverse = [1.0 / stat_s[1, h] for h in range(per)]
    delta = [stat_s[2, h] * inverse[h] for h in range(per)]

    def second(d, carry):
        at = place - d
        for h in range(per):
            p = e_s[d, h] * (jnp.exp2((md_s[d, h] - tops[h]) * power) * inverse[h])
            p_s[:, h * rows : (h + 1) * rows] = p.astype(BF)
            ds_s[:, h * rows : (h + 1) * rows] = (p * (dp_s[d, h] - delta[h])).astype(BF)
        acc_s[at, :, hd:] += dot(p_s[...], dk_s[...])
        acc_s[at, :, :hd] += dot(ds_s[...], qk_s[...])
        dqt_s[...] += dot(kt_s[slot(d)], ds_s[...])
        return carry

    lax.fori_loop(0, used, second, 0)

    for h in range(per):
        dq_ref[:, h * hd : (h + 1) * hd] = (dqt_s[:, h * rows : (h + 1) * rows].T * scale).astype(BF)
    out_ref[:, :, :hd] = (acc_s[:, :, :hd] * scale).astype(BF)
    out_ref[:, :, hd:] = acc_s[:, :, hd:].astype(BF)


def attention(q, do, kv, info, starts):
    rows = q.shape[0]
    hd = kv[0].shape[2] // 2
    width = q.shape[1]
    per = width // hd
    ny = len(kv)
    blocks = 2 * ny
    slab = whole((rows, width))
    pair = kv[0].shape
    return pl.pallas_call(
        functools.partial(attention_kernel, ny, per, hd ** (-0.5)),
        grid=(1,),
        in_specs=[pl.BlockSpec(memory_space=pltpu.SMEM), whole((1, rows)), slab, slab]
        + [pl.BlockSpec(memory_space=pl.ANY)] * ny,
        out_specs=[whole((rows, width)), whole((blocks, *pair[1:]))],
        out_shape=[
            jax.ShapeDtypeStruct((rows, width), BF),
            jax.ShapeDtypeStruct((blocks, *pair[1:]), BF),
        ],
        scratch_shapes=[
            pltpu.VMEM((blocks, rows, 2 * hd), BF),
            pltpu.VMEM((blocks, hd, rows), BF),
            pltpu.VMEM((blocks, rows, 2 * hd), F32),
            pltpu.VMEM((blocks, per, rows, rows), F32),
            pltpu.VMEM((blocks, per, rows, rows), F32),
            pltpu.VMEM((blocks, per, 1, rows), F32),
            pltpu.VMEM((3, per, 1, rows), F32),
            pltpu.VMEM((hd, per * rows), F32),
            pltpu.VMEM((per, hd, rows), BF),
            pltpu.VMEM((per, hd, rows), BF),
            pltpu.VMEM((rows, per * rows), BF),
            pltpu.VMEM((rows, per * rows), BF),
            pltpu.VMEM((per * rows, hd), BF),
            pltpu.VMEM((per * rows, hd), BF),
            pltpu.SemaphoreType.DMA((ny,)),
        ],
        compiler_params=pltpu.CompilerParams(vmem_limit_bytes=52 * 2**20),
        cost_estimate=pl.CostEstimate(
            flops=10 * per * rows * rows * blocks * hd,
            bytes_accessed=4 * 2**20,
            transcendentals=per * rows * rows * blocks,
        ),
        name="attention_backward",
    )(info, starts, q, do, *kv)


def split_kernel(info, *refs):
    half = len(refs) // 2
    for src, dst in zip(refs[:half], refs[half:]):
        dst[...] = src[...].T


def split_features(x, my_x, z_hi, nx):
    rows, dim = x.shape
    wide = dim // (z_hi * nx)

    def source(s):
        return pl.BlockSpec((rows, wide), lambda g, info: (0, g * nx + (info[0] + s) % nx))

    return pl.pallas_call(
        split_kernel,
        grid_spec=pltpu.PrefetchScalarGridSpec(
            num_scalar_prefetch=1,
            grid=(z_hi,),
            in_specs=[source(s) for s in range(nx)],
            out_specs=[pl.BlockSpec((wide, rows), lambda g, info: (g, 0))] * nx,
        ),
        out_shape=[jax.ShapeDtypeStruct((z_hi * wide, rows), x.dtype)] * nx,
        compiler_params=pltpu.CompilerParams(vmem_limit_bytes=16 * 2**20),
        name="split_features",
    )(my_x[None], *([x] * nx))


def weight_kernel(nx, z_hi, narrow, info, *refs):
    f_refs, wide_refs, narrow_refs = refs[:nx], refs[nx : 2 * nx], refs[2 * nx : 3 * nx]
    out_ref, ft_s, sem = refs[3 * nx :]
    rows = f_refs[0].shape[1]
    each = f_refs[0].shape[0] // (z_hi * 2)
    step = pl.program_id(0)

    def fetch(s, z):
        at = pl.multiple_of((z * 2 + info[0]) * each, each)
        into = ft_s.at[s, pl.ds(z * each, each)]
        return pltpu.make_async_copy(f_refs[s].at[pl.ds(at, each)], into, sem.at[s, z])

    @pl.when(step == 0)
    def _():
        for s in range(nx):
            for z in range(z_hi):
                fetch(s, z).start()
        for s in range(nx):
            for z in range(z_hi):
                fetch(s, z).wait()

    def store(g_refs):
        total = dot(ft_s[0], g_refs[0][...])
        for s in range(1, nx):
            total += dot(ft_s[s], g_refs[s][...])
        total = total.astype(BF)
        part = out_ref.shape[2]
        for z in range(z_hi):
            for p in range(out_ref.shape[0]):
                at = z * each + p * part
                out_ref[p, z] = total[at : at + part]

    first_narrow = pl.num_programs(0) - narrow
    pl.when(step < first_narrow)(lambda: store(wide_refs))
    pl.when(step >= first_narrow)(lambda: store(narrow_refs))


def weight_part(features, wide, narrow, which, z_hi, pieces):
    nx = len(features)
    rows = wide[0].shape[0]
    each = features[0].shape[0] // (z_hi * 2)
    cols = 256
    n_wide, n_narrow = wide[0].shape[1] // cols, narrow[0].shape[1] // cols
    n = (n_wide + n_narrow) * cols
    return pl.pallas_call(
        functools.partial(weight_kernel, nx, z_hi, n_narrow),
        grid=(n_wide + n_narrow,),
        in_specs=[pl.BlockSpec(memory_space=pltpu.SMEM)]
        + [pl.BlockSpec(memory_space=pl.ANY)] * nx
        + [pl.BlockSpec((rows, cols), lambda g: (0, jnp.minimum(g, n_wide - 1)))] * nx
        + [pl.BlockSpec((rows, cols), lambda g: (0, jnp.maximum(g - n_wide, 0)))] * nx,
        out_specs=pl.BlockSpec((pieces, z_hi, each // pieces, cols), lambda g: (0, 0, 0, g)),
        out_shape=jax.ShapeDtypeStruct((pieces, z_hi, each // pieces, n), BF),
        scratch_shapes=[
            pltpu.VMEM((nx, z_hi * each, rows), BF),
            pltpu.SemaphoreType.DMA((nx, z_hi)),
        ],
        compiler_params=pltpu.CompilerParams(vmem_limit_bytes=24 * 2**20),
        cost_estimate=pl.CostEstimate(
            flops=2 * z_hi * each * nx * rows * n,
            bytes_accessed=6 * 2**20,
            transcendentals=0,
        ),
        name="weight_part",
    )(which[None], *features, *wide, *narrow)


def local(layer_input, queries, key_head, value_head, grad_output, doc_ids):
    x, q, k, v, do, docs = (
        a[0] for a in (layer_input, queries, key_head, value_head, grad_output, doc_ids)
    )
    rows, hd = k.shape
    ctx = lax.axis_size(CTX)
    nx, nc, z_hi = lax.axis_size("x"), lax.axis_size("core"), lax.axis_size("zh")
    ny, zl = lax.axis_size("y"), lax.axis_size("zl")
    place = lax.axis_index(CTX)
    my_x, my_core = lax.axis_index("x"), lax.axis_index("core")

    kv = jnp.concatenate([k, v], axis=1)
    pair = jnp.stack([kv, shifted(kv, "zl", zl, 1)])
    before, after = shifted(pair, "y", ny, 1), shifted(pair, "y", ny, -1)
    parts = split_features(x, my_x, z_hi, nx)
    far = jnp.stack([shifted(before[0], "y", ny, 1), shifted(after[1], "y", ny, -1)])
    kv_pairs = [pair, before, far, after]
    features = [shifted(part, "x", nx, s) if s else part for s, part in enumerate(parts)]

    my_docs = lax.dynamic_slice_in_dim(docs, place * rows, rows)
    starts = jnp.sum((docs[:, None] < my_docs[None, :]).astype(jnp.int32), axis=0)
    info = jnp.stack([place - starts[0] // rows + 1, place, starts[rows - 1]])
    starts = starts[None, :]

    def along_x(grads):
        return [grads] + [shifted(grads, "x", nx, s) for s in range(1, nx)]

    dq, dkv = attention(q, do, kv_pairs, info, starts)
    dq, dkv, features = lax.optimization_barrier((dq, dkv, features))
    wide = along_x(dq)
    dkv = lax.all_to_all(dkv, CTX, 0, 0, tiled=True)
    dkv_own = jnp.sum(dkv.astype(F32), axis=0).astype(BF)
    narrow = along_x(dkv_own)

    theirs = weight_part(features, wide, narrow, 1 - my_core, z_hi, ctx)
    theirs = shifted(theirs, "core", nc, 1)
    mine = weight_part(features, wide, narrow, my_core, z_hi, ctx)
    n = mine.shape[-1]
    part = plus(mine, theirs).reshape(ctx, -1, n)
    part = lax.all_to_all(part, CTX, 0, 0, tiled=True)
    part = jnp.sum(part.astype(F32), axis=0).astype(BF).reshape(z_hi, -1, n)
    part = lax.all_to_all(part, "zh", 0, 0, tiled=True)
    tokens = rows * ctx * nx * nc * z_hi
    weight = jnp.sum(part.astype(F32), axis=0) * (1.0 / math.sqrt(tokens))
    width = q.shape[1]
    return (
        dq[None],
        dkv_own[None, :, :hd],
        dkv_own[None, :, hd:],
        weight[:, :width],
        weight[:, width : width + hd],
        weight[:, width + hd :],
    )


def solution(mesh):
    fine = Mesh(mesh.devices.reshape(SIZES), AXES)
    dp = ("zh", "x", "core")
    tok = P(dp, CTX, None)
    row = P(dp + CTX, None)
    return jax.shard_map(
        local,
        mesh=fine,
        in_specs=(tok, tok, tok, tok, tok, P(dp, None)),
        out_specs=(tok, tok, tok, row, row, row),
        check_vma=False,
    )
```

```python
import functools
import math

import jax
import jax.numpy as jnp
from jax import lax
from jax.experimental import pallas as pl
from jax.experimental.pallas import tpu as pltpu
from jax.sharding import Mesh, PartitionSpec as P

NEG = -1e30
DOCS = 4
AXES = ("zh", "x", "core", "y", "zl")
SIZES = (4, 4, 2, 4, 2)
CTX = ("y", "zl")
BF = jnp.bfloat16
F32 = jnp.float32
NN = (((1,), (0,)), ((), ()))


def dot(a, b):
    return lax.dot_general(a, b, NN, preferred_element_type=F32)


def shifted(value, axis, count, step, wrap=True):
    pairs = []
    for src in range(count):
        dst = src + step
        if wrap:
            pairs.append((src, dst % count))
        elif 0 <= dst < count:
            pairs.append((src, dst))
    return lax.ppermute(value, axis, pairs)


def plus(a, b):
    return (a.astype(F32) + b.astype(F32)).astype(BF)


def whole(shape):
    return pl.BlockSpec(shape, lambda *g: (0,) * len(shape))


def attention_kernel(ny, per, docs, scale, info, docs_ref, q_ref, do_ref, *refs):
    (pair_ref, before_ref, far_refs, after_ref), refs = (refs[0], refs[1], refs[2:4], refs[4]), refs[5:]
    dq_ref, refs = refs[0], refs[1:]
    out_ref, refs = refs[0], refs[1:]
    kv_s, kt_s, acc_s, e_s, dp_s, md_s, stat_s, dqt_s, qt_s, dot_s, p_s, ds_s, qk_s, dk_s, starts_ref, sem = refs
    rows = q_ref.shape[0]
    hd = kt_s.shape[1]
    place = info[0]
    documents = docs_ref[...]
    mine = docs_ref[:, pl.ds(pl.multiple_of(place * rows, rows), rows)]
    starts = jnp.zeros((1, rows), jnp.int32)
    for t in range(docs - 1):
        length = jnp.sum((documents == t).astype(jnp.int32))
        starts += jnp.where(mine > t, length, 0)
    starts_ref[...] = starts
    limit = jnp.max(starts)
    used = place - jnp.min(starts) // rows + 1
    power = scale * math.log2(math.e)
    farthest = place // 2 - (place - used + 1) // 2

    copies = [
        (0, pltpu.make_async_copy(pair_ref, kv_s.at[pl.ds(0, 2)], sem.at[0])),
        (1, pltpu.make_async_copy(before_ref, kv_s.at[pl.ds(2, 2)], sem.at[1])),
        (2, pltpu.make_async_copy(far_refs[0], kv_s.at[4], sem.at[2])),
        (2, pltpu.make_async_copy(far_refs[1], kv_s.at[5], sem.at[3])),
        (3, pltpu.make_async_copy(after_ref, kv_s.at[pl.ds(6, 2)], sem.at[4])),
    ]
    for s, copy in copies:
        pl.when(s <= farthest)(copy.start)

    acc_s[...] = jnp.zeros_like(acc_s)
    for h in range(per):
        cols = slice(h * hd, (h + 1) * hd)
        span = slice(h * rows, (h + 1) * rows)
        qk_s[span] = q_ref[:, cols]
        dk_s[span] = do_ref[:, cols]
        qt_s[h] = q_ref[:, cols].T
        dot_s[h] = do_ref[:, cols].T
        stat_s[0, h] = jnp.full((1, rows), NEG, F32)
        stat_s[1, h] = jnp.zeros((1, rows), F32)
        stat_s[2, h] = jnp.zeros((1, rows), F32)
    dqt_s[...] = jnp.zeros_like(dqt_s)

    for s, copy in copies:
        pl.when(s <= farthest)(copy.wait)
    for s in range(ny):

        @pl.when(s <= farthest)
        def _():
            for k in range(2):
                kt_s[2 * s + k] = kv_s[2 * s + k, :, :hd].T

    def slot(d):
        block = place - d
        return 2 * (place // 2 - block // 2) + (d % 2)

    def forward(d, masked):
        at = slot(d)
        kd = kv_s[at, :, :hd]
        vd = kv_s[at, :, hd:]
        if masked:
            kp = lax.broadcasted_iota(jnp.int32, (rows, rows), 0) + (place - d) * rows
            qp = lax.broadcasted_iota(jnp.int32, (rows, rows), 1) + place * rows
            ok = (kp >= starts_ref[...]) & (kp <= qp)
        for h in range(per):
            s = dot(kd, qt_s[h])
            if masked:
                s = jnp.where(ok, s, NEG)
            old = stat_s[0, h]
            top = jnp.maximum(old, jnp.max(s, axis=0, keepdims=True))
            e = jnp.exp2(s * power - top * power)
            alpha = jnp.exp2((old - top) * power)
            dp = dot(vd, dot_s[h])
            stat_s[0, h] = top
            stat_s[1, h] = stat_s[1, h] * alpha + jnp.sum(e, axis=0, keepdims=True)
            stat_s[2, h] = stat_s[2, h] * alpha + jnp.sum(e * dp, axis=0, keepdims=True)
            e_s[d, h] = e
            dp_s[d, h] = dp
            md_s[d, h] = top

    def first(d, carry):
        masked = (d == 0) | ((place - d) * rows < limit)
        pl.when(masked)(lambda: forward(d, True))
        pl.when(jnp.logical_not(masked))(lambda: forward(d, False))
        return carry

    lax.fori_loop(0, used, first, 0)

    tops = [stat_s[0, h] for h in range(per)]
    inverse = [1.0 / stat_s[1, h] for h in range(per)]
    delta = [stat_s[2, h] * inverse[h] for h in range(per)]

    def second(d, carry):
        at = place - d
        for h in range(per):
            p = e_s[d, h] * (jnp.exp2((md_s[d, h] - tops[h]) * power) * inverse[h])
            p_s[:, h * rows : (h + 1) * rows] = p.astype(BF)
            ds_s[:, h * rows : (h + 1) * rows] = (p * (dp_s[d, h] - delta[h])).astype(BF)
        acc_s[at, :, hd:] += dot(p_s[...], dk_s[...])
        acc_s[at, :, :hd] += dot(ds_s[...], qk_s[...])
        dqt_s[...] += dot(kt_s[slot(d)], ds_s[...])
        return carry

    lax.fori_loop(0, used, second, 0)

    for h in range(per):
        dq_ref[:, h * hd : (h + 1) * hd] = (dqt_s[:, h * rows : (h + 1) * rows].T * scale).astype(BF)
    out_ref[:, :, :hd] = (acc_s[:, :, :hd] * scale).astype(BF)
    out_ref[:, :, hd:] = acc_s[:, :, hd:].astype(BF)


def attention(q, do, kv, docs, place, ny):
    rows = q.shape[0]
    hd = kv[0].shape[2] // 2
    width = q.shape[1]
    per = width // hd
    blocks = 2 * ny
    slab = whole((rows, width))
    pair = kv[0].shape
    return pl.pallas_call(
        functools.partial(attention_kernel, ny, per, DOCS, hd ** (-0.5)),
        grid=(1,),
        in_specs=[pl.BlockSpec(memory_space=pltpu.SMEM), whole(docs.shape), slab, slab]
        + [pl.BlockSpec(memory_space=pl.ANY)] * len(kv),
        out_specs=[whole((rows, width)), whole((blocks, *pair[1:]))],
        out_shape=[
            jax.ShapeDtypeStruct((rows, width), BF),
            jax.ShapeDtypeStruct((blocks, *pair[1:]), BF),
        ],
        scratch_shapes=[
            pltpu.VMEM((blocks, rows, 2 * hd), BF),
            pltpu.VMEM((blocks, hd, rows), BF),
            pltpu.VMEM((blocks, rows, 2 * hd), F32),
            pltpu.VMEM((blocks, per, rows, rows), F32),
            pltpu.VMEM((blocks, per, rows, rows), F32),
            pltpu.VMEM((blocks, per, 1, rows), F32),
            pltpu.VMEM((3, per, 1, rows), F32),
            pltpu.VMEM((hd, per * rows), F32),
            pltpu.VMEM((per, hd, rows), BF),
            pltpu.VMEM((per, hd, rows), BF),
            pltpu.VMEM((rows, per * rows), BF),
            pltpu.VMEM((rows, per * rows), BF),
            pltpu.VMEM((per * rows, hd), BF),
            pltpu.VMEM((per * rows, hd), BF),
            pltpu.VMEM((1, rows), jnp.int32),
            pltpu.SemaphoreType.DMA((len(kv),)),
        ],
        compiler_params=pltpu.CompilerParams(vmem_limit_bytes=52 * 2**20),
        cost_estimate=pl.CostEstimate(
            flops=10 * per * rows * rows * blocks * hd,
            bytes_accessed=4 * 2**20,
            transcendentals=per * rows * rows * blocks,
        ),
        name="attention_backward",
    )(place[None], docs, q, do, *kv)


def split_kernel(info, *refs):
    half = len(refs) // 2
    for src, dst in zip(refs[:half], refs[half:]):
        dst[...] = src[...].T


def split_features(x, my_x, z_hi, nx):
    rows, dim = x.shape
    wide = dim // (z_hi * nx)

    def source(s):
        return pl.BlockSpec((rows, wide), lambda g, info: (0, g * nx + (info[0] + s) % nx))

    return pl.pallas_call(
        split_kernel,
        grid_spec=pltpu.PrefetchScalarGridSpec(
            num_scalar_prefetch=1,
            grid=(z_hi,),
            in_specs=[source(s) for s in range(nx)],
            out_specs=[pl.BlockSpec((wide, rows), lambda g, info: (g, 0))] * nx,
        ),
        out_shape=[jax.ShapeDtypeStruct((z_hi * wide, rows), x.dtype)] * nx,
        compiler_params=pltpu.CompilerParams(vmem_limit_bytes=16 * 2**20),
        name="split_features",
    )(my_x[None], *([x] * nx))


def weight_kernel(nx, z_hi, n_wide, info, *refs):
    f_refs, wide_refs, narrow_refs = refs[:nx], refs[nx : 2 * nx], refs[2 * nx : 3 * nx]
    out_ref, ft_s = refs[3 * nx :]
    rows = wide_refs[0].shape[0]
    each = f_refs[0].shape[0] // (z_hi * 2)
    cols = 256
    part = out_ref.shape[2]
    for s in range(nx):
        for z in range(z_hi):
            at = pl.multiple_of((z * 2 + info[0]) * each, each)
            ft_s[z * each : (z + 1) * each, s * rows : (s + 1) * rows] = f_refs[s][pl.ds(at, each)]

    def columns(g_refs, at, to):
        total = dot(ft_s[:, :rows], g_refs[0][:, at : at + cols])
        for s in range(1, nx):
            total += dot(ft_s[:, s * rows : (s + 1) * rows], g_refs[s][:, at : at + cols])
        total = total.astype(BF)
        for z in range(z_hi):
            for p in range(out_ref.shape[0]):
                row = z * each + p * part
                out_ref[p, z, :, to : to + cols] = total[row : row + part]

    for j in range(out_ref.shape[3] // cols):
        if j < n_wide:
            columns(wide_refs, j * cols, j * cols)
        else:
            columns(narrow_refs, (j - n_wide) * cols, j * cols)


def weight_part(features, wide, narrow, which, z_hi, pieces):
    nx = len(features)
    rows = wide[0].shape[0]
    each = features[0].shape[0] // (z_hi * 2)
    n = wide[0].shape[1] + narrow[0].shape[1]
    operands = [*features, *wide, *narrow]
    out_shape = (pieces, z_hi, each // pieces, n)
    return pl.pallas_call(
        functools.partial(weight_kernel, nx, z_hi, wide[0].shape[1] // 256),
        in_specs=[pl.BlockSpec(memory_space=pltpu.SMEM)]
        + [pl.BlockSpec(memory_space=pltpu.VMEM)] * len(operands),
        out_specs=pl.BlockSpec(memory_space=pltpu.VMEM),
        out_shape=jax.ShapeDtypeStruct(out_shape, BF),
        scratch_shapes=[pltpu.VMEM((z_hi * each, nx * rows), BF)],
        compiler_params=pltpu.CompilerParams(vmem_limit_bytes=20 * 2**20),
        cost_estimate=pl.CostEstimate(
            flops=2 * z_hi * each * nx * rows * n,
            bytes_accessed=6 * 2**20,
            transcendentals=0,
        ),
        name="weight_part",
    )(which[None], *operands)


def local(layer_input, queries, key_head, value_head, grad_output, doc_ids):
    x, q, k, v, do = (a[0] for a in (layer_input, queries, key_head, value_head, grad_output))
    rows, hd = k.shape
    ctx = lax.axis_size(CTX)
    nx, nc, z_hi = lax.axis_size("x"), lax.axis_size("core"), lax.axis_size("zh")
    ny, zl = lax.axis_size("y"), lax.axis_size("zl")
    place = lax.axis_index(CTX)
    my_x, my_core = lax.axis_index("x"), lax.axis_index("core")

    kv = jnp.concatenate([k, v], axis=1)
    other = shifted(kv, "zl", zl, 1)
    parts = split_features(x, my_x, z_hi, nx)
    other, parts = lax.optimization_barrier((other, parts))
    pair = jnp.stack([kv, other])
    before, after = shifted(pair, "y", ny, 1), shifted(pair, "y", ny, -1)
    far = shifted(before[0], "y", ny, 1), shifted(after[1], "y", ny, -1)
    features = [shifted(part, "x", nx, s) if s else part for s, part in enumerate(parts)]

    def along_x(grads):
        return [grads] + [shifted(grads, "x", nx, s) for s in range(1, nx)]

    dq, dkv = attention(q, do, [pair, before, *far, after], doc_ids, place, ny)
    dq, dkv, features = lax.optimization_barrier((dq, dkv, features))
    wide = along_x(dq)
    dkv = lax.all_to_all(dkv, CTX, 0, 0, tiled=True)
    dkv_own = jnp.sum(dkv.astype(F32), axis=0).astype(BF)
    narrow = along_x(dkv_own)

    theirs = weight_part(features, wide, narrow, 1 - my_core, z_hi, ctx)
    theirs = shifted(theirs, "core", nc, 1)
    mine = weight_part(features, wide, narrow, my_core, z_hi, ctx)
    n = mine.shape[-1]
    part = plus(mine, theirs).reshape(ctx, -1, n)
    part = lax.all_to_all(part, CTX, 0, 0, tiled=True)
    part = jnp.sum(part.astype(F32), axis=0).astype(BF).reshape(z_hi, -1, n)
    part = lax.all_to_all(part, "zh", 0, 0, tiled=True)
    tokens = rows * ctx * nx * nc * z_hi
    weight = jnp.sum(part.astype(F32), axis=0) * (1.0 / math.sqrt(tokens))
    width = q.shape[1]
    return (
        dq[None],
        dkv_own[None, :, :hd],
        dkv_own[None, :, hd:],
        weight[:, :width],
        weight[:, width : width + hd],
        weight[:, width + hd :],
    )


def solution(mesh):
    fine = Mesh(mesh.devices.reshape(SIZES), AXES)
    dp = ("zh", "x", "core")
    tok = P(dp, CTX, None)
    row = P(dp + CTX, None)
    return jax.shard_map(
        local,
        mesh=fine,
        in_specs=(tok, tok, tok, tok, tok, P(dp, None)),
        out_specs=(tok, tok, tok, row, row, row),
        check_vma=False,
    )
```

```python
import functools
import math

import jax
import jax.numpy as jnp
from jax import lax
from jax.experimental import pallas as pl
from jax.experimental.pallas import tpu as pltpu
from jax.sharding import Mesh, PartitionSpec as P

NEG = -1e30
DOCS = 4
AXES = ("zh", "x", "core", "y", "zl")
SIZES = (4, 4, 2, 4, 2)
CTX = ("y", "zl")
BF = jnp.bfloat16
F32 = jnp.float32
NN = (((1,), (0,)), ((), ()))


def dot(a, b):
    return lax.dot_general(a, b, NN, preferred_element_type=F32)


def shifted(value, axis, count, step, wrap=True):
    pairs = []
    for src in range(count):
        dst = src + step
        if wrap:
            pairs.append((src, dst % count))
        elif 0 <= dst < count:
            pairs.append((src, dst))
    return lax.ppermute(value, axis, pairs)


def plus(a, b):
    return (a.astype(F32) + b.astype(F32)).astype(BF)


def whole(shape):
    return pl.BlockSpec(shape, lambda *g: (0,) * len(shape))


def attention_kernel(ny, per, docs, scale, info, docs_ref, q_ref, do_ref, *refs):
    (pair_ref, before_ref, far_refs, after_ref), refs = (refs[0], refs[1], refs[2:4], refs[4]), refs[5:]
    dq_ref, refs = refs[0], refs[1:]
    out_ref, refs = refs[0], refs[1:]
    kv_s, kt_s, e_s, dp_s, md_s, stat_s, dqt_s, qt_s, dot_s, p_s, ds_s, qk_s, dk_s, starts_ref, sem = refs
    rows = q_ref.shape[0]
    hd = kt_s.shape[1]
    place = info[0]
    power = scale * math.log2(math.e)
    farthest = place // 2

    copies = [
        (0, pltpu.make_async_copy(pair_ref, kv_s.at[pl.ds(0, 2)], sem.at[0])),
        (1, pltpu.make_async_copy(before_ref, kv_s.at[pl.ds(2, 2)], sem.at[1])),
        (2, pltpu.make_async_copy(far_refs[0], kv_s.at[4], sem.at[2])),
        (2, pltpu.make_async_copy(far_refs[1], kv_s.at[5], sem.at[3])),
        (3, pltpu.make_async_copy(after_ref, kv_s.at[pl.ds(6, 2)], sem.at[4])),
    ]
    for s, copy in copies:
        pl.when(s <= farthest)(copy.start)

    for h in range(per):
        cols = slice(h * hd, (h + 1) * hd)
        span = slice(h * rows, (h + 1) * rows)
        qk_s[span] = q_ref[:, cols]
        dk_s[span] = do_ref[:, cols]
        qt_s[h] = q_ref[:, cols].T
        dot_s[h] = do_ref[:, cols].T
        stat_s[0, h] = jnp.full((1, rows), NEG, F32)
        stat_s[1, h] = jnp.zeros((1, rows), F32)
        stat_s[2, h] = jnp.zeros((1, rows), F32)
    dqt_s[...] = jnp.zeros_like(dqt_s)

    documents = docs_ref[...]
    mine = docs_ref[:, pl.ds(pl.multiple_of(place * rows, rows), rows)]
    starts = jnp.zeros((1, rows), jnp.int32)
    for t in range(docs - 1):
        length = jnp.sum((documents == t).astype(jnp.int32))
        starts += jnp.where(mine > t, length, 0)
    starts_ref[...] = starts
    limit = jnp.max(starts)
    used = place - jnp.min(starts) // rows + 1
    for s, copy in copies:
        pl.when(s <= farthest)(copy.wait)

    def clear(block, carry):
        out_ref[block] = jnp.zeros(out_ref.shape[1:], BF)
        return carry

    lax.fori_loop(0, place - used + 1, clear, 0)
    lax.fori_loop(place + 1, out_ref.shape[0], clear, 0)

    def slot(d):
        block = place - d
        return 2 * (place // 2 - block // 2) + (d % 2)

    def forward(d, masked):
        at = slot(d)
        kd = kv_s[at, :, :hd]
        vd = kv_s[at, :, hd:]
        kt_s[at] = kd.T
        if masked:
            kp = lax.broadcasted_iota(jnp.int32, (rows, rows), 0) + (place - d) * rows
            qp = lax.broadcasted_iota(jnp.int32, (rows, rows), 1) + place * rows
            ok = (kp >= starts_ref[...]) & (kp <= qp)
        for h in range(per):
            s = dot(kd, qt_s[h])
            if masked:
                s = jnp.where(ok, s, NEG)
            old = stat_s[0, h]
            top = jnp.maximum(old, jnp.max(s, axis=0, keepdims=True))
            e = jnp.exp2(s * power - top * power)
            alpha = jnp.exp2((old - top) * power)
            dp = dot(vd, dot_s[h])
            stat_s[0, h] = top
            stat_s[1, h] = stat_s[1, h] * alpha + jnp.sum(e, axis=0, keepdims=True)
            stat_s[2, h] = stat_s[2, h] * alpha + jnp.sum(e * dp, axis=0, keepdims=True)
            e_s[d, h] = e
            dp_s[d, h] = dp
            md_s[d, h] = top

    def first(d, carry):
        masked = (d == 0) | ((place - d) * rows < limit)
        pl.when(masked)(lambda: forward(d, True))
        pl.when(jnp.logical_not(masked))(lambda: forward(d, False))
        return carry

    lax.fori_loop(0, used, first, 0)

    tops = [stat_s[0, h] for h in range(per)]
    inverse = [1.0 / stat_s[1, h] for h in range(per)]
    delta = [stat_s[2, h] * inverse[h] for h in range(per)]

    def second(d, carry):
        for h in range(per):
            p = e_s[d, h] * (jnp.exp2((md_s[d, h] - tops[h]) * power) * inverse[h])
            p_s[:, h * rows : (h + 1) * rows] = p.astype(BF)
            ds_s[:, h * rows : (h + 1) * rows] = (p * (dp_s[d, h] - delta[h])).astype(BF)
        out_ref[place - d, :, hd:] = dot(p_s[...], dk_s[...]).astype(BF)
        out_ref[place - d, :, :hd] = (dot(ds_s[...], qk_s[...]) * scale).astype(BF)
        dqt_s[...] += dot(kt_s[slot(d)], ds_s[...])
        return carry

    lax.fori_loop(0, used, second, 0)

    for h in range(per):
        dq_ref[:, h * hd : (h + 1) * hd] = (dqt_s[:, h * rows : (h + 1) * rows].T * scale).astype(BF)


def attention(q, do, kv, docs, place, ny):
    rows = q.shape[0]
    hd = kv[0].shape[2] // 2
    width = q.shape[1]
    per = width // hd
    blocks = 2 * ny
    slab = whole((rows, width))
    pair = kv[0].shape
    return pl.pallas_call(
        functools.partial(attention_kernel, ny, per, DOCS, hd ** (-0.5)),
        grid=(1,),
        in_specs=[pl.BlockSpec(memory_space=pltpu.SMEM), whole(docs.shape), slab, slab]
        + [pl.BlockSpec(memory_space=pl.ANY)] * len(kv),
        out_specs=[whole((rows, width)), whole((blocks, *pair[1:]))],
        out_shape=[
            jax.ShapeDtypeStruct((rows, width), BF),
            jax.ShapeDtypeStruct((blocks, *pair[1:]), BF),
        ],
        scratch_shapes=[
            pltpu.VMEM((blocks, rows, 2 * hd), BF),
            pltpu.VMEM((blocks, hd, rows), BF),
            pltpu.VMEM((blocks, per, rows, rows), F32),
            pltpu.VMEM((blocks, per, rows, rows), F32),
            pltpu.VMEM((blocks, per, 1, rows), F32),
            pltpu.VMEM((3, per, 1, rows), F32),
            pltpu.VMEM((hd, per * rows), F32),
            pltpu.VMEM((per, hd, rows), BF),
            pltpu.VMEM((per, hd, rows), BF),
            pltpu.VMEM((rows, per * rows), BF),
            pltpu.VMEM((rows, per * rows), BF),
            pltpu.VMEM((per * rows, hd), BF),
            pltpu.VMEM((per * rows, hd), BF),
            pltpu.VMEM((1, rows), jnp.int32),
            pltpu.SemaphoreType.DMA((len(kv),)),
        ],
        compiler_params=pltpu.CompilerParams(vmem_limit_bytes=52 * 2**20),
        cost_estimate=pl.CostEstimate(
            flops=10 * per * rows * rows * blocks * hd,
            bytes_accessed=4 * 2**20,
            transcendentals=per * rows * rows * blocks,
        ),
        name="attention_backward",
    )(place[None], docs, q, do, *kv)


def split_kernel(info, *refs):
    half = len(refs) // 2
    for src, dst in zip(refs[:half], refs[half:]):
        dst[...] = src[...].T


def split_features(x, my_x, z_hi, nx):
    rows, dim = x.shape
    wide = dim // (z_hi * nx)

    def source(s):
        return pl.BlockSpec((rows, wide), lambda g, info: (0, g * nx + (info[0] + s) % nx))

    return pl.pallas_call(
        split_kernel,
        grid_spec=pltpu.PrefetchScalarGridSpec(
            num_scalar_prefetch=1,
            grid=(z_hi,),
            in_specs=[source(s) for s in range(nx)],
            out_specs=[pl.BlockSpec((wide, rows), lambda g, info: (g, 0))] * nx,
        ),
        out_shape=[jax.ShapeDtypeStruct((z_hi * wide, rows), x.dtype)] * nx,
        compiler_params=pltpu.CompilerParams(vmem_limit_bytes=16 * 2**20),
        name="split_features",
    )(my_x[None], *([x] * nx))


def weight_kernel(nx, z_hi, info, *refs):
    f_refs, wide_refs, narrow_refs = refs[:nx], refs[nx : 2 * nx + 1], refs[2 * nx + 1 : 3 * nx + 1]
    out_ref, ft_s = refs[3 * nx + 1 :]
    rows, width = wide_refs[0].shape
    each = f_refs[0].shape[0] // (z_hi * 2)
    cols = 256
    part = out_ref.shape[2]
    for s in range(nx):
        for z in range(z_hi):
            at = pl.multiple_of((z * 2 + info[0]) * each, each)
            ft_s[z * each : (z + 1) * each, s * rows : (s + 1) * rows] = f_refs[s][pl.ds(at, each)]

    def columns(blocks, to):
        total = dot(ft_s[:, :rows], blocks[0])
        for s in range(1, nx):
            total += dot(ft_s[:, s * rows : (s + 1) * rows], blocks[s])
        total = total.astype(BF)
        for z in range(z_hi):
            for p in range(out_ref.shape[0]):
                row = z * each + p * part
                out_ref[p, z, :, to : to + cols] = total[row : row + part]

    for at in range(0, width, cols):
        own, left, far_first, far_second, right = wide_refs
        split = far_first.shape[1]
        far = far_first[:, at : at + cols] if at < split else far_second[:, at - split : at - split + cols]
        columns([own[:, at : at + cols], left[:, at : at + cols], far, right[:, at : at + cols]], at)
    for at in range(0, narrow_refs[0].shape[1], cols):
        columns([ref[:, at : at + cols] for ref in narrow_refs], width + at)


def weight_part(features, wide, narrow, which, z_hi, pieces):
    nx = len(features)
    rows = wide[0].shape[0]
    each = features[0].shape[0] // (z_hi * 2)
    n = wide[0].shape[1] + narrow[0].shape[1]
    operands = [*features, *wide, *narrow]
    out_shape = (pieces, z_hi, each // pieces, n)
    return pl.pallas_call(
        functools.partial(weight_kernel, nx, z_hi),
        in_specs=[pl.BlockSpec(memory_space=pltpu.SMEM)]
        + [pl.BlockSpec(memory_space=pltpu.VMEM)] * len(operands),
        out_specs=pl.BlockSpec(memory_space=pltpu.VMEM),
        out_shape=jax.ShapeDtypeStruct(out_shape, BF),
        scratch_shapes=[pltpu.VMEM((z_hi * each, nx * rows), BF)],
        compiler_params=pltpu.CompilerParams(vmem_limit_bytes=20 * 2**20),
        cost_estimate=pl.CostEstimate(
            flops=2 * z_hi * each * nx * rows * n,
            bytes_accessed=6 * 2**20,
            transcendentals=0,
        ),
        name="weight_part",
    )(which[None], *operands)


def local(layer_input, queries, key_head, value_head, grad_output, doc_ids):
    x, q, k, v, do = (a[0] for a in (layer_input, queries, key_head, value_head, grad_output))
    rows, hd = k.shape
    ctx = lax.axis_size(CTX)
    nx, nc, z_hi = lax.axis_size("x"), lax.axis_size("core"), lax.axis_size("zh")
    ny, zl = lax.axis_size("y"), lax.axis_size("zl")
    place = lax.axis_index(CTX)
    my_x, my_core = lax.axis_index("x"), lax.axis_index("core")

    kv = jnp.concatenate([k, v], axis=1)
    other = shifted(kv, "zl", zl, 1)
    parts = split_features(x, my_x, z_hi, nx)
    other, parts = lax.optimization_barrier((other, parts))
    pair = jnp.stack([kv, other])
    before, after = shifted(pair, "y", ny, 1), shifted(pair, "y", ny, -1)
    far = shifted(before[0], "y", ny, 1), shifted(after[1], "y", ny, -1)
    features = [shifted(part, "x", nx, s) if s else part for s, part in enumerate(parts)]

    dq, dkv = attention(q, do, [pair, before, *far, after], doc_ids, place, ny)
    dq, dkv, features = lax.optimization_barrier((dq, dkv, features))
    left, right = shifted(dq, "x", nx, 1), shifted(dq, "x", nx, -1)
    half = dq.shape[1] // 2
    far = shifted(left[:, :half], "x", nx, 1), shifted(right[:, half:], "x", nx, -1)
    wide = [dq, left, *far, right]
    dkv = lax.all_to_all(dkv, CTX, 0, 0, tiled=True)
    dkv_own = jnp.sum(dkv.astype(F32), axis=0).astype(BF)
    narrow = [dkv_own] + [shifted(dkv_own, "x", nx, s) for s in range(1, nx)]

    theirs = weight_part(features, wide, narrow, 1 - my_core, z_hi, ctx)
    theirs = shifted(theirs, "core", nc, 1)
    mine = weight_part(features, wide, narrow, my_core, z_hi, ctx)
    n = mine.shape[-1]
    part = plus(mine, theirs).reshape(ctx, -1, n)
    part = lax.all_to_all(part, CTX, 0, 0, tiled=True)
    part = jnp.sum(part.astype(F32), axis=0).astype(BF).reshape(z_hi, -1, n)
    part = lax.all_to_all(part, "zh", 0, 0, tiled=True)
    tokens = rows * ctx * nx * nc * z_hi
    weight = jnp.sum(part.astype(F32), axis=0) * (1.0 / math.sqrt(tokens))
    width = q.shape[1]
    return (
        dq[None],
        dkv_own[None, :, :hd],
        dkv_own[None, :, hd:],
        weight[:, :width],
        weight[:, width : width + hd],
        weight[:, width + hd :],
    )


def solution(mesh):
    fine = Mesh(mesh.devices.reshape(SIZES), AXES)
    dp = ("zh", "x", "core")
    tok = P(dp, CTX, None)
    row = P(dp + CTX, None)
    return jax.shard_map(
        local,
        mesh=fine,
        in_specs=(tok, tok, tok, tok, tok, P(dp, None)),
        out_specs=(tok, tok, tok, row, row, row),
        check_vma=False,
    )
```

```python
import functools
import math

import jax
import jax.numpy as jnp
from jax import lax
from jax.experimental import pallas as pl
from jax.experimental.pallas import tpu as pltpu
from jax.sharding import Mesh, PartitionSpec as P

NEG = -1e30
DOCS = 4
AXES = ("zh", "x", "core", "y", "zl")
SIZES = (4, 4, 2, 4, 2)
CTX = ("y", "zl")
BF = jnp.bfloat16
F32 = jnp.float32
NN = (((1,), (0,)), ((), ()))


def dot(a, b):
    return lax.dot_general(a, b, NN, preferred_element_type=F32)


def shifted(value, axis, count, step, wrap=True):
    pairs = []
    for src in range(count):
        dst = src + step
        if wrap:
            pairs.append((src, dst % count))
        elif 0 <= dst < count:
            pairs.append((src, dst))
    return lax.ppermute(value, axis, pairs)


def plus(a, b):
    return (a.astype(F32) + b.astype(F32)).astype(BF)


def whole(shape):
    return pl.BlockSpec(shape, lambda *g: (0,) * len(shape))


def attention_kernel(ny, per, docs, scale, info, docs_ref, q_ref, do_ref, *refs):
    (pair_ref, before_ref, far_refs, after_ref), refs = (refs[0], refs[1], refs[2:4], refs[4]), refs[5:]
    dq_ref, refs = refs[0], refs[1:]
    out_refs, refs = refs[: 2 * ny], refs[2 * ny :]
    kv_s, kt_s, e_s, dp_s, md_s, stat_s, dqt_s, qt_s, dot_s, p_s, ds_s, qk_s, dk_s, starts_ref, out_s, sem, out_sem = refs
    rows = q_ref.shape[0]
    hd = kt_s.shape[1]
    place = info[0]
    power = scale * math.log2(math.e)
    farthest = place // 2

    copies = [
        (0, pltpu.make_async_copy(pair_ref, kv_s.at[pl.ds(0, 2)], sem.at[0])),
        (1, pltpu.make_async_copy(before_ref, kv_s.at[pl.ds(2, 2)], sem.at[1])),
        (2, pltpu.make_async_copy(far_refs[0], kv_s.at[4], sem.at[2])),
        (2, pltpu.make_async_copy(far_refs[1], kv_s.at[5], sem.at[3])),
        (3, pltpu.make_async_copy(after_ref, kv_s.at[pl.ds(6, 2)], sem.at[4])),
    ]
    for s, copy in copies:
        pl.when(s <= farthest)(copy.start)

    for h in range(per):
        cols = slice(h * hd, (h + 1) * hd)
        span = slice(h * rows, (h + 1) * rows)
        qk_s[span] = q_ref[:, cols]
        dk_s[span] = do_ref[:, cols]
        qt_s[h] = q_ref[:, cols].T
        dot_s[h] = do_ref[:, cols].T
        stat_s[0, h] = jnp.full((1, rows), NEG, F32)
        stat_s[1, h] = jnp.zeros((1, rows), F32)
        stat_s[2, h] = jnp.zeros((1, rows), F32)
    dqt_s[...] = jnp.zeros_like(dqt_s)

    documents = docs_ref[...]
    mine = docs_ref[:, pl.ds(pl.multiple_of(place * rows, rows), rows)]
    starts = jnp.zeros((1, rows), jnp.int32)
    for t in range(docs - 1):
        length = jnp.sum((documents == t).astype(jnp.int32))
        starts += jnp.where(mine > t, length, 0)
    starts_ref[...] = starts
    limit = jnp.max(starts)
    used = place - jnp.min(starts) // rows + 1
    for s, copy in copies:
        pl.when(s <= farthest)(copy.wait)

    results = [
        pltpu.make_async_copy(out_s.at[d], out_refs[d], out_sem.at[d]) for d in range(2 * ny)
    ]

    def slot(d):
        block = place - d
        return 2 * (place // 2 - block // 2) + (d % 2)

    def forward(d, masked):
        at = slot(d)
        kd = kv_s[at, :, :hd]
        vd = kv_s[at, :, hd:]
        kt_s[at] = kd.T
        if masked:
            kp = lax.broadcasted_iota(jnp.int32, (rows, rows), 0) + (place - d) * rows
            qp = lax.broadcasted_iota(jnp.int32, (rows, rows), 1) + place * rows
            ok = (kp >= starts_ref[...]) & (kp <= qp)
        for h in range(per):
            s = dot(kd, qt_s[h])
            if masked:
                s = jnp.where(ok, s, NEG)
            old = stat_s[0, h]
            top = jnp.maximum(old, jnp.max(s, axis=0, keepdims=True))
            e = jnp.exp2(s * power - top * power)
            alpha = jnp.exp2((old - top) * power)
            dp = dot(vd, dot_s[h])
            stat_s[0, h] = top
            stat_s[1, h] = stat_s[1, h] * alpha + jnp.sum(e, axis=0, keepdims=True)
            stat_s[2, h] = stat_s[2, h] * alpha + jnp.sum(e * dp, axis=0, keepdims=True)
            e_s[d, h] = e
            dp_s[d, h] = dp
            md_s[d, h] = top

    def first(d, carry):
        masked = (d == 0) | ((place - d) * rows < limit)
        pl.when(masked)(lambda: forward(d, True))
        pl.when(jnp.logical_not(masked))(lambda: forward(d, False))
        return carry

    lax.fori_loop(0, used, first, 0)

    tops = [stat_s[0, h] for h in range(per)]
    inverse = [1.0 / stat_s[1, h] for h in range(per)]
    delta = [stat_s[2, h] * inverse[h] for h in range(per)]

    def second(d, carry):
        for h in range(per):
            p = e_s[d, h] * (jnp.exp2((md_s[d, h] - tops[h]) * power) * inverse[h])
            p_s[:, h * rows : (h + 1) * rows] = p.astype(BF)
            ds_s[:, h * rows : (h + 1) * rows] = (p * (dp_s[d, h] - delta[h])).astype(BF)
        out_s[d, :, hd:] = dot(p_s[...], dk_s[...]).astype(BF)
        out_s[d, :, :hd] = (dot(ds_s[...], qk_s[...]) * scale).astype(BF)
        for i, copy in enumerate(results):
            pl.when(d == i)(copy.start)
        dqt_s[...] += dot(kt_s[slot(d)], ds_s[...])
        return carry

    lax.fori_loop(0, used, second, 0)

    for d, copy in enumerate(results):

        @pl.when(d >= used)
        def _():
            out_s[d] = jnp.zeros(out_s.shape[1:], BF)
            copy.start()

    for h in range(per):
        dq_ref[:, h * hd : (h + 1) * hd] = (dqt_s[:, h * rows : (h + 1) * rows].T * scale).astype(BF)
    for copy in results:
        copy.wait()


def attention(q, do, kv, docs, place, ny):
    rows = q.shape[0]
    hd = kv[0].shape[2] // 2
    width = q.shape[1]
    per = width // hd
    blocks = 2 * ny
    slab = whole((rows, width))
    pair = kv[0].shape
    return pl.pallas_call(
        functools.partial(attention_kernel, ny, per, DOCS, hd ** (-0.5)),
        grid=(1,),
        in_specs=[pl.BlockSpec(memory_space=pltpu.SMEM), whole(docs.shape), slab, slab]
        + [pl.BlockSpec(memory_space=pl.ANY)] * len(kv),
        out_specs=[whole((rows, width))] + [pl.BlockSpec(memory_space=pl.ANY)] * blocks,
        out_shape=[jax.ShapeDtypeStruct((rows, width), BF)]
        + [jax.ShapeDtypeStruct(pair[1:], BF)] * blocks,
        scratch_shapes=[
            pltpu.VMEM((blocks, rows, 2 * hd), BF),
            pltpu.VMEM((blocks, hd, rows), BF),
            pltpu.VMEM((blocks, per, rows, rows), F32),
            pltpu.VMEM((blocks, per, rows, rows), F32),
            pltpu.VMEM((blocks, per, 1, rows), F32),
            pltpu.VMEM((3, per, 1, rows), F32),
            pltpu.VMEM((hd, per * rows), F32),
            pltpu.VMEM((per, hd, rows), BF),
            pltpu.VMEM((per, hd, rows), BF),
            pltpu.VMEM((rows, per * rows), BF),
            pltpu.VMEM((rows, per * rows), BF),
            pltpu.VMEM((per * rows, hd), BF),
            pltpu.VMEM((per * rows, hd), BF),
            pltpu.VMEM((1, rows), jnp.int32),
            pltpu.VMEM((blocks, rows, 2 * hd), BF),
            pltpu.SemaphoreType.DMA((len(kv),)),
            pltpu.SemaphoreType.DMA((blocks,)),
        ],
        compiler_params=pltpu.CompilerParams(vmem_limit_bytes=52 * 2**20),
        cost_estimate=pl.CostEstimate(
            flops=10 * per * rows * rows * blocks * hd,
            bytes_accessed=4 * 2**20,
            transcendentals=per * rows * rows * blocks,
        ),
        name="attention_backward",
    )(place[None], docs, q, do, *kv)


def split_kernel(info, *refs):
    half = len(refs) // 2
    for src, dst in zip(refs[:half], refs[half:]):
        dst[...] = src[...].T


def split_features(x, my_x, z_hi, nx):
    rows, dim = x.shape
    wide = dim // (z_hi * nx)

    def source(s):
        return pl.BlockSpec((rows, wide), lambda g, info: (0, g * nx + (info[0] + s) % nx))

    return pl.pallas_call(
        split_kernel,
        grid_spec=pltpu.PrefetchScalarGridSpec(
            num_scalar_prefetch=1,
            grid=(z_hi,),
            in_specs=[source(s) for s in range(nx)],
            out_specs=[pl.BlockSpec((wide, rows), lambda g, info: (g, 0))] * nx,
        ),
        out_shape=[jax.ShapeDtypeStruct((z_hi * wide, rows), x.dtype)] * nx,
        compiler_params=pltpu.CompilerParams(vmem_limit_bytes=16 * 2**20),
        name="split_features",
    )(my_x[None], *([x] * nx))


def weight_kernel(nx, z_hi, info, *refs):
    f_refs, wide_refs, narrow_refs = refs[:nx], refs[nx : 2 * nx + 1], refs[2 * nx + 1 : 3 * nx + 1]
    out_ref, ft_s = refs[3 * nx + 1 :]
    rows, width = wide_refs[0].shape
    each = f_refs[0].shape[0] // (z_hi * 2)
    cols = 256
    part = out_ref.shape[2]
    for s in range(nx):
        for z in range(z_hi):
            at = pl.multiple_of((z * 2 + info[0]) * each, each)
            ft_s[z * each : (z + 1) * each, s * rows : (s + 1) * rows] = f_refs[s][pl.ds(at, each)]

    def columns(blocks, to):
        total = dot(ft_s[:, :rows], blocks[0])
        for s in range(1, nx):
            total += dot(ft_s[:, s * rows : (s + 1) * rows], blocks[s])
        total = total.astype(BF)
        for z in range(z_hi):
            for p in range(out_ref.shape[0]):
                row = z * each + p * part
                out_ref[p, z, :, to : to + cols] = total[row : row + part]

    for at in range(0, width, cols):
        own, left, far_first, far_second, right = wide_refs
        split = far_first.shape[1]
        far = far_first[:, at : at + cols] if at < split else far_second[:, at - split : at - split + cols]
        columns([own[:, at : at + cols], left[:, at : at + cols], far, right[:, at : at + cols]], at)
    for at in range(0, narrow_refs[0].shape[1], cols):
        columns([ref[:, at : at + cols] for ref in narrow_refs], width + at)


def weight_part(features, wide, narrow, which, z_hi, pieces):
    nx = len(features)
    rows = wide[0].shape[0]
    each = features[0].shape[0] // (z_hi * 2)
    n = wide[0].shape[1] + narrow[0].shape[1]
    operands = [*features, *wide, *narrow]
    out_shape = (pieces, z_hi, each // pieces, n)
    return pl.pallas_call(
        functools.partial(weight_kernel, nx, z_hi),
        in_specs=[pl.BlockSpec(memory_space=pltpu.SMEM)]
        + [pl.BlockSpec(memory_space=pltpu.VMEM)] * len(operands),
        out_specs=pl.BlockSpec(memory_space=pltpu.VMEM),
        out_shape=jax.ShapeDtypeStruct(out_shape, BF),
        scratch_shapes=[pltpu.VMEM((z_hi * each, nx * rows), BF)],
        compiler_params=pltpu.CompilerParams(vmem_limit_bytes=20 * 2**20),
        cost_estimate=pl.CostEstimate(
            flops=2 * z_hi * each * nx * rows * n,
            bytes_accessed=6 * 2**20,
            transcendentals=0,
        ),
        name="weight_part",
    )(which[None], *operands)


def local(layer_input, queries, key_head, value_head, grad_output, doc_ids):
    x, q, k, v, do = (a[0] for a in (layer_input, queries, key_head, value_head, grad_output))
    rows, hd = k.shape
    ctx = lax.axis_size(CTX)
    nx, nc, z_hi = lax.axis_size("x"), lax.axis_size("core"), lax.axis_size("zh")
    ny, zl = lax.axis_size("y"), lax.axis_size("zl")
    place = lax.axis_index(CTX)
    my_x, my_core = lax.axis_index("x"), lax.axis_index("core")

    kv = jnp.concatenate([k, v], axis=1)
    other = shifted(kv, "zl", zl, 1)
    parts = split_features(x, my_x, z_hi, nx)
    other, parts = lax.optimization_barrier((other, parts))
    pair = jnp.stack([kv, other])
    before, after = shifted(pair, "y", ny, 1), shifted(pair, "y", ny, -1)
    far = shifted(before[0], "y", ny, 1), shifted(after[1], "y", ny, -1)
    features = [shifted(part, "x", nx, s) if s else part for s, part in enumerate(parts)]

    dq, *dkv = attention(q, do, [pair, before, *far, after], doc_ids, place, ny)
    dq, dkv, features = lax.optimization_barrier((dq, dkv, features))
    left, right = shifted(dq, "x", nx, 1), shifted(dq, "x", nx, -1)
    half = dq.shape[1] // 2
    far = shifted(left[:, :half], "x", nx, 1), shifted(right[:, half:], "x", nx, -1)
    wide = [dq, left, *far, right]
    total = dkv[0].astype(F32)
    for d in range(1, ctx):
        total = total + shifted(dkv[d], CTX, ctx, -d, False).astype(F32)
    dkv_own = total.astype(BF)
    narrow = [dkv_own] + [shifted(dkv_own, "x", nx, s) for s in range(1, nx)]

    theirs = weight_part(features, wide, narrow, 1 - my_core, z_hi, ctx)
    theirs = shifted(theirs, "core", nc, 1)
    mine = weight_part(features, wide, narrow, my_core, z_hi, ctx)
    n = mine.shape[-1]
    part = plus(mine, theirs).reshape(ctx, -1, n)
    part = lax.all_to_all(part, CTX, 0, 0, tiled=True)
    part = jnp.sum(part.astype(F32), axis=0).astype(BF).reshape(z_hi, -1, n)
    part = lax.all_to_all(part, "zh", 0, 0, tiled=True)
    tokens = rows * ctx * nx * nc * z_hi
    weight = jnp.sum(part.astype(F32), axis=0) * (1.0 / math.sqrt(tokens))
    width = q.shape[1]
    return (
        dq[None],
        dkv_own[None, :, :hd],
        dkv_own[None, :, hd:],
        weight[:, :width],
        weight[:, width : width + hd],
        weight[:, width + hd :],
    )


def solution(mesh):
    fine = Mesh(mesh.devices.reshape(SIZES), AXES)
    dp = ("zh", "x", "core")
    tok = P(dp, CTX, None)
    row = P(dp + CTX, None)
    return jax.shard_map(
        local,
        mesh=fine,
        in_specs=(tok, tok, tok, tok, tok, P(dp, None)),
        out_specs=(tok, tok, tok, row, row, row),
        check_vma=False,
    )
```

```python
import functools
import math

import jax
import jax.numpy as jnp
from jax import lax
from jax.experimental import pallas as pl
from jax.experimental.pallas import tpu as pltpu
from jax.sharding import Mesh, PartitionSpec as P

NEG = -1e30
DOCS = 4
AXES = ("zh", "x", "core", "y", "zl")
SIZES = (4, 4, 2, 4, 2)
CTX = ("y", "zl")
BF = jnp.bfloat16
F32 = jnp.float32
NN = (((1,), (0,)), ((), ()))


def dot(a, b):
    return lax.dot_general(a, b, NN, preferred_element_type=F32)


def shifted(value, axis, count, step, wrap=True):
    pairs = []
    for src in range(count):
        dst = src + step
        if wrap:
            pairs.append((src, dst % count))
        elif 0 <= dst < count:
            pairs.append((src, dst))
    return lax.ppermute(value, axis, pairs)


def plus(a, b):
    return (a.astype(F32) + b.astype(F32)).astype(BF)


def whole(shape):
    return pl.BlockSpec(shape, lambda *g: (0,) * len(shape))


def attention_kernel(ny, per, docs, scale, info, docs_ref, q_hbm, do_hbm, *refs):
    (pair_ref, before_ref, far_refs, after_ref), refs = (refs[0], refs[1], refs[2:4], refs[4]), refs[5:]
    dq_ref, refs = refs[0], refs[1:]
    out_ref, refs = refs[0], refs[1:]
    kv_s, kt_s, e_s, dp_s, md_s, stat_s, dqt_s, qt_s, dot_s, p_s, ds_s, qk_s, dk_s, starts_ref, q_ref, do_ref, sem, q_sem = refs
    rows = q_ref.shape[0]
    hd = kt_s.shape[1]
    place = info[0]
    power = scale * math.log2(math.e)
    farthest = place // 2

    copies = [
        (0, pltpu.make_async_copy(pair_ref, kv_s.at[pl.ds(0, 2)], sem.at[0])),
        (1, pltpu.make_async_copy(before_ref, kv_s.at[pl.ds(2, 2)], sem.at[1])),
        (2, pltpu.make_async_copy(far_refs[0], kv_s.at[4], sem.at[2])),
        (2, pltpu.make_async_copy(far_refs[1], kv_s.at[5], sem.at[3])),
        (3, pltpu.make_async_copy(after_ref, kv_s.at[pl.ds(6, 2)], sem.at[4])),
    ]
    loads = [
        pltpu.make_async_copy(q_hbm, q_ref, q_sem.at[0]),
        pltpu.make_async_copy(do_hbm, do_ref, q_sem.at[1]),
    ]
    for copy in loads:
        copy.start()
    for s, copy in copies:
        pl.when(s <= farthest)(copy.start)
    for copy in loads:
        copy.wait()

    for h in range(per):
        cols = slice(h * hd, (h + 1) * hd)
        span = slice(h * rows, (h + 1) * rows)
        qk_s[span] = q_ref[:, cols]
        dk_s[span] = do_ref[:, cols]
        qt_s[h] = q_ref[:, cols].T
        dot_s[h] = do_ref[:, cols].T
        stat_s[0, h] = jnp.full((1, rows), NEG, F32)
        stat_s[1, h] = jnp.zeros((1, rows), F32)
        stat_s[2, h] = jnp.zeros((1, rows), F32)
    dqt_s[...] = jnp.zeros_like(dqt_s)

    documents = docs_ref[...]
    mine = docs_ref[:, pl.ds(pl.multiple_of(place * rows, rows), rows)]
    starts = jnp.zeros((1, rows), jnp.int32)
    for t in range(docs - 1):
        length = jnp.sum((documents == t).astype(jnp.int32))
        starts += jnp.where(mine > t, length, 0)
    starts_ref[...] = starts
    limit = jnp.max(starts)
    used = place - jnp.min(starts) // rows + 1
    for s, copy in copies:
        pl.when(s <= farthest)(copy.wait)

    def clear(block, carry):
        out_ref[block] = jnp.zeros(out_ref.shape[1:], BF)
        return carry

    lax.fori_loop(0, place - used + 1, clear, 0)
    lax.fori_loop(place + 1, out_ref.shape[0], clear, 0)

    def slot(d):
        block = place - d
        return 2 * (place // 2 - block // 2) + (d % 2)

    def forward(d, masked):
        at = slot(d)
        kd = kv_s[at, :, :hd]
        vd = kv_s[at, :, hd:]
        kt_s[at] = kd.T
        if masked:
            kp = lax.broadcasted_iota(jnp.int32, (rows, rows), 0) + (place - d) * rows
            qp = lax.broadcasted_iota(jnp.int32, (rows, rows), 1) + place * rows
            ok = (kp >= starts_ref[...]) & (kp <= qp)
        for h in range(per):
            s = dot(kd, qt_s[h])
            if masked:
                s = jnp.where(ok, s, NEG)
            old = stat_s[0, h]
            top = jnp.maximum(old, jnp.max(s, axis=0, keepdims=True))
            e = jnp.exp2(s * power - top * power)
            alpha = jnp.exp2((old - top) * power)
            dp = dot(vd, dot_s[h])
            stat_s[0, h] = top
            stat_s[1, h] = stat_s[1, h] * alpha + jnp.sum(e, axis=0, keepdims=True)
            stat_s[2, h] = stat_s[2, h] * alpha + jnp.sum(e * dp, axis=0, keepdims=True)
            e_s[d, h] = e
            dp_s[d, h] = dp
            md_s[d, h] = top

    def first(d, carry):
        masked = (d == 0) | ((place - d) * rows < limit)
        pl.when(masked)(lambda: forward(d, True))
        pl.when(jnp.logical_not(masked))(lambda: forward(d, False))
        return carry

    lax.fori_loop(0, used, first, 0)

    tops = [stat_s[0, h] for h in range(per)]
    inverse = [1.0 / stat_s[1, h] for h in range(per)]
    delta = [stat_s[2, h] * inverse[h] for h in range(per)]

    def second(d, carry):
        for h in range(per):
            p = e_s[d, h] * (jnp.exp2((md_s[d, h] - tops[h]) * power) * inverse[h])
            p_s[:, h * rows : (h + 1) * rows] = p.astype(BF)
            ds_s[:, h * rows : (h + 1) * rows] = (p * (dp_s[d, h] - delta[h])).astype(BF)
        out_ref[place - d, :, hd:] = dot(p_s[...], dk_s[...]).astype(BF)
        out_ref[place - d, :, :hd] = (dot(ds_s[...], qk_s[...]) * scale).astype(BF)
        dqt_s[...] += dot(kt_s[slot(d)], ds_s[...])
        return carry

    lax.fori_loop(0, used, second, 0)

    for h in range(per):
        dq_ref[:, h * hd : (h + 1) * hd] = (dqt_s[:, h * rows : (h + 1) * rows].T * scale).astype(BF)


def attention(q, do, kv, docs, place, ny):
    rows = q.shape[0]
    hd = kv[0].shape[2] // 2
    width = q.shape[1]
    per = width // hd
    blocks = 2 * ny
    slab = pl.BlockSpec(memory_space=pltpu.HBM)
    pair = kv[0].shape
    return pl.pallas_call(
        functools.partial(attention_kernel, ny, per, DOCS, hd ** (-0.5)),
        grid=(1,),
        in_specs=[pl.BlockSpec(memory_space=pltpu.SMEM), whole(docs.shape), slab, slab]
        + [pl.BlockSpec(memory_space=pl.ANY)] * len(kv),
        out_specs=[whole((rows, width)), whole((blocks, *pair[1:]))],
        out_shape=[
            jax.ShapeDtypeStruct((rows, width), BF),
            jax.ShapeDtypeStruct((blocks, *pair[1:]), BF),
        ],
        scratch_shapes=[
            pltpu.VMEM((blocks, rows, 2 * hd), BF),
            pltpu.VMEM((blocks, hd, rows), BF),
            pltpu.VMEM((blocks, per, rows, rows), F32),
            pltpu.VMEM((blocks, per, rows, rows), F32),
            pltpu.VMEM((blocks, per, 1, rows), F32),
            pltpu.VMEM((3, per, 1, rows), F32),
            pltpu.VMEM((hd, per * rows), F32),
            pltpu.VMEM((per, hd, rows), BF),
            pltpu.VMEM((per, hd, rows), BF),
            pltpu.VMEM((rows, per * rows), BF),
            pltpu.VMEM((rows, per * rows), BF),
            pltpu.VMEM((per * rows, hd), BF),
            pltpu.VMEM((per * rows, hd), BF),
            pltpu.VMEM((1, rows), jnp.int32),
            pltpu.VMEM((rows, width), BF),
            pltpu.VMEM((rows, width), BF),
            pltpu.SemaphoreType.DMA((len(kv),)),
            pltpu.SemaphoreType.DMA((2,)),
        ],
        compiler_params=pltpu.CompilerParams(vmem_limit_bytes=52 * 2**20),
        cost_estimate=pl.CostEstimate(
            flops=10 * per * rows * rows * blocks * hd,
            bytes_accessed=4 * 2**20,
            transcendentals=per * rows * rows * blocks,
        ),
        name="attention_backward",
    )(place[None], docs, q, do, *kv)


def split_kernel(info, *refs):
    half = len(refs) // 2
    for src, dst in zip(refs[:half], refs[half:]):
        dst[...] = src[...].T


def split_features(x, my_x, z_hi, nx):
    rows, dim = x.shape
    wide = dim // (z_hi * nx)

    def source(s):
        return pl.BlockSpec((rows, wide), lambda g, info: (0, g * nx + (info[0] + s) % nx))

    return pl.pallas_call(
        split_kernel,
        grid_spec=pltpu.PrefetchScalarGridSpec(
            num_scalar_prefetch=1,
            grid=(z_hi,),
            in_specs=[source(s) for s in range(nx)],
            out_specs=[pl.BlockSpec((wide, rows), lambda g, info: (g, 0))] * nx,
        ),
        out_shape=[jax.ShapeDtypeStruct((z_hi * wide, rows), x.dtype)] * nx,
        compiler_params=pltpu.CompilerParams(vmem_limit_bytes=16 * 2**20),
        name="split_features",
    )(my_x[None], *([x] * nx))


def weight_kernel(nx, z_hi, info, *refs):
    f_refs, wide_refs, narrow_refs = refs[:nx], refs[nx : 2 * nx + 1], refs[2 * nx + 1 : 3 * nx + 1]
    out_ref, ft_s = refs[3 * nx + 1 :]
    rows, width = wide_refs[0].shape
    each = f_refs[0].shape[0] // (z_hi * 2)
    cols = 256
    part = out_ref.shape[2]
    for s in range(nx):
        for z in range(z_hi):
            at = pl.multiple_of((z * 2 + info[0]) * each, each)
            ft_s[z * each : (z + 1) * each, s * rows : (s + 1) * rows] = f_refs[s][pl.ds(at, each)]

    def columns(blocks, to):
        total = dot(ft_s[:, :rows], blocks[0])
        for s in range(1, nx):
            total += dot(ft_s[:, s * rows : (s + 1) * rows], blocks[s])
        total = total.astype(BF)
        for z in range(z_hi):
            for p in range(out_ref.shape[0]):
                row = z * each + p * part
                out_ref[p, z, :, to : to + cols] = total[row : row + part]

    for at in range(0, width, cols):
        own, left, far_first, far_second, right = wide_refs
        split = far_first.shape[1]
        far = far_first[:, at : at + cols] if at < split else far_second[:, at - split : at - split + cols]
        columns([own[:, at : at + cols], left[:, at : at + cols], far, right[:, at : at + cols]], at)
    for at in range(0, narrow_refs[0].shape[1], cols):
        columns([ref[:, at : at + cols] for ref in narrow_refs], width + at)


def weight_part(features, wide, narrow, which, z_hi, pieces):
    nx = len(features)
    rows = wide[0].shape[0]
    each = features[0].shape[0] // (z_hi * 2)
    n = wide[0].shape[1] + narrow[0].shape[1]
    operands = [*features, *wide, *narrow]
    out_shape = (pieces, z_hi, each // pieces, n)
    return pl.pallas_call(
        functools.partial(weight_kernel, nx, z_hi),
        in_specs=[pl.BlockSpec(memory_space=pltpu.SMEM)]
        + [pl.BlockSpec(memory_space=pltpu.VMEM)] * len(operands),
        out_specs=pl.BlockSpec(memory_space=pltpu.VMEM),
        out_shape=jax.ShapeDtypeStruct(out_shape, BF),
        scratch_shapes=[pltpu.VMEM((z_hi * each, nx * rows), BF)],
        compiler_params=pltpu.CompilerParams(vmem_limit_bytes=20 * 2**20),
        cost_estimate=pl.CostEstimate(
            flops=2 * z_hi * each * nx * rows * n,
            bytes_accessed=6 * 2**20,
            transcendentals=0,
        ),
        name="weight_part",
    )(which[None], *operands)


def local(layer_input, queries, key_head, value_head, grad_output, doc_ids):
    x, q, k, v, do = (a[0] for a in (layer_input, queries, key_head, value_head, grad_output))
    rows, hd = k.shape
    ctx = lax.axis_size(CTX)
    nx, nc, z_hi = lax.axis_size("x"), lax.axis_size("core"), lax.axis_size("zh")
    ny, zl = lax.axis_size("y"), lax.axis_size("zl")
    place = lax.axis_index(CTX)
    my_x, my_core = lax.axis_index("x"), lax.axis_index("core")

    kv = jnp.concatenate([k, v], axis=1)
    other = shifted(kv, "zl", zl, 1)
    parts = split_features(x, my_x, z_hi, nx)
    other, parts = lax.optimization_barrier((other, parts))
    pair = jnp.stack([kv, other])
    before, after = shifted(pair, "y", ny, 1), shifted(pair, "y", ny, -1)
    far = shifted(before[0], "y", ny, 1), shifted(after[1], "y", ny, -1)
    features = [shifted(part, "x", nx, s) if s else part for s, part in enumerate(parts)]

    dq, dkv = attention(q, do, [pair, before, *far, after], doc_ids, place, ny)
    dq, dkv, features = lax.optimization_barrier((dq, dkv, features))
    left, right = shifted(dq, "x", nx, 1), shifted(dq, "x", nx, -1)
    dkv = lax.all_to_all(dkv, CTX, 0, 0, tiled=True)
    dkv_own = jnp.sum(dkv.astype(F32), axis=0).astype(BF)
    narrow = [dkv_own] + [shifted(dkv_own, "x", nx, s) for s in range(1, nx)]
    left, right, dkv_own = lax.optimization_barrier((left, right, dkv_own))
    half = dq.shape[1] // 2
    far = shifted(left[:, :half], "x", nx, 1), shifted(right[:, half:], "x", nx, -1)
    wide = [dq, left, *far, right]

    theirs = weight_part(features, wide, narrow, 1 - my_core, z_hi, ctx)
    theirs = shifted(theirs, "core", nc, 1)
    mine = weight_part(features, wide, narrow, my_core, z_hi, ctx)
    n = mine.shape[-1]
    part = plus(mine, theirs).reshape(ctx, -1, n)
    part = lax.all_to_all(part, CTX, 0, 0, tiled=True)
    part = jnp.sum(part.astype(F32), axis=0).astype(BF).reshape(z_hi, -1, n)
    part = lax.all_to_all(part, "zh", 0, 0, tiled=True)
    tokens = rows * ctx * nx * nc * z_hi
    weight = jnp.sum(part.astype(F32), axis=0) * (1.0 / math.sqrt(tokens))
    width = q.shape[1]
    return (
        dq[None],
        dkv_own[None, :, :hd],
        dkv_own[None, :, hd:],
        weight[:, :width],
        weight[:, width : width + hd],
        weight[:, width + hd :],
    )


def solution(mesh):
    fine = Mesh(mesh.devices.reshape(SIZES), AXES)
    dp = ("zh", "x", "core")
    tok = P(dp, CTX, None)
    row = P(dp + CTX, None)
    return jax.shard_map(
        local,
        mesh=fine,
        in_specs=(tok, tok, tok, tok, tok, P(dp, None)),
        out_specs=(tok, tok, tok, row, row, row),
        check_vma=False,
    )
```

```python
import functools
import math

import jax
import jax.numpy as jnp
from jax import lax
from jax.experimental import pallas as pl
from jax.experimental.pallas import tpu as pltpu
from jax.sharding import Mesh, PartitionSpec as P

NEG = -1e30
DOCS = 4
AXES = ("zh", "x", "core", "y", "zl")
SIZES = (4, 4, 2, 4, 2)
CTX = ("y", "zl")
BF = jnp.bfloat16
F32 = jnp.float32
NN = (((1,), (0,)), ((), ()))


def dot(a, b):
    return lax.dot_general(a, b, NN, preferred_element_type=F32)


def shifted(value, axis, count, step, wrap=True):
    pairs = []
    for src in range(count):
        dst = src + step
        if wrap:
            pairs.append((src, dst % count))
        elif 0 <= dst < count:
            pairs.append((src, dst))
    return lax.ppermute(value, axis, pairs)


def plus(a, b):
    return (a.astype(F32) + b.astype(F32)).astype(BF)


def whole(shape):
    return pl.BlockSpec(shape, lambda *g: (0,) * len(shape))


def attention_kernel(ny, per, docs, scale, info, docs_ref, q_hbm, do_hbm, *refs):
    (pair_ref, before_ref, far_refs, after_ref), refs = (refs[0], refs[1], refs[2:4], refs[4]), refs[5:]
    dq_ref, refs = refs[0], refs[1:]
    out_ref, refs = refs[0], refs[1:]
    kv_s, kt_s, e_s, dp_s, md_s, stat_s, dqt_s, qt_s, dot_s, p_s, ds_s, qk_s, dk_s, starts_ref, q_ref, do_ref, sem, q_sem = refs
    rows = q_ref.shape[0]
    hd = kt_s.shape[1]
    place = info[0]
    power = scale * math.log2(math.e)
    farthest = place // 2

    copies = [
        (0, pltpu.make_async_copy(pair_ref, kv_s.at[pl.ds(0, 2)], sem.at[0])),
        (1, pltpu.make_async_copy(before_ref, kv_s.at[pl.ds(2, 2)], sem.at[1])),
        (2, pltpu.make_async_copy(far_refs[0], kv_s.at[4], sem.at[2])),
        (2, pltpu.make_async_copy(far_refs[1], kv_s.at[5], sem.at[3])),
        (3, pltpu.make_async_copy(after_ref, kv_s.at[pl.ds(6, 2)], sem.at[4])),
    ]
    loads = [
        pltpu.make_async_copy(q_hbm, q_ref, q_sem.at[0]),
        pltpu.make_async_copy(do_hbm, do_ref, q_sem.at[1]),
    ]
    for copy in loads:
        copy.start()
    for s, copy in copies:
        pl.when(s <= farthest)(copy.start)
    for copy in loads:
        copy.wait()

    for h in range(per):
        cols = slice(h * hd, (h + 1) * hd)
        span = slice(h * rows, (h + 1) * rows)
        qk_s[span] = q_ref[:, cols]
        dk_s[span] = do_ref[:, cols]
        qt_s[h] = q_ref[:, cols].T
        dot_s[h] = do_ref[:, cols].T
        stat_s[0, h] = jnp.full((1, rows), NEG, F32)
        stat_s[1, h] = jnp.zeros((1, rows), F32)
        stat_s[2, h] = jnp.zeros((1, rows), F32)
    dqt_s[...] = jnp.zeros_like(dqt_s)

    documents = docs_ref[...]
    mine = docs_ref[:, pl.ds(pl.multiple_of(place * rows, rows), rows)]
    starts = jnp.zeros((1, rows), jnp.int32)
    for t in range(docs - 1):
        length = jnp.sum((documents == t).astype(jnp.int32))
        starts += jnp.where(mine > t, length, 0)
    starts_ref[...] = starts
    limit = jnp.max(starts)
    used = place - jnp.min(starts) // rows + 1
    for s, copy in copies:
        pl.when(s <= farthest)(copy.wait)

    def clear(block, carry):
        out_ref[block] = jnp.zeros(out_ref.shape[1:], BF)
        return carry

    lax.fori_loop(0, place - used + 1, clear, 0)
    lax.fori_loop(place + 1, out_ref.shape[0], clear, 0)

    def slot(d):
        block = place - d
        return 2 * (place // 2 - block // 2) + (d % 2)

    def forward(d, masked):
        at = slot(d)
        kd = kv_s[at, :, :hd]
        vd = kv_s[at, :, hd:]
        kt_s[at] = kd.T
        if masked:
            kp = lax.broadcasted_iota(jnp.int32, (rows, rows), 0) + (place - d) * rows
            qp = lax.broadcasted_iota(jnp.int32, (rows, rows), 1) + place * rows
            ok = (kp >= starts_ref[...]) & (kp <= qp)
        for h in range(per):
            s = dot(kd, qt_s[h])
            if masked:
                s = jnp.where(ok, s, NEG)
            old = stat_s[0, h]
            top = jnp.maximum(old, jnp.max(s, axis=0, keepdims=True))
            e = jnp.exp2(s * power - top * power)
            alpha = jnp.exp2((old - top) * power)
            dp = dot(vd, dot_s[h])
            stat_s[0, h] = top
            stat_s[1, h] = stat_s[1, h] * alpha + jnp.sum(e, axis=0, keepdims=True)
            stat_s[2, h] = stat_s[2, h] * alpha + jnp.sum(e * dp, axis=0, keepdims=True)
            e_s[d, h] = e
            dp_s[d, h] = dp
            md_s[d, h] = top

    def first(d, carry):
        masked = (d == 0) | ((place - d) * rows < limit)
        pl.when(masked)(lambda: forward(d, True))
        pl.when(jnp.logical_not(masked))(lambda: forward(d, False))
        return carry

    lax.fori_loop(0, used, first, 0)

    tops = [stat_s[0, h] for h in range(per)]
    inverse = [1.0 / stat_s[1, h] for h in range(per)]
    delta = [stat_s[2, h] * inverse[h] for h in range(per)]

    def second(d, carry):
        for h in range(per):
            p = e_s[d, h] * (jnp.exp2((md_s[d, h] - tops[h]) * power) * inverse[h])
            p_s[:, h * rows : (h + 1) * rows] = p.astype(BF)
            ds_s[:, h * rows : (h + 1) * rows] = (p * (dp_s[d, h] - delta[h])).astype(BF)
        out_ref[place - d, :, hd:] = dot(p_s[...], dk_s[...]).astype(BF)
        out_ref[place - d, :, :hd] = (dot(ds_s[...], qk_s[...]) * scale).astype(BF)
        dqt_s[...] += dot(kt_s[slot(d)], ds_s[...])
        return carry

    lax.fori_loop(0, used, second, 0)

    for h in range(per):
        dq_ref[:, h * hd : (h + 1) * hd] = (dqt_s[:, h * rows : (h + 1) * rows].T * scale).astype(BF)


def attention(q, do, kv, docs, place, ny):
    rows = q.shape[0]
    hd = kv[0].shape[2] // 2
    width = q.shape[1]
    per = width // hd
    blocks = 2 * ny
    slab = pl.BlockSpec(memory_space=pltpu.HBM)
    pair = kv[0].shape
    return pl.pallas_call(
        functools.partial(attention_kernel, ny, per, DOCS, hd ** (-0.5)),
        grid=(1,),
        in_specs=[pl.BlockSpec(memory_space=pltpu.SMEM), whole(docs.shape), slab, slab]
        + [pl.BlockSpec(memory_space=pl.ANY)] * len(kv),
        out_specs=[whole((rows, width)), whole((blocks, *pair[1:]))],
        out_shape=[
            jax.ShapeDtypeStruct((rows, width), BF),
            jax.ShapeDtypeStruct((blocks, *pair[1:]), BF),
        ],
        scratch_shapes=[
            pltpu.VMEM((blocks, rows, 2 * hd), BF),
            pltpu.VMEM((blocks, hd, rows), BF),
            pltpu.VMEM((blocks, per, rows, rows), F32),
            pltpu.VMEM((blocks, per, rows, rows), F32),
            pltpu.VMEM((blocks, per, 1, rows), F32),
            pltpu.VMEM((3, per, 1, rows), F32),
            pltpu.VMEM((hd, per * rows), F32),
            pltpu.VMEM((per, hd, rows), BF),
            pltpu.VMEM((per, hd, rows), BF),
            pltpu.VMEM((rows, per * rows), BF),
            pltpu.VMEM((rows, per * rows), BF),
            pltpu.VMEM((per * rows, hd), BF),
            pltpu.VMEM((per * rows, hd), BF),
            pltpu.VMEM((1, rows), jnp.int32),
            pltpu.VMEM((rows, width), BF),
            pltpu.VMEM((rows, width), BF),
            pltpu.SemaphoreType.DMA((len(kv),)),
            pltpu.SemaphoreType.DMA((2,)),
        ],
        compiler_params=pltpu.CompilerParams(vmem_limit_bytes=52 * 2**20),
        cost_estimate=pl.CostEstimate(
            flops=4 * per * rows * rows * blocks * hd,
            bytes_accessed=4 * 2**20,
            transcendentals=0,
        ),
        name="attention_backward",
    )(place[None], docs, q, do, *kv)


def split_kernel(info, *refs):
    half = len(refs) // 2
    for src, dst in zip(refs[:half], refs[half:]):
        dst[...] = src[...].T


def split_features(x, my_x, z_hi, nx):
    rows, dim = x.shape
    wide = dim // (z_hi * nx)

    def source(s):
        return pl.BlockSpec((rows, wide), lambda g, info: (0, g * nx + (info[0] + s) % nx))

    return pl.pallas_call(
        split_kernel,
        grid_spec=pltpu.PrefetchScalarGridSpec(
            num_scalar_prefetch=1,
            grid=(z_hi,),
            in_specs=[source(s) for s in range(nx)],
            out_specs=[pl.BlockSpec((wide, rows), lambda g, info: (g, 0))] * nx,
        ),
        out_shape=[jax.ShapeDtypeStruct((z_hi * wide, rows), x.dtype)] * nx,
        compiler_params=pltpu.CompilerParams(vmem_limit_bytes=16 * 2**20),
        name="split_features",
    )(my_x[None], *([x] * nx))


def weight_kernel(nx, z_hi, info, *refs):
    f_refs, wide_refs, narrow_refs = refs[:nx], refs[nx : 2 * nx + 1], refs[2 * nx + 1 : 3 * nx + 1]
    out_ref, ft_s = refs[3 * nx + 1 :]
    rows, width = wide_refs[0].shape
    each = f_refs[0].shape[0] // (z_hi * 2)
    cols = 256
    part = out_ref.shape[2]
    for s in range(nx):
        for z in range(z_hi):
            at = pl.multiple_of((z * 2 + info[0]) * each, each)
            ft_s[z * each : (z + 1) * each, s * rows : (s + 1) * rows] = f_refs[s][pl.ds(at, each)]

    def columns(blocks, to):
        total = dot(ft_s[:, :rows], blocks[0])
        for s in range(1, nx):
            total += dot(ft_s[:, s * rows : (s + 1) * rows], blocks[s])
        total = total.astype(BF)
        for z in range(z_hi):
            for p in range(out_ref.shape[0]):
                row = z * each + p * part
                out_ref[p, z, :, to : to + cols] = total[row : row + part]

    for at in range(0, width, cols):
        own, left, far_first, far_second, right = wide_refs
        split = far_first.shape[1]
        far = far_first[:, at : at + cols] if at < split else far_second[:, at - split : at - split + cols]
        columns([own[:, at : at + cols], left[:, at : at + cols], far, right[:, at : at + cols]], at)
    for at in range(0, narrow_refs[0].shape[1], cols):
        columns([ref[:, at : at + cols] for ref in narrow_refs], width + at)


def weight_part(features, wide, narrow, which, z_hi, pieces):
    nx = len(features)
    rows = wide[0].shape[0]
    each = features[0].shape[0] // (z_hi * 2)
    n = wide[0].shape[1] + narrow[0].shape[1]
    operands = [*features, *wide, *narrow]
    out_shape = (pieces, z_hi, each // pieces, n)
    return pl.pallas_call(
        functools.partial(weight_kernel, nx, z_hi),
        in_specs=[pl.BlockSpec(memory_space=pltpu.SMEM)]
        + [pl.BlockSpec(memory_space=pltpu.VMEM)] * len(operands),
        out_specs=pl.BlockSpec(memory_space=pltpu.VMEM),
        out_shape=jax.ShapeDtypeStruct(out_shape, BF),
        scratch_shapes=[pltpu.VMEM((z_hi * each, nx * rows), BF)],
        compiler_params=pltpu.CompilerParams(vmem_limit_bytes=20 * 2**20),
        cost_estimate=pl.CostEstimate(
            flops=2 * z_hi * each * nx * rows * n,
            bytes_accessed=6 * 2**20,
            transcendentals=0,
        ),
        name="weight_part",
    )(which[None], *operands)


def local(layer_input, queries, key_head, value_head, grad_output, doc_ids):
    x, q, k, v, do = (a[0] for a in (layer_input, queries, key_head, value_head, grad_output))
    rows, hd = k.shape
    ctx = lax.axis_size(CTX)
    nx, nc, z_hi = lax.axis_size("x"), lax.axis_size("core"), lax.axis_size("zh")
    ny, zl = lax.axis_size("y"), lax.axis_size("zl")
    place = lax.axis_index(CTX)
    my_x, my_core = lax.axis_index("x"), lax.axis_index("core")

    kv = jnp.concatenate([k, v], axis=1)
    other = shifted(kv, "zl", zl, 1)
    parts = split_features(x, my_x, z_hi, nx)
    other, parts = lax.optimization_barrier((other, parts))
    pair = jnp.stack([kv, other])
    before, after = shifted(pair, "y", ny, 1), shifted(pair, "y", ny, -1)
    far = shifted(before[0], "y", ny, 1), shifted(after[1], "y", ny, -1)
    features = [shifted(part, "x", nx, s) if s else part for s, part in enumerate(parts)]

    dq, dkv = attention(q, do, [pair, before, *far, after], doc_ids, place, ny)
    dq, dkv, features = lax.optimization_barrier((dq, dkv, features))
    left, right = shifted(dq, "x", nx, 1), shifted(dq, "x", nx, -1)
    dkv = lax.all_to_all(dkv, CTX, 0, 0, tiled=True)
    dkv_own = jnp.sum(dkv.astype(F32), axis=0).astype(BF)
    narrow = [dkv_own] + [shifted(dkv_own, "x", nx, s) for s in range(1, nx)]
    left, right, dkv_own = lax.optimization_barrier((left, right, dkv_own))
    half = dq.shape[1] // 2
    far = shifted(left[:, :half], "x", nx, 1), shifted(right[:, half:], "x", nx, -1)
    wide = [dq, left, *far, right]

    theirs = weight_part(features, wide, narrow, 1 - my_core, z_hi, ctx)
    theirs = shifted(theirs, "core", nc, 1)
    mine = weight_part(features, wide, narrow, my_core, z_hi, ctx)
    n = mine.shape[-1]
    part = plus(mine, theirs).reshape(ctx, -1, n)
    part = lax.all_to_all(part, CTX, 0, 0, tiled=True)
    part = jnp.sum(part.astype(F32), axis=0).astype(BF).reshape(z_hi, -1, n)
    part = lax.all_to_all(part, "zh", 0, 0, tiled=True)
    tokens = rows * ctx * nx * nc * z_hi
    weight = jnp.sum(part.astype(F32), axis=0) * (1.0 / math.sqrt(tokens))
    width = q.shape[1]
    return (
        dq[None],
        dkv_own[None, :, :hd],
        dkv_own[None, :, hd:],
        weight[:, :width],
        weight[:, width : width + hd],
        weight[:, width + hd :],
    )


def solution(mesh):
    fine = Mesh(mesh.devices.reshape(SIZES), AXES)
    dp = ("zh", "x", "core")
    tok = P(dp, CTX, None)
    row = P(dp + CTX, None)
    return jax.shard_map(
        local,
        mesh=fine,
        in_specs=(tok, tok, tok, tok, tok, P(dp, None)),
        out_specs=(tok, tok, tok, row, row, row),
        check_vma=False,
    )
```

```python
import functools
import math

import jax
import jax.numpy as jnp
from jax import lax
from jax.experimental import pallas as pl
from jax.experimental.pallas import tpu as pltpu
from jax.sharding import Mesh, PartitionSpec as P

NEG = -1e30
DOCS = 4
AXES = ("zh", "x", "core", "y", "zl")
SIZES = (4, 4, 2, 4, 2)
CTX = ("y", "zl")
BF = jnp.bfloat16
F32 = jnp.float32
NN = (((1,), (0,)), ((), ()))


def dot(a, b):
    return lax.dot_general(a, b, NN, preferred_element_type=F32)


def shifted(value, axis, count, step, wrap=True):
    pairs = []
    for src in range(count):
        dst = src + step
        if wrap:
            pairs.append((src, dst % count))
        elif 0 <= dst < count:
            pairs.append((src, dst))
    return lax.ppermute(value, axis, pairs)


def plus(a, b):
    return (a.astype(F32) + b.astype(F32)).astype(BF)


def whole(shape):
    return pl.BlockSpec(shape, lambda *g: (0,) * len(shape))


def attention_kernel(ny, per, docs, scale, info, docs_ref, q_hbm, do_hbm, *refs):
    (pair_ref, before_ref, far_refs, after_ref), refs = (refs[0], refs[1], refs[2:4], refs[4]), refs[5:]
    dq_ref, refs = refs[0], refs[1:]
    out_ref, refs = refs[0], refs[1:]
    kv_s, kt_s, e_s, dp_s, md_s, stat_s, dqt_s, qt_s, dot_s, p_s, ds_s, qk_s, dk_s, starts_ref, q_ref, do_ref, sem, q_sem = refs
    rows = q_ref.shape[0]
    hd = kt_s.shape[1]
    place = info[0]
    power = scale * math.log2(math.e)
    farthest = place // 2

    copies = [
        (0, pltpu.make_async_copy(pair_ref, kv_s.at[pl.ds(0, 2)], sem.at[0])),
        (1, pltpu.make_async_copy(before_ref, kv_s.at[pl.ds(2, 2)], sem.at[1])),
        (2, pltpu.make_async_copy(far_refs[0], kv_s.at[4], sem.at[2])),
        (2, pltpu.make_async_copy(far_refs[1], kv_s.at[5], sem.at[3])),
        (3, pltpu.make_async_copy(after_ref, kv_s.at[pl.ds(6, 2)], sem.at[4])),
    ]
    loads = [
        pltpu.make_async_copy(q_hbm, q_ref, q_sem.at[0]),
        pltpu.make_async_copy(do_hbm, do_ref, q_sem.at[1]),
    ]
    for copy in loads:
        copy.start()
    for s, copy in copies:
        pl.when(s <= farthest)(copy.start)
    for copy in loads:
        copy.wait()

    for h in range(per):
        cols = slice(h * hd, (h + 1) * hd)
        span = slice(h * rows, (h + 1) * rows)
        qk_s[span] = q_ref[:, cols]
        dk_s[span] = do_ref[:, cols]
        qt_s[h] = q_ref[:, cols].T
        dot_s[h] = do_ref[:, cols].T
        stat_s[0, h] = jnp.full((1, rows), NEG, F32)
        stat_s[1, h] = jnp.zeros((1, rows), F32)
        stat_s[2, h] = jnp.zeros((1, rows), F32)
    dqt_s[...] = jnp.zeros_like(dqt_s)

    documents = docs_ref[...]
    mine = docs_ref[:, pl.ds(pl.multiple_of(place * rows, rows), rows)]
    starts = jnp.zeros((1, rows), jnp.int32)
    for t in range(docs - 1):
        length = jnp.sum((documents == t).astype(jnp.int32))
        starts += jnp.where(mine > t, length, 0)
    starts_ref[...] = starts
    limit = jnp.max(starts)
    used = place - jnp.min(starts) // rows + 1
    for s, copy in copies:
        pl.when(s <= farthest)(copy.wait)

    def clear(block, carry):
        out_ref[block] = jnp.zeros(out_ref.shape[1:], BF)
        return carry

    lax.fori_loop(0, place - used + 1, clear, 0)
    lax.fori_loop(place + 1, out_ref.shape[0], clear, 0)

    def slot(d):
        block = place - d
        return 2 * (place // 2 - block // 2) + (d % 2)

    def forward(d, masked):
        at = slot(d)
        kd = kv_s[at, :, :hd]
        vd = kv_s[at, :, hd:]
        kt_s[at] = kd.T
        if masked:
            kp = lax.broadcasted_iota(jnp.int32, (rows, rows), 0) + (place - d) * rows
            qp = lax.broadcasted_iota(jnp.int32, (rows, rows), 1) + place * rows
            ok = (kp >= starts_ref[...]) & (kp <= qp)
        for h in range(per):
            s = dot(kd, qt_s[h])
            if masked:
                s = jnp.where(ok, s, NEG)
            old = stat_s[0, h]
            top = jnp.maximum(old, jnp.max(s, axis=0, keepdims=True))
            e = jnp.exp2(s * power - top * power)
            alpha = jnp.exp2((old - top) * power)
            dp = dot(vd, dot_s[h])
            stat_s[0, h] = top
            stat_s[1, h] = stat_s[1, h] * alpha + jnp.sum(e, axis=0, keepdims=True)
            stat_s[2, h] = stat_s[2, h] * alpha + jnp.sum(e * dp, axis=0, keepdims=True)
            e_s[d, h] = e
            dp_s[d, h] = dp
            md_s[d, h] = top

    def first(d, carry):
        masked = (d == 0) | ((place - d) * rows < limit)
        pl.when(masked)(lambda: forward(d, True))
        pl.when(jnp.logical_not(masked))(lambda: forward(d, False))
        return carry

    lax.fori_loop(0, used, first, 0)

    tops = [stat_s[0, h] for h in range(per)]
    inverse = [1.0 / stat_s[1, h] for h in range(per)]
    delta = [stat_s[2, h] * inverse[h] for h in range(per)]

    def second(d, carry):
        for h in range(per):
            p = e_s[d, h] * (jnp.exp2((md_s[d, h] - tops[h]) * power) * inverse[h])
            p_s[:, h * rows : (h + 1) * rows] = p.astype(BF)
            ds_s[:, h * rows : (h + 1) * rows] = (p * (dp_s[d, h] - delta[h])).astype(BF)
        out_ref[place - d, :, hd:] = dot(p_s[...], dk_s[...]).astype(BF)
        out_ref[place - d, :, :hd] = (dot(ds_s[...], qk_s[...]) * scale).astype(BF)
        dqt_s[...] += dot(kt_s[slot(d)], ds_s[...])
        return carry

    lax.fori_loop(0, used, second, 0)

    for h in range(per):
        dq_ref[:, h * hd : (h + 1) * hd] = (dqt_s[:, h * rows : (h + 1) * rows].T * scale).astype(BF)


def attention(q, do, kv, docs, place, ny):
    rows = q.shape[0]
    hd = kv[0].shape[2] // 2
    width = q.shape[1]
    per = width // hd
    blocks = 2 * ny
    slab = pl.BlockSpec(memory_space=pltpu.HBM)
    pair = kv[0].shape
    return pl.pallas_call(
        functools.partial(attention_kernel, ny, per, DOCS, hd ** (-0.5)),
        grid=(1,),
        in_specs=[pl.BlockSpec(memory_space=pltpu.SMEM), whole(docs.shape), slab, slab]
        + [pl.BlockSpec(memory_space=pl.ANY)] * len(kv),
        out_specs=[whole((rows, width)), whole((blocks, *pair[1:]))],
        out_shape=[
            jax.ShapeDtypeStruct((rows, width), BF),
            jax.ShapeDtypeStruct((blocks, *pair[1:]), BF),
        ],
        scratch_shapes=[
            pltpu.VMEM((blocks, rows, 2 * hd), BF),
            pltpu.VMEM((blocks, hd, rows), BF),
            pltpu.VMEM((blocks, per, rows, rows), F32),
            pltpu.VMEM((blocks, per, rows, rows), F32),
            pltpu.VMEM((blocks, per, 1, rows), F32),
            pltpu.VMEM((3, per, 1, rows), F32),
            pltpu.VMEM((hd, per * rows), F32),
            pltpu.VMEM((per, hd, rows), BF),
            pltpu.VMEM((per, hd, rows), BF),
            pltpu.VMEM((rows, per * rows), BF),
            pltpu.VMEM((rows, per * rows), BF),
            pltpu.VMEM((per * rows, hd), BF),
            pltpu.VMEM((per * rows, hd), BF),
            pltpu.VMEM((1, rows), jnp.int32),
            pltpu.VMEM((rows, width), BF),
            pltpu.VMEM((rows, width), BF),
            pltpu.SemaphoreType.DMA((len(kv),)),
            pltpu.SemaphoreType.DMA((2,)),
        ],
        compiler_params=pltpu.CompilerParams(vmem_limit_bytes=52 * 2**20),
        cost_estimate=pl.CostEstimate(
            flops=4 * per * rows * rows * blocks * hd,
            bytes_accessed=4 * 2**20,
            transcendentals=0,
        ),
        name="attention_backward",
    )(place[None], docs, q, do, *kv)


def split_kernel(info, *refs):
    half = len(refs) // 2
    for src, dst in zip(refs[:half], refs[half:]):
        dst[...] = src[...].T


def split_features(x, my_x, z_hi, nx):
    rows, dim = x.shape
    wide = dim // (z_hi * nx)

    def source(s):
        return pl.BlockSpec((rows, wide), lambda g, info: (0, g * nx + (info[0] + s) % nx))

    return pl.pallas_call(
        split_kernel,
        grid_spec=pltpu.PrefetchScalarGridSpec(
            num_scalar_prefetch=1,
            grid=(z_hi,),
            in_specs=[source(s) for s in range(nx)],
            out_specs=[pl.BlockSpec((wide, rows), lambda g, info: (g, 0))] * nx,
        ),
        out_shape=[jax.ShapeDtypeStruct((z_hi * wide, rows), x.dtype)] * nx,
        compiler_params=pltpu.CompilerParams(vmem_limit_bytes=16 * 2**20),
        name="split_features",
    )(my_x[None], *([x] * nx))


def weight_kernel(nx, z_hi, info, *refs):
    f_refs, wide_refs, narrow_refs = refs[:nx], refs[nx : 2 * nx + 1], refs[2 * nx + 1 : 3 * nx + 1]
    out_ref, ft_s = refs[3 * nx + 1 :]
    rows, width = wide_refs[0].shape
    each = f_refs[0].shape[0] // (z_hi * 2)
    cols = 256
    part = out_ref.shape[2]
    for s in range(nx):
        for z in range(z_hi):
            at = pl.multiple_of((z * 2 + info[0]) * each, each)
            ft_s[z * each : (z + 1) * each, s * rows : (s + 1) * rows] = f_refs[s][pl.ds(at, each)]

    def columns(blocks, to):
        total = dot(ft_s[:, :rows], blocks[0])
        for s in range(1, nx):
            total += dot(ft_s[:, s * rows : (s + 1) * rows], blocks[s])
        total = total.astype(BF)
        for z in range(z_hi):
            for p in range(out_ref.shape[0]):
                row = z * each + p * part
                out_ref[p, z, :, to : to + cols] = total[row : row + part]

    for at in range(0, width, cols):
        own, left, far_first, far_second, right = wide_refs
        split = far_first.shape[1]
        far = far_first[:, at : at + cols] if at < split else far_second[:, at - split : at - split + cols]
        columns([own[:, at : at + cols], left[:, at : at + cols], far, right[:, at : at + cols]], at)
    for at in range(0, narrow_refs[0].shape[1], cols):
        columns([ref[:, at : at + cols] for ref in narrow_refs], width + at)


def weight_part(features, wide, narrow, which, z_hi, pieces):
    nx = len(features)
    rows = wide[0].shape[0]
    each = features[0].shape[0] // (z_hi * 2)
    n = wide[0].shape[1] + narrow[0].shape[1]
    operands = [*features, *wide, *narrow]
    out_shape = (pieces, z_hi, each // pieces, n)
    return pl.pallas_call(
        functools.partial(weight_kernel, nx, z_hi),
        in_specs=[pl.BlockSpec(memory_space=pltpu.SMEM)]
        + [pl.BlockSpec(memory_space=pltpu.VMEM)] * len(operands),
        out_specs=pl.BlockSpec(memory_space=pltpu.VMEM),
        out_shape=jax.ShapeDtypeStruct(out_shape, BF),
        scratch_shapes=[pltpu.VMEM((z_hi * each, nx * rows), BF)],
        compiler_params=pltpu.CompilerParams(vmem_limit_bytes=20 * 2**20),
        cost_estimate=pl.CostEstimate(
            flops=2 * z_hi * each * nx * rows * n,
            bytes_accessed=6 * 2**20,
            transcendentals=0,
        ),
        name="weight_part",
    )(which[None], *operands)


def local(layer_input, queries, key_head, value_head, grad_output, doc_ids):
    x, q, k, v, do = (a[0] for a in (layer_input, queries, key_head, value_head, grad_output))
    rows, hd = k.shape
    ctx = lax.axis_size(CTX)
    nx, nc, z_hi = lax.axis_size("x"), lax.axis_size("core"), lax.axis_size("zh")
    ny, zl = lax.axis_size("y"), lax.axis_size("zl")
    place = lax.axis_index(CTX)
    my_x, my_core = lax.axis_index("x"), lax.axis_index("core")

    kv = jnp.concatenate([k, v], axis=1)
    other = shifted(kv, "zl", zl, 1)
    parts = split_features(x, my_x, z_hi, nx)
    other, parts = lax.optimization_barrier((other, parts))
    pair = jnp.stack([kv, other])
    before, after = shifted(pair, "y", ny, 1), shifted(pair, "y", ny, -1)
    far = shifted(before[0], "y", ny, 1), shifted(after[1], "y", ny, -1)
    features = [shifted(part, "x", nx, s) if s else part for s, part in enumerate(parts)]

    dq, dkv = attention(q, do, [pair, before, *far, after], doc_ids, place, ny)
    dq, dkv, features = lax.optimization_barrier((dq, dkv, features))
    left, right = shifted(dq, "x", nx, 1), shifted(dq, "x", nx, -1)
    dkv = lax.all_to_all(dkv, CTX, 0, 0, tiled=True)
    dkv_own = jnp.sum(dkv.astype(F32), axis=0).astype(BF)
    narrow = [dkv_own] + [shifted(dkv_own, "x", nx, s) for s in range(1, nx)]
    left, right, dkv_own = lax.optimization_barrier((left, right, dkv_own))
    half = dq.shape[1] // 2
    far = shifted(left[:, :half], "x", nx, 1), shifted(right[:, half:], "x", nx, -1)
    wide = [dq, left, *far, right]

    theirs = weight_part(features, wide, narrow, 1 - my_core, z_hi, ctx)
    theirs = shifted(theirs, "core", nc, 1)
    mine = weight_part(features, wide, narrow, my_core, z_hi, ctx)
    n = mine.shape[-1]
    part = plus(mine, theirs).reshape(ctx, -1, n)
    part = lax.all_to_all(part, CTX, 0, 0, tiled=True)
    part = jnp.sum(part.astype(F32), axis=0).astype(BF).reshape(z_hi, -1, n)
    my_zh = lax.axis_index("zh")
    weight = 0.0
    for step in range(z_hi):
        piece = lax.dynamic_index_in_dim(part, (my_zh + step) % z_hi, 0, keepdims=False)
        weight = weight + (shifted(piece, "zh", z_hi, step) if step else piece).astype(F32)
    tokens = rows * ctx * nx * nc * z_hi
    weight = weight * (1.0 / math.sqrt(tokens))
    width = q.shape[1]
    return (
        dq[None],
        dkv_own[None, :, :hd],
        dkv_own[None, :, hd:],
        weight[:, :width],
        weight[:, width : width + hd],
        weight[:, width + hd :],
    )


def solution(mesh):
    fine = Mesh(mesh.devices.reshape(SIZES), AXES)
    dp = ("zh", "x", "core")
    tok = P(dp, CTX, None)
    row = P(dp + CTX, None)
    return jax.shard_map(
        local,
        mesh=fine,
        in_specs=(tok, tok, tok, tok, tok, P(dp, None)),
        out_specs=(tok, tok, tok, row, row, row),
        check_vma=False,
    )
```

```python
import functools
import math

import jax
import jax.numpy as jnp
from jax import lax
from jax.experimental import pallas as pl
from jax.experimental.pallas import tpu as pltpu
from jax.sharding import Mesh, PartitionSpec as P

NEG = -1e30
DOCS = 4
AXES = ("zh", "x", "core", "y", "zl")
SIZES = (4, 4, 2, 4, 2)
CTX = ("y", "zl")
BF = jnp.bfloat16
F32 = jnp.float32
NN = (((1,), (0,)), ((), ()))


def dot(a, b):
    return lax.dot_general(a, b, NN, preferred_element_type=F32)


def shifted(value, axis, count, step, wrap=True):
    pairs = []
    for src in range(count):
        dst = src + step
        if wrap:
            pairs.append((src, dst % count))
        elif 0 <= dst < count:
            pairs.append((src, dst))
    return lax.ppermute(value, axis, pairs)


def plus(a, b):
    return (a.astype(F32) + b.astype(F32)).astype(BF)


def whole(shape):
    return pl.BlockSpec(shape, lambda *g: (0,) * len(shape))


def attention_kernel(ny, per, docs, scale, info, docs_ref, q_hbm, do_hbm, *refs):
    (pair_ref, before_ref, far_refs, after_ref), refs = (refs[0], refs[1], refs[2:4], refs[4]), refs[5:]
    dq_ref, refs = refs[0], refs[1:]
    out_ref, refs = refs[0], refs[1:]
    kv_s, kt_s, e_s, dp_s, md_s, stat_s, dqt_s, qt_s, dot_s, p_s, ds_s, qk_s, dk_s, starts_ref, q_ref, do_ref, sem, q_sem = refs
    rows = q_ref.shape[0]
    hd = kt_s.shape[1]
    place = info[0]
    power = scale * math.log2(math.e)
    farthest = place // 2

    copies = [
        (0, pltpu.make_async_copy(pair_ref, kv_s.at[pl.ds(0, 2)], sem.at[0])),
        (1, pltpu.make_async_copy(before_ref, kv_s.at[pl.ds(2, 2)], sem.at[1])),
        (2, pltpu.make_async_copy(far_refs[0], kv_s.at[4], sem.at[2])),
        (2, pltpu.make_async_copy(far_refs[1], kv_s.at[5], sem.at[3])),
        (3, pltpu.make_async_copy(after_ref, kv_s.at[pl.ds(6, 2)], sem.at[4])),
    ]
    loads = [
        pltpu.make_async_copy(q_hbm, q_ref, q_sem.at[0]),
        pltpu.make_async_copy(do_hbm, do_ref, q_sem.at[1]),
    ]
    for copy in loads:
        copy.start()
    for s, copy in copies:
        pl.when(s <= farthest)(copy.start)
    for copy in loads:
        copy.wait()

    for h in range(per):
        cols = slice(h * hd, (h + 1) * hd)
        span = slice(h * rows, (h + 1) * rows)
        qk_s[span] = q_ref[:, cols]
        dk_s[span] = do_ref[:, cols]
        qt_s[h] = q_ref[:, cols].T
        dot_s[h] = do_ref[:, cols].T
        stat_s[0, h] = jnp.full((1, rows), NEG, F32)
        stat_s[1, h] = jnp.zeros((1, rows), F32)
        stat_s[2, h] = jnp.zeros((1, rows), F32)
    dqt_s[...] = jnp.zeros_like(dqt_s)

    documents = docs_ref[...]
    mine = docs_ref[:, pl.ds(pl.multiple_of(place * rows, rows), rows)]
    starts = jnp.zeros((1, rows), jnp.int32)
    for t in range(docs - 1):
        length = jnp.sum((documents == t).astype(jnp.int32))
        starts += jnp.where(mine > t, length, 0)
    starts_ref[...] = starts
    limit = jnp.max(starts)
    used = place - jnp.min(starts) // rows + 1
    for s, copy in copies:
        pl.when(s <= farthest)(copy.wait)

    def clear(block, carry):
        out_ref[block] = jnp.zeros(out_ref.shape[1:], BF)
        return carry

    lax.fori_loop(0, place - used + 1, clear, 0)
    lax.fori_loop(place + 1, out_ref.shape[0], clear, 0)

    def slot(d):
        block = place - d
        return 2 * (place // 2 - block // 2) + (d % 2)

    def forward(d, masked):
        at = slot(d)
        kd = kv_s[at, :, :hd]
        vd = kv_s[at, :, hd:]
        kt_s[at] = kd.T
        if masked:
            kp = lax.broadcasted_iota(jnp.int32, (rows, rows), 0) + (place - d) * rows
            qp = lax.broadcasted_iota(jnp.int32, (rows, rows), 1) + place * rows
            ok = (kp >= starts_ref[...]) & (kp <= qp)
        for h in range(per):
            s = dot(kd, qt_s[h])
            if masked:
                s = jnp.where(ok, s, NEG)
            old = stat_s[0, h]
            top = jnp.maximum(old, jnp.max(s, axis=0, keepdims=True))
            e = jnp.exp2(s * power - top * power)
            alpha = jnp.exp2((old - top) * power)
            dp = dot(vd, dot_s[h])
            stat_s[0, h] = top
            stat_s[1, h] = stat_s[1, h] * alpha + jnp.sum(e, axis=0, keepdims=True)
            stat_s[2, h] = stat_s[2, h] * alpha + jnp.sum(e * dp, axis=0, keepdims=True)
            e_s[d, h] = e
            dp_s[d, h] = dp
            md_s[d, h] = top

    def first(d, carry):
        masked = (d == 0) | ((place - d) * rows < limit)
        pl.when(masked)(lambda: forward(d, True))
        pl.when(jnp.logical_not(masked))(lambda: forward(d, False))
        return carry

    lax.fori_loop(0, used, first, 0)

    tops = [stat_s[0, h] for h in range(per)]
    inverse = [1.0 / stat_s[1, h] for h in range(per)]
    delta = [stat_s[2, h] * inverse[h] for h in range(per)]

    def second(d, carry):
        for h in range(per):
            p = e_s[d, h] * (jnp.exp2((md_s[d, h] - tops[h]) * power) * inverse[h])
            p_s[:, h * rows : (h + 1) * rows] = p.astype(BF)
            ds_s[:, h * rows : (h + 1) * rows] = (p * (dp_s[d, h] - delta[h])).astype(BF)
        out_ref[place - d, :, hd:] = dot(p_s[...], dk_s[...]).astype(BF)
        out_ref[place - d, :, :hd] = (dot(ds_s[...], qk_s[...]) * scale).astype(BF)
        dqt_s[...] += dot(kt_s[slot(d)], ds_s[...])
        return carry

    lax.fori_loop(0, used, second, 0)

    for h in range(per):
        dq_ref[:, h * hd : (h + 1) * hd] = (dqt_s[:, h * rows : (h + 1) * rows].T * scale).astype(BF)


def attention(q, do, kv, docs, place, ny):
    rows = q.shape[0]
    hd = kv[0].shape[2] // 2
    width = q.shape[1]
    per = width // hd
    blocks = 2 * ny
    slab = pl.BlockSpec(memory_space=pltpu.HBM)
    pair = kv[0].shape
    return pl.pallas_call(
        functools.partial(attention_kernel, ny, per, DOCS, hd ** (-0.5)),
        grid=(1,),
        in_specs=[pl.BlockSpec(memory_space=pltpu.SMEM), whole(docs.shape), slab, slab]
        + [pl.BlockSpec(memory_space=pl.ANY)] * len(kv),
        out_specs=[whole((rows, width)), whole((blocks, *pair[1:]))],
        out_shape=[
            jax.ShapeDtypeStruct((rows, width), BF),
            jax.ShapeDtypeStruct((blocks, *pair[1:]), BF),
        ],
        scratch_shapes=[
            pltpu.VMEM((blocks, rows, 2 * hd), BF),
            pltpu.VMEM((blocks, hd, rows), BF),
            pltpu.VMEM((blocks, per, rows, rows), F32),
            pltpu.VMEM((blocks, per, rows, rows), F32),
            pltpu.VMEM((blocks, per, 1, rows), F32),
            pltpu.VMEM((3, per, 1, rows), F32),
            pltpu.VMEM((hd, per * rows), F32),
            pltpu.VMEM((per, hd, rows), BF),
            pltpu.VMEM((per, hd, rows), BF),
            pltpu.VMEM((rows, per * rows), BF),
            pltpu.VMEM((rows, per * rows), BF),
            pltpu.VMEM((per * rows, hd), BF),
            pltpu.VMEM((per * rows, hd), BF),
            pltpu.VMEM((1, rows), jnp.int32),
            pltpu.VMEM((rows, width), BF),
            pltpu.VMEM((rows, width), BF),
            pltpu.SemaphoreType.DMA((len(kv),)),
            pltpu.SemaphoreType.DMA((2,)),
        ],
        compiler_params=pltpu.CompilerParams(vmem_limit_bytes=52 * 2**20),
        cost_estimate=pl.CostEstimate(
            flops=4 * per * rows * rows * blocks * hd,
            bytes_accessed=4 * 2**20,
            transcendentals=0,
        ),
        name="attention_backward",
    )(place[None], docs, q, do, *kv)


def halves_kernel(left_ref, right_ref, first_ref, second_ref):
    half = first_ref.shape[1]
    first_ref[...] = left_ref[:, :half]
    second_ref[...] = right_ref[:, half:]


def halves(left, right):
    half = jax.ShapeDtypeStruct((left.shape[0], left.shape[1] // 2), left.dtype)
    return pl.pallas_call(
        halves_kernel,
        in_specs=[pl.BlockSpec(memory_space=pltpu.VMEM)] * 2,
        out_specs=[pl.BlockSpec(memory_space=pltpu.VMEM)] * 2,
        out_shape=[half, half],
        compiler_params=pltpu.CompilerParams(vmem_limit_bytes=4 * 2**20),
        cost_estimate=pl.CostEstimate(flops=2**36, bytes_accessed=2**21, transcendentals=0),
        name="halves",
    )(left, right)


def split_kernel(info, *refs):
    half = len(refs) // 2
    for src, dst in zip(refs[:half], refs[half:]):
        dst[...] = src[...].T


def split_features(x, my_x, z_hi, nx):
    rows, dim = x.shape
    wide = dim // (z_hi * nx)

    def source(s):
        return pl.BlockSpec((rows, wide), lambda g, info: (0, g * nx + (info[0] + s) % nx))

    return pl.pallas_call(
        split_kernel,
        grid_spec=pltpu.PrefetchScalarGridSpec(
            num_scalar_prefetch=1,
            grid=(z_hi,),
            in_specs=[source(s) for s in range(nx)],
            out_specs=[pl.BlockSpec((wide, rows), lambda g, info: (g, 0))] * nx,
        ),
        out_shape=[jax.ShapeDtypeStruct((z_hi * wide, rows), x.dtype)] * nx,
        compiler_params=pltpu.CompilerParams(vmem_limit_bytes=16 * 2**20),
        name="split_features",
    )(my_x[None], *([x] * nx))


def weight_kernel(nx, z_hi, info, *refs):
    f_refs, wide_refs, narrow_refs = refs[:nx], refs[nx : 2 * nx + 1], refs[2 * nx + 1 : 3 * nx + 1]
    out_ref, ft_s = refs[3 * nx + 1 :]
    rows, width = wide_refs[0].shape
    each = f_refs[0].shape[0] // (z_hi * 2)
    cols = 256
    part = out_ref.shape[2]
    for s in range(nx):
        for z in range(z_hi):
            at = pl.multiple_of((z * 2 + info[0]) * each, each)
            ft_s[z * each : (z + 1) * each, s * rows : (s + 1) * rows] = f_refs[s][pl.ds(at, each)]

    def columns(blocks, to):
        total = dot(ft_s[:, :rows], blocks[0])
        for s in range(1, nx):
            total += dot(ft_s[:, s * rows : (s + 1) * rows], blocks[s])
        total = total.astype(BF)
        for z in range(z_hi):
            for p in range(out_ref.shape[0]):
                row = z * each + p * part
                out_ref[p, z, :, to : to + cols] = total[row : row + part]

    for at in range(0, width, cols):
        own, left, far_first, far_second, right = wide_refs
        split = far_first.shape[1]
        far = far_first[:, at : at + cols] if at < split else far_second[:, at - split : at - split + cols]
        columns([own[:, at : at + cols], left[:, at : at + cols], far, right[:, at : at + cols]], at)
    for at in range(0, narrow_refs[0].shape[1], cols):
        columns([ref[:, at : at + cols] for ref in narrow_refs], width + at)


def weight_part(features, wide, narrow, which, z_hi, pieces):
    nx = len(features)
    rows = wide[0].shape[0]
    each = features[0].shape[0] // (z_hi * 2)
    n = wide[0].shape[1] + narrow[0].shape[1]
    operands = [*features, *wide, *narrow]
    out_shape = (pieces, z_hi, each // pieces, n)
    return pl.pallas_call(
        functools.partial(weight_kernel, nx, z_hi),
        in_specs=[pl.BlockSpec(memory_space=pltpu.SMEM)]
        + [pl.BlockSpec(memory_space=pltpu.VMEM)] * len(operands),
        out_specs=pl.BlockSpec(memory_space=pltpu.VMEM),
        out_shape=jax.ShapeDtypeStruct(out_shape, BF),
        scratch_shapes=[pltpu.VMEM((z_hi * each, nx * rows), BF)],
        compiler_params=pltpu.CompilerParams(vmem_limit_bytes=20 * 2**20),
        cost_estimate=pl.CostEstimate(
            flops=2 * z_hi * each * nx * rows * n,
            bytes_accessed=6 * 2**20,
            transcendentals=0,
        ),
        name="weight_part",
    )(which[None], *operands)


def local(layer_input, queries, key_head, value_head, grad_output, doc_ids):
    x, q, k, v, do = (a[0] for a in (layer_input, queries, key_head, value_head, grad_output))
    rows, hd = k.shape
    ctx = lax.axis_size(CTX)
    nx, nc, z_hi = lax.axis_size("x"), lax.axis_size("core"), lax.axis_size("zh")
    ny, zl = lax.axis_size("y"), lax.axis_size("zl")
    place = lax.axis_index(CTX)
    my_x, my_core = lax.axis_index("x"), lax.axis_index("core")

    kv = jnp.concatenate([k, v], axis=1)
    other = shifted(kv, "zl", zl, 1)
    parts = split_features(x, my_x, z_hi, nx)
    other, parts = lax.optimization_barrier((other, parts))
    pair = jnp.stack([kv, other])
    before, after = shifted(pair, "y", ny, 1), shifted(pair, "y", ny, -1)
    far = shifted(before[0], "y", ny, 1), shifted(after[1], "y", ny, -1)
    features = [shifted(part, "x", nx, s) if s else part for s, part in enumerate(parts)]

    dq, dkv = attention(q, do, [pair, before, *far, after], doc_ids, place, ny)
    dq, dkv, features = lax.optimization_barrier((dq, dkv, features))
    left, right = shifted(dq, "x", nx, 1), shifted(dq, "x", nx, -1)
    first, second = halves(left, right)
    dkv = lax.all_to_all(dkv, CTX, 0, 0, tiled=True)
    dkv, first, second = lax.optimization_barrier((dkv, first, second))
    dkv_own = jnp.sum(dkv.astype(F32), axis=0).astype(BF)
    narrow = [dkv_own] + [shifted(dkv_own, "x", nx, s) for s in range(1, nx)]
    far = shifted(first, "x", nx, 1), shifted(second, "x", nx, -1)
    wide = [dq, left, *far, right]

    theirs = weight_part(features, wide, narrow, 1 - my_core, z_hi, ctx)
    theirs = shifted(theirs, "core", nc, 1)
    mine = weight_part(features, wide, narrow, my_core, z_hi, ctx)
    n = mine.shape[-1]
    part = plus(mine, theirs).reshape(ctx, -1, n)
    part = lax.all_to_all(part, CTX, 0, 0, tiled=True)
    part = jnp.sum(part.astype(F32), axis=0).astype(BF).reshape(z_hi, -1, n)
    my_zh = lax.axis_index("zh")
    weight = 0.0
    for step in range(z_hi):
        piece = lax.dynamic_index_in_dim(part, (my_zh + step) % z_hi, 0, keepdims=False)
        weight = weight + (shifted(piece, "zh", z_hi, step) if step else piece).astype(F32)
    tokens = rows * ctx * nx * nc * z_hi
    weight = weight * (1.0 / math.sqrt(tokens))
    width = q.shape[1]
    return (
        dq[None],
        dkv_own[None, :, :hd],
        dkv_own[None, :, hd:],
        weight[:, :width],
        weight[:, width : width + hd],
        weight[:, width + hd :],
    )


def solution(mesh):
    fine = Mesh(mesh.devices.reshape(SIZES), AXES)
    dp = ("zh", "x", "core")
    tok = P(dp, CTX, None)
    row = P(dp + CTX, None)
    return jax.shard_map(
        local,
        mesh=fine,
        in_specs=(tok, tok, tok, tok, tok, P(dp, None)),
        out_specs=(tok, tok, tok, row, row, row),
        check_vma=False,
    )
```

```python
import functools
import math

import jax
import jax.numpy as jnp
from jax import lax
from jax.experimental import pallas as pl
from jax.experimental.pallas import tpu as pltpu
from jax.sharding import Mesh, PartitionSpec as P

NEG = -1e30
DOCS = 4
AXES = ("zh", "x", "core", "y", "zl")
SIZES = (4, 4, 2, 4, 2)
CTX = ("y", "zl")
BF = jnp.bfloat16
F32 = jnp.float32
NN = (((1,), (0,)), ((), ()))


def dot(a, b):
    return lax.dot_general(a, b, NN, preferred_element_type=F32)


def shifted(value, axis, count, step, wrap=True):
    pairs = []
    for src in range(count):
        dst = src + step
        if wrap:
            pairs.append((src, dst % count))
        elif 0 <= dst < count:
            pairs.append((src, dst))
    return lax.ppermute(value, axis, pairs)


def plus(a, b):
    return (a.astype(F32) + b.astype(F32)).astype(BF)


def whole(shape):
    return pl.BlockSpec(shape, lambda *g: (0,) * len(shape))


def attention_kernel(ny, per, docs, scale, info, docs_ref, q_hbm, do_hbm, *refs):
    (pair_ref, before_ref, far_refs, after_ref), refs = (refs[0], refs[1], refs[2:4], refs[4]), refs[5:]
    dq_ref, refs = refs[0], refs[1:]
    out_ref, refs = refs[0], refs[1:]
    kv_s, kt_s, e_s, dp_s, md_s, stat_s, dqt_s, qt_s, dot_s, p_s, ds_s, qk_s, dk_s, starts_ref, q_ref, do_ref, sem, q_sem = refs
    rows = q_ref.shape[0]
    hd = kt_s.shape[1]
    place = info[0]
    power = scale * math.log2(math.e)
    farthest = place // 2

    copies = [
        (0, pltpu.make_async_copy(pair_ref, kv_s.at[pl.ds(0, 2)], sem.at[0])),
        (1, pltpu.make_async_copy(before_ref, kv_s.at[pl.ds(2, 2)], sem.at[1])),
        (2, pltpu.make_async_copy(far_refs[0], kv_s.at[4], sem.at[2])),
        (2, pltpu.make_async_copy(far_refs[1], kv_s.at[5], sem.at[3])),
        (3, pltpu.make_async_copy(after_ref, kv_s.at[pl.ds(6, 2)], sem.at[4])),
    ]
    loads = [
        pltpu.make_async_copy(q_hbm, q_ref, q_sem.at[0]),
        pltpu.make_async_copy(do_hbm, do_ref, q_sem.at[1]),
    ]
    for copy in loads:
        copy.start()
    for s, copy in copies:
        pl.when(s <= farthest)(copy.start)
    for copy in loads:
        copy.wait()

    for h in range(per):
        cols = slice(h * hd, (h + 1) * hd)
        span = slice(h * rows, (h + 1) * rows)
        qk_s[span] = q_ref[:, cols]
        dk_s[span] = do_ref[:, cols]
        qt_s[h] = q_ref[:, cols].T
        dot_s[h] = do_ref[:, cols].T
        stat_s[0, h] = jnp.full((1, rows), NEG, F32)
        stat_s[1, h] = jnp.zeros((1, rows), F32)
        stat_s[2, h] = jnp.zeros((1, rows), F32)
    dqt_s[...] = jnp.zeros_like(dqt_s)

    documents = docs_ref[...]
    mine = docs_ref[:, pl.ds(pl.multiple_of(place * rows, rows), rows)]
    starts = jnp.zeros((1, rows), jnp.int32)
    for t in range(docs - 1):
        length = jnp.sum((documents == t).astype(jnp.int32))
        starts += jnp.where(mine > t, length, 0)
    starts_ref[...] = starts
    limit = jnp.max(starts)
    used = place - jnp.min(starts) // rows + 1
    for s, copy in copies:
        pl.when(s <= farthest)(copy.wait)

    def clear(block, carry):
        out_ref[block] = jnp.zeros(out_ref.shape[1:], BF)
        return carry

    lax.fori_loop(0, place - used + 1, clear, 0)
    lax.fori_loop(place + 1, out_ref.shape[0], clear, 0)

    def slot(d):
        block = place - d
        return 2 * (place // 2 - block // 2) + (d % 2)

    def forward(d, masked):
        at = slot(d)
        kd = kv_s[at, :, :hd]
        vd = kv_s[at, :, hd:]
        kt_s[at] = kd.T
        if masked:
            kp = lax.broadcasted_iota(jnp.int32, (rows, rows), 0) + (place - d) * rows
            qp = lax.broadcasted_iota(jnp.int32, (rows, rows), 1) + place * rows
            ok = (kp >= starts_ref[...]) & (kp <= qp)
        for h in range(per):
            s = dot(kd, qt_s[h])
            if masked:
                s = jnp.where(ok, s, NEG)
            old = stat_s[0, h]
            top = jnp.maximum(old, jnp.max(s, axis=0, keepdims=True))
            e = jnp.exp2(s * power - top * power)
            alpha = jnp.exp2((old - top) * power)
            dp = dot(vd, dot_s[h])
            stat_s[0, h] = top
            stat_s[1, h] = stat_s[1, h] * alpha + jnp.sum(e, axis=0, keepdims=True)
            stat_s[2, h] = stat_s[2, h] * alpha + jnp.sum(e * dp, axis=0, keepdims=True)
            e_s[d, h] = e
            dp_s[d, h] = dp
            md_s[d, h] = top

    def first(d, carry):
        masked = (d == 0) | ((place - d) * rows < limit)
        pl.when(masked)(lambda: forward(d, True))
        pl.when(jnp.logical_not(masked))(lambda: forward(d, False))
        return carry

    lax.fori_loop(0, used, first, 0)

    tops = [stat_s[0, h] for h in range(per)]
    inverse = [1.0 / stat_s[1, h] for h in range(per)]
    delta = [stat_s[2, h] * inverse[h] for h in range(per)]

    def second(d, carry):
        for h in range(per):
            p = e_s[d, h] * (jnp.exp2((md_s[d, h] - tops[h]) * power) * inverse[h])
            p_s[:, h * rows : (h + 1) * rows] = p.astype(BF)
            ds_s[:, h * rows : (h + 1) * rows] = (p * (dp_s[d, h] - delta[h])).astype(BF)
        out_ref[place - d, :, hd:] = dot(p_s[...], dk_s[...]).astype(BF)
        out_ref[place - d, :, :hd] = (dot(ds_s[...], qk_s[...]) * scale).astype(BF)
        dqt_s[...] += dot(kt_s[slot(d)], ds_s[...])
        return carry

    lax.fori_loop(0, used, second, 0)

    for h in range(per):
        dq_ref[:, h * hd : (h + 1) * hd] = (dqt_s[:, h * rows : (h + 1) * rows].T * scale).astype(BF)


def attention(q, do, kv, docs, place, ny):
    rows = q.shape[0]
    hd = kv[0].shape[2] // 2
    width = q.shape[1]
    per = width // hd
    blocks = 2 * ny
    slab = pl.BlockSpec(memory_space=pltpu.HBM)
    pair = kv[0].shape
    return pl.pallas_call(
        functools.partial(attention_kernel, ny, per, DOCS, hd ** (-0.5)),
        grid=(1,),
        in_specs=[pl.BlockSpec(memory_space=pltpu.SMEM), whole(docs.shape), slab, slab]
        + [pl.BlockSpec(memory_space=pl.ANY)] * len(kv),
        out_specs=[whole((rows, width)), whole((blocks, *pair[1:]))],
        out_shape=[
            jax.ShapeDtypeStruct((rows, width), BF),
            jax.ShapeDtypeStruct((blocks, *pair[1:]), BF),
        ],
        scratch_shapes=[
            pltpu.VMEM((blocks, rows, 2 * hd), BF),
            pltpu.VMEM((blocks, hd, rows), BF),
            pltpu.VMEM((blocks, per, rows, rows), F32),
            pltpu.VMEM((blocks, per, rows, rows), F32),
            pltpu.VMEM((blocks, per, 1, rows), F32),
            pltpu.VMEM((3, per, 1, rows), F32),
            pltpu.VMEM((hd, per * rows), F32),
            pltpu.VMEM((per, hd, rows), BF),
            pltpu.VMEM((per, hd, rows), BF),
            pltpu.VMEM((rows, per * rows), BF),
            pltpu.VMEM((rows, per * rows), BF),
            pltpu.VMEM((per * rows, hd), BF),
            pltpu.VMEM((per * rows, hd), BF),
            pltpu.VMEM((1, rows), jnp.int32),
            pltpu.VMEM((rows, width), BF),
            pltpu.VMEM((rows, width), BF),
            pltpu.SemaphoreType.DMA((len(kv),)),
            pltpu.SemaphoreType.DMA((2,)),
        ],
        compiler_params=pltpu.CompilerParams(vmem_limit_bytes=52 * 2**20),
        cost_estimate=pl.CostEstimate(
            flops=4 * per * rows * rows * blocks * hd,
            bytes_accessed=4 * 2**20,
            transcendentals=0,
        ),
        name="attention_backward",
    )(place[None], docs, q, do, *kv)


def halves_kernel(left_ref, right_ref, first_ref, second_ref):
    half = first_ref.shape[1]
    first_ref[...] = left_ref[:, :half]
    second_ref[...] = right_ref[:, half:]


def halves(left, right):
    half = jax.ShapeDtypeStruct((left.shape[0], left.shape[1] // 2), left.dtype)
    return pl.pallas_call(
        halves_kernel,
        in_specs=[pl.BlockSpec(memory_space=pltpu.VMEM)] * 2,
        out_specs=[pl.BlockSpec(memory_space=pltpu.VMEM)] * 2,
        out_shape=[half, half],
        compiler_params=pltpu.CompilerParams(vmem_limit_bytes=4 * 2**20),
        cost_estimate=pl.CostEstimate(flops=2**36, bytes_accessed=2**21, transcendentals=0),
        name="halves",
    )(left, right)


def split_kernel(info, *refs):
    half = len(refs) // 2
    for src, dst in zip(refs[:half], refs[half:]):
        dst[...] = src[...].T


def split_features(x, my_x, z_hi, nx):
    rows, dim = x.shape
    wide = dim // (z_hi * nx)

    def source(s):
        return pl.BlockSpec((rows, wide), lambda g, info: (0, g * nx + (info[0] + s) % nx))

    return pl.pallas_call(
        split_kernel,
        grid_spec=pltpu.PrefetchScalarGridSpec(
            num_scalar_prefetch=1,
            grid=(z_hi,),
            in_specs=[source(s) for s in range(nx)],
            out_specs=[pl.BlockSpec((wide, rows), lambda g, info: (g, 0))] * nx,
        ),
        out_shape=[jax.ShapeDtypeStruct((z_hi * wide, rows), x.dtype)] * nx,
        compiler_params=pltpu.CompilerParams(vmem_limit_bytes=16 * 2**20),
        name="split_features",
    )(my_x[None], *([x] * nx))


def weight_kernel(nx, z_hi, info, *refs):
    f_refs, wide_refs, narrow_refs = refs[:nx], refs[nx : 2 * nx + 1], refs[2 * nx + 1 : 3 * nx + 1]
    out_ref, ft_s = refs[3 * nx + 1 :]
    rows, width = wide_refs[0].shape
    each = f_refs[0].shape[0] // (z_hi * 2)
    cols = 256
    part = out_ref.shape[2]
    for s in range(nx):
        for z in range(z_hi):
            at = pl.multiple_of((z * 2 + info[0]) * each, each)
            ft_s[z * each : (z + 1) * each, s * rows : (s + 1) * rows] = f_refs[s][pl.ds(at, each)]

    def columns(blocks, to):
        total = dot(ft_s[:, :rows], blocks[0])
        for s in range(1, nx):
            total += dot(ft_s[:, s * rows : (s + 1) * rows], blocks[s])
        total = total.astype(BF)
        for z in range(z_hi):
            for p in range(out_ref.shape[0]):
                row = z * each + p * part
                out_ref[p, z, :, to : to + cols] = total[row : row + part]

    for at in range(0, width, cols):
        own, left, far_first, far_second, right = wide_refs
        split = far_first.shape[1]
        far = far_first[:, at : at + cols] if at < split else far_second[:, at - split : at - split + cols]
        columns([own[:, at : at + cols], left[:, at : at + cols], far, right[:, at : at + cols]], at)
    for at in range(0, narrow_refs[0].shape[1], cols):
        columns([ref[:, at : at + cols] for ref in narrow_refs], width + at)


def weight_part(features, wide, narrow, which, z_hi, pieces):
    nx = len(features)
    rows = wide[0].shape[0]
    each = features[0].shape[0] // (z_hi * 2)
    n = wide[0].shape[1] + narrow[0].shape[1]
    operands = [*features, *wide, *narrow]
    out_shape = (pieces, z_hi, each // pieces, n)
    return pl.pallas_call(
        functools.partial(weight_kernel, nx, z_hi),
        in_specs=[pl.BlockSpec(memory_space=pltpu.SMEM)]
        + [pl.BlockSpec(memory_space=pltpu.VMEM)] * len(operands),
        out_specs=pl.BlockSpec(memory_space=pltpu.VMEM),
        out_shape=jax.ShapeDtypeStruct(out_shape, BF),
        scratch_shapes=[pltpu.VMEM((z_hi * each, nx * rows), BF)],
        compiler_params=pltpu.CompilerParams(vmem_limit_bytes=20 * 2**20),
        cost_estimate=pl.CostEstimate(
            flops=2 * z_hi * each * nx * rows * n,
            bytes_accessed=6 * 2**20,
            transcendentals=0,
        ),
        name="weight_part",
    )(which[None], *operands)


def local(layer_input, queries, key_head, value_head, grad_output, doc_ids):
    x, q, k, v, do = (a[0] for a in (layer_input, queries, key_head, value_head, grad_output))
    rows, hd = k.shape
    ctx = lax.axis_size(CTX)
    nx, nc, z_hi = lax.axis_size("x"), lax.axis_size("core"), lax.axis_size("zh")
    ny, zl = lax.axis_size("y"), lax.axis_size("zl")
    place = lax.axis_index(CTX)
    my_x, my_core = lax.axis_index("x"), lax.axis_index("core")

    kv = jnp.concatenate([k, v], axis=1)
    other = shifted(kv, "zl", zl, 1)
    parts = split_features(x, my_x, z_hi, nx)
    other, parts = lax.optimization_barrier((other, parts))
    pair = jnp.stack([kv, other])
    before, after = shifted(pair, "y", ny, 1), shifted(pair, "y", ny, -1)
    far = shifted(before[0], "y", ny, 1), shifted(after[1], "y", ny, -1)
    features = [shifted(part, "x", nx, s) if s else part for s, part in enumerate(parts)]

    dq, dkv = attention(q, do, [pair, before, *far, after], doc_ids, place, ny)
    dq, dkv, features = lax.optimization_barrier((dq, dkv, features))
    left, right = shifted(dq, "x", nx, 1), shifted(dq, "x", nx, -1)
    first, second = halves(left, right)
    dkv = lax.all_to_all(dkv, CTX, 0, 0, tiled=True)
    dkv_own = jnp.sum(dkv.astype(F32), axis=0).astype(BF)
    narrow = [dkv_own] + [shifted(dkv_own, "x", nx, s) for s in range(1, nx)]
    dkv_own, first, second = lax.optimization_barrier((dkv_own, first, second))
    far = shifted(first, "x", nx, 1), shifted(second, "x", nx, -1)
    wide = [dq, left, *far, right]

    theirs = weight_part(features, wide, narrow, 1 - my_core, z_hi, ctx)
    theirs = shifted(theirs, "core", nc, 1)
    mine = weight_part(features, wide, narrow, my_core, z_hi, ctx)
    n = mine.shape[-1]
    part = plus(mine, theirs).reshape(ctx, -1, n)
    part = lax.all_to_all(part, CTX, 0, 0, tiled=True)
    part = jnp.sum(part.astype(F32), axis=0).astype(BF).reshape(z_hi, -1, n)
    my_zh = lax.axis_index("zh")
    pieces = []
    for step in range(z_hi):
        piece = lax.dynamic_index_in_dim(part, (my_zh + step) % z_hi, 0, keepdims=False)
        pieces.append(shifted(piece, "zh", z_hi, step) if step else piece)
    factor = 1.0 / math.sqrt(rows * ctx * nx * nc * z_hi)
    width = q.shape[1]

    def weight(first, last):
        return sum(piece[:, first:last].astype(F32) for piece in pieces) * factor

    return (
        dq[None],
        dkv_own[None, :, :hd],
        dkv_own[None, :, hd:],
        weight(0, width),
        weight(width, width + hd),
        weight(width + hd, n),
    )


def solution(mesh):
    fine = Mesh(mesh.devices.reshape(SIZES), AXES)
    dp = ("zh", "x", "core")
    tok = P(dp, CTX, None)
    row = P(dp + CTX, None)
    return jax.shard_map(
        local,
        mesh=fine,
        in_specs=(tok, tok, tok, tok, tok, P(dp, None)),
        out_specs=(tok, tok, tok, row, row, row),
        check_vma=False,
    )
```
